32 devices in a mesh: dp: 8 (over y, x, core), expert: 4 (over z).
Axes of the slice: x: 2, y: 2, z: 4, core: 2. Of those that a mesh axis runs over, the one named last changes fastest.
Arguments:
- acts: float32 [8192, 1024], P(('dp', 'expert')), may hold values from -18 to 18, as said below
- grads_out: float32 [8192, 1024], P(('dp', 'expert')), may hold values from -18 to 18, as said below
- routes: int32 [8192, 2], P(('dp', 'expert')), may hold values from 0 to 3, all different within a row; in each aligned block of 256 rows (0 to 255, 256 to 511, ...) at most 192 rows name the same one
- counts: int32 [32, 4], P(('dp', 'expert')), may hold values from 96 to 192
- old_act_factor: float32 [4, 1024, 1024], P('expert', 'dp'), may hold values from -1 to 4, as said below
- old_grad_factor: float32 [4, 1024, 1024], P('expert', 'dp'), may hold values from -1 to 4, as said below
- momentum: float32 [4, 1024, 1024], P('expert', 'dp'), may hold values from -0.0018 to 0.0018
- weights: float32 [4, 1024, 1024], P('expert', 'dp'), may hold values from -0.1875 to 0.1875
Outputs:
- act_factor: float32 [4, 1024, 1024], P('expert', 'dp')
- grad_factor: float32 [4, 1024, 1024], P('expert', 'dp')
- new_momentum: float32 [4, 1024, 1024], P('expert', 'dp')
- new_weights: float32 [4, 1024, 1024], P('expert', 'dp')
The draws below stay inside these ranges and needn't reach their ends.
Inputs may be any that keep to these rules, and one draw needn't show every extreme that they name: `acts`: entries are independent across rows; each feature has its own scale. `grads_out`: entries are independent across rows; each feature has its own scale. `old_act_factor`: each expert's matrix is symmetric, and each diagonal entry exceeds the sum of the magnitudes of the other entries of its row. `old_grad_factor`: each expert's matrix is symmetric, and each diagonal entry exceeds the sum of the magnitudes of the other entries of its row. `routes`: within the rows of one device no expert is named by more than 192 rows.
All inputs are finite; a program needn't handle non-finite values. Where the reference program divides by a largest or mean magnitude, that divisor is 1e-20 or more.
Results may differ from the reference program's by a relative error of at most 0.00013.
Values sent between devices are 32-bit elements; how exact they have to be, the bound alone decides.
No kernel may reach another device: no remote copies, remote signals or barrier semaphores. Data moves between devices by JAX's collectives and lax.ppermute only.
A program may use at most 128 MiB of HBM per device.

```python
import math
import jax
import jax.numpy as jnp
import numpy as np
from jax import lax

FEAT = 1024
TOPK = 2
S_DEV = 256
EXPERTS = 4
CAP = 192
ROWS = 8192
DEVICES = 32


def feature_draw(key):
    k_scale, k_base = jax.random.split(key, 2)
    scales = jnp.exp(jax.random.uniform(k_scale, (FEAT,), jnp.float32, jnp.log(0.3), jnp.log(3.0)))
    base = jnp.clip(jax.random.normal(k_base, (ROWS, FEAT), jnp.float32), -6.0, 6.0)
    return base * scales[None, :]


def dominant_draw(key):
    k_diag, k_off = jax.random.split(key)
    diag = jnp.exp(jax.random.uniform(k_diag, (EXPERTS, FEAT), jnp.float32, 0.0, jnp.log(4.0)))
    raw = jax.random.uniform(k_off, (EXPERTS, FEAT, FEAT), jnp.float32, -1.0, 1.0) * (1.2 / FEAT)
    off = 0.5 * (raw + jnp.swapaxes(raw, 1, 2))
    unit = jnp.eye(FEAT, dtype=jnp.float32)[None, :, :]
    return off * (1.0 - unit) + diag[:, :, None] * unit


def draw_acts(key, part):
    return feature_draw(jax.random.fold_in(key, 11))


def draw_grads_out(key, part):
    return feature_draw(jax.random.fold_in(key, 23))


def draw_old_act_factor(key, part):
    return dominant_draw(jax.random.fold_in(key, 37))


def draw_old_grad_factor(key, part):
    return dominant_draw(jax.random.fold_in(key, 41))


def touch_ends(entries, stream_key, least, largest):
    index_at = [jax.random.randint(jax.random.fold_in(stream_key, axis), (), 0, length) for axis, length in enumerate(entries.shape)]
    main_axis = entries.shape.index(max(entries.shape))
    beside = index_at[:main_axis] + [(index_at[main_axis] + 1) % entries.shape[main_axis]] + index_at[main_axis + 1:]
    return entries.at[tuple(index_at)].set(least).at[tuple(beside)].set(largest)


def steps_of(stream_key, dims, cuts, smallest, high):
    def one(dim, shards_of):
        heights = jax.random.uniform(jax.random.fold_in(jax.random.fold_in(stream_key, 6), dim), (shards_of,), jnp.float32, smallest / len(cuts), high / len(cuts))
        return jnp.repeat(jnp.exp(heights), dims[dim] // shards_of).reshape((-1,) + (1,) * (len(dims) - dim - 1))

    level = one(*cuts[0])
    for cut in cuts[1:]:
        level = level * one(*cut)
    return level


def routed_block(stream_key, own, number, rows, count, top, bound, skew):
    ranking = jax.random.permutation(stream_key, count)
    packed, ordinary = portions_of(count, rows * top, bound, skew, True), portions_of(count, rows * top, bound, skew, False)
    places = jnp.arange(count)

    def named(lengths, turn):
        used = int((lengths > 0).sum())
        fixed = max(1, used // 4)
        moved = fixed + (places - fixed + turn * (used - fixed)) % max(1, count - fixed)
        return jnp.zeros((count,), jnp.int32).at[ranking[jnp.where(places < fixed, places, moved)]].set(jnp.asarray(lengths, jnp.int32))

    lengths = jnp.where(number % 4 == 0, named(packed, number // 4), named(ordinary, number - number // 4 - 1))
    mixed = jax.random.permutation(jax.random.fold_in(own, 3), count)
    donor, sink = mixed[0:count // 2 * 2:2], mixed[1:count // 2 * 2:2]
    slack = jnp.minimum(lengths[donor] - 1, bound - lengths[sink]) // 2
    slack = jnp.where((donor == ranking[0]) | (sink == ranking[0]) | (lengths[sink] == 0), 0, jnp.maximum(slack, 0))
    moved = jax.random.randint(jax.random.fold_in(own, 4), (count // 2,), 0, 1 << 20) % (slack + 1)
    lengths = lengths.at[donor].add(-moved).at[sink].add(moved)
    items = jnp.searchsorted(jnp.cumsum(lengths), jnp.arange(rows * top), side="right").astype(jnp.int32)
    table = items.reshape(top, rows).T
    table = table[jax.random.permutation(jax.random.fold_in(own, 1), rows)]
    turn = jax.random.randint(jax.random.fold_in(own, 2), (rows, 1), 0, top)
    return jnp.take_along_axis(table, (jnp.arange(top)[None, :] + turn) % top, axis=1)


def portions_of(count, total, reach, slope, full):
    loads = [(1 << 20) // math.isqrt(rank ** slope) + 1 for rank in range(1, count + 1)]
    largest = reach if full else min(reach, max(-(-total // count), total * loads[0] // sum(loads)))
    least = 1 if total - largest >= count - 1 else 0
    holding, spare = [largest] + [least] * (count - 1), total - largest - least * (count - 1)
    while spare > 0:
        movable = [i for i in range(1, count) if holding[i] < largest] or [i for i in range(1, count) if holding[i] < reach]
        whole, left = sum([loads[i] for i in movable]), spare
        for i in movable:
            extra = min(reach - holding[i], max(1, left * loads[i] // whole), spare)
            holding[i] = holding[i] + extra
            spare = spare - extra
    return np.array(holding)


def bell_draw(rng, extent, deviation, limit, pieces=(), held_as=jnp.bfloat16):
    level = steps_of(rng, extent, pieces, -0.22, 0.18) if pieces else 1.0
    drawn = jax.random.normal(rng, extent, jnp.float32) * deviation * level
    return jnp.minimum(jnp.maximum(drawn, -limit), limit).astype(held_as)


def setup_inputs(seed: int = 0) -> dict:
    seeds = jax.random.split(jax.random.key(seed), 9)
    acts = draw_acts(jax.random.fold_in(seeds[8], 71), 0)
    grads_out = draw_grads_out(jax.random.fold_in(seeds[8], 71), 0)
    routes_keys = jax.random.split(jax.random.fold_in(seeds[2], 1), ROWS // S_DEV)
    routes_turns = jax.random.permutation(jax.random.fold_in(seeds[2], 3), ROWS // S_DEV)
    routes = jax.vmap(lambda own, number: routed_block(jax.random.fold_in(seeds[2], 2), own, number, S_DEV, EXPERTS, TOPK, CAP, 2))(routes_keys, routes_turns).reshape((ROWS, TOPK))
    counts = touch_ends(jax.random.randint(seeds[3], (DEVICES, EXPERTS), CAP // 2, CAP + 1), jax.random.fold_in(seeds[3], 1), CAP // 2, CAP).astype(jnp.int32)
    old_act_factor = draw_old_act_factor(jax.random.fold_in(seeds[8], 71), 0)
    old_grad_factor = draw_old_grad_factor(jax.random.fold_in(seeds[8], 71), 0)
    momentum = bell_draw(seeds[6], (EXPERTS, FEAT, FEAT), 0.0003, 0.0018, ((0, 4), (1, 8)), jnp.float32)
    weights = bell_draw(seeds[7], (EXPERTS, FEAT, FEAT), FEAT ** -0.5, 0.1875, ((0, 4), (1, 8)), jnp.float32)
    return {"acts": acts, "grads_out": grads_out, "routes": routes, "counts": counts, "old_act_factor": old_act_factor, "old_grad_factor": old_grad_factor, "momentum": momentum, "weights": weights}


def product(left, right):
    return jnp.dot(left, right, precision=lax.Precision.HIGHEST, preferred_element_type=jnp.float32)


def damped_inverse(factor):
    size = factor.shape[0]
    unit = jnp.eye(size, dtype=jnp.float32)
    damp = 0.1 * jnp.trace(factor) / size
    shifted = factor + damp * unit
    alpha = 1.0 / jnp.max(jnp.sum(jnp.abs(shifted), axis=1))
    first = alpha * (2.0 * unit - alpha * shifted)
    return 2.0 * first - product(product(first, shifted), first)


def reference(acts, grads_out, routes, counts, old_act_factor, old_grad_factor, momentum, weights):
    rows = routes.shape[0]
    devices = rows // S_DEV
    experts = jnp.arange(EXPERTS, dtype=jnp.int32)
    hit = jnp.sum((routes[:, :, None] == experts[None, None, :]).astype(jnp.int32), axis=1, dtype=jnp.int32)
    hit_dev = hit.reshape(devices, S_DEV, EXPERTS)
    rank = jnp.cumsum(hit_dev, axis=1, dtype=jnp.int32) - hit_dev
    keep = (hit_dev * (rank < counts[:, None, :]).astype(jnp.int32)).reshape(rows, EXPERTS)
    weight = keep.astype(jnp.float32)
    total = jnp.maximum(jnp.sum(weight, axis=0), jnp.float32(1.0))

    def one_expert(item):
        column, count, old_a, old_g, moment, current = item
        kept_acts = acts * column[:, None]
        kept_grads = grads_out * column[:, None]
        act_stat = product(kept_acts.T, kept_acts) / count
        grad_stat = product(kept_grads.T, kept_grads) / count
        gradient = product(kept_grads.T, kept_acts) / count
        act_new = 0.5 * old_a + 0.5 * act_stat
        grad_new = 0.5 * old_g + 0.5 * grad_stat
        precond = product(product(damped_inverse(grad_new), gradient), damped_inverse(act_new))
        moment_new = 0.9 * moment + precond
        return act_new, grad_new, moment_new, current - 0.5 * moment_new

    act_factor, grad_factor, new_momentum, new_weights = lax.map(
        one_expert, (weight.T, total, old_act_factor, old_grad_factor, momentum, weights))
    return (act_factor, grad_factor, new_momentum, new_weights)
```

```python
import functools

import jax
import jax.numpy as jnp
from jax import lax
from jax.experimental import pallas as pl
from jax.experimental.pallas import tpu as pltpu
from jax.sharding import PartitionSpec as P

F32 = jnp.float32
BF16 = jnp.bfloat16
TILE = 128
VMEM_LIMIT = 56 * 1024 * 1024


def split(value):
    high = value.astype(BF16)
    return high, (value - high.astype(F32)).astype(BF16)


def dot(left, right):
    return jnp.dot(left, right, preferred_element_type=F32)


def band_place(owner, block):
    per_tile = TILE // block
    if per_tile == 1:
        return pl.multiple_of(owner * TILE, TILE), 0
    return (
        pl.multiple_of(lax.div(owner, per_tile) * TILE, TILE),
        pl.multiple_of(lax.rem(owner, per_tile) * block, block),
    )


def split_rows(parts, high, low, feat):
    extra = high.shape[1] - feat
    for number, part in enumerate(parts):
        rows = part.shape[0]
        here = slice(number * rows, (number + 1) * rows)
        top, rest = split(part[...])
        high[here, 0:feat] = top
        low[here, 0:feat] = rest
        if extra:
            high[here, feat : feat + extra] = top[:, 0:extra]
            low[here, feat : feat + extra] = rest[:, 0:extra]


def left_rows(parts, turned, column, row, block):
    for number, part in enumerate(parts):
        rows = part.shape[0]
        turned[:, number * rows : (number + 1) * rows] = part[:, pl.ds(column, TILE)].T
    return turned[pl.ds(row, block), :]


def weighted(rows, weights, lanes):
    halves = [split(rows * weights[pl.ds(lane, 1), :]) for lane in lanes]
    tops = [half[0] for half in halves]
    return jnp.concatenate(tops + [half[1] for half in halves], axis=0), jnp.concatenate(tops, axis=0)


def act_kernel(turns, block, place, weights, *refs):
    parts, outs, (high, low, turned) = refs[:4], refs[4:-3], refs[-3:]
    feat = parts[0].shape[1]
    width = outs[0].shape[2]
    mine, expert = place[0], place[1]
    split_rows(parts, high, low, feat)
    lanes = [expert ^ (2 * turn) for turn in turns]
    for k, out in enumerate(outs):
        column, row = band_place(mine ^ (2 * k), block)
        both, tops = weighted(left_rows(parts, turned, column, row, block), weights, lanes)
        first = dot(both, high[:, pl.ds(column, width)])
        second = dot(tops, low[:, pl.ds(column, width)])
        half = len(turns) * block
        total = first[0:half] + first[half : 2 * half] + second
        for number in range(len(turns)):
            out[number] = total[number * block : (number + 1) * block]


def grad_kernel(turns, block, place, weights, *refs):
    grads, acts, outs = refs[:4], refs[4:8], refs[8:-5]
    high, low, act_high, act_low, turned = refs[-5:]
    feat = grads[0].shape[1]
    width = outs[0].shape[2] - feat
    mine, expert = place[0], place[1]
    split_rows(grads, high, low, feat)
    split_rows(acts, act_high, act_low, feat)
    lanes = [expert ^ (2 * turn) for turn in turns]
    half = len(turns) * block
    for k, out in enumerate(outs):
        column, row = band_place(mine ^ (2 * k), block)
        both, tops = weighted(left_rows(grads, turned, column, row, block), weights, lanes)
        first = dot(both, high[:, pl.ds(column, width)])
        second = dot(tops, low[:, pl.ds(column, width)])
        total = first[0:half] + first[half : 2 * half] + second
        first = dot(both, act_high[...])
        second = dot(tops, act_low[...])
        mixed = first[0:half] + first[half : 2 * half] + second
        for number in range(len(turns)):
            here = slice(number * block, (number + 1) * block)
            out[number, :, 0:width] = total[here]
            out[number, :, width : width + feat] = mixed[here]


def whole_in_vmem(count):
    return [pl.BlockSpec(memory_space=pltpu.VMEM)] * count


def act_bands(turns, place, weights, parts, chips, block, width):
    rows, feat = parts[0].shape
    return pl.pallas_call(
        functools.partial(act_kernel, turns, block),
        out_shape=[jax.ShapeDtypeStruct((len(turns), block, width), F32)] * chips,
        in_specs=[pl.BlockSpec(memory_space=pltpu.SMEM)] + whole_in_vmem(5),
        out_specs=whole_in_vmem(chips),
        scratch_shapes=[
            pltpu.VMEM((4 * rows, feat + width - TILE), BF16),
            pltpu.VMEM((4 * rows, feat + width - TILE), BF16),
            pltpu.VMEM((TILE, 4 * rows), F32),
        ],
        compiler_params=pltpu.CompilerParams(vmem_limit_bytes=VMEM_LIMIT),
    )(place, weights, *parts)


def grad_bands(turns, place, weights, grads, acts, chips, block, width):
    rows, feat = grads[0].shape
    return pl.pallas_call(
        functools.partial(grad_kernel, turns, block),
        out_shape=[jax.ShapeDtypeStruct((len(turns), block, width + feat), F32)] * chips,
        in_specs=[pl.BlockSpec(memory_space=pltpu.SMEM)] + whole_in_vmem(9),
        out_specs=whole_in_vmem(chips),
        scratch_shapes=[
            pltpu.VMEM((4 * rows, feat + width - TILE), BF16),
            pltpu.VMEM((4 * rows, feat + width - TILE), BF16),
            pltpu.VMEM((4 * rows, feat), BF16),
            pltpu.VMEM((4 * rows, feat), BF16),
            pltpu.VMEM((TILE, 4 * rows), F32),
        ],
        compiler_params=pltpu.CompilerParams(vmem_limit_bytes=VMEM_LIMIT),
    )(place, weights, *grads, *acts)


def unfold(bands, full):
    tiles = full.shape[0] // TILE
    for i in range(tiles):
        for step in range(tiles // 2 + 1):
            j = (i + step) % tiles
            here = bands[i * TILE : (i + 1) * TILE, step * TILE : (step + 1) * TILE]
            full[i * TILE : (i + 1) * TILE, j * TILE : (j + 1) * TILE] = here
            if 0 < step < tiles // 2:
                full[j * TILE : (j + 1) * TILE, i * TILE : (i + 1) * TILE] = here.T


def damping(full):
    size = full.shape[0]
    value = full[...]
    lanes = lax.broadcasted_iota(jnp.int32, (size, size), 1)
    sublanes = lax.broadcasted_iota(jnp.int32, (size, size), 0)
    trace = jnp.sum(jnp.sum(jnp.where(lanes == sublanes, value, 0.0), axis=0, keepdims=True), axis=1, keepdims=True)
    largest = jnp.max(jnp.sum(jnp.abs(value), axis=0, keepdims=True), axis=1, keepdims=True)
    damp = trace * (0.1 / size)
    return damp, 1.0 / (largest + damp)


def times(left, high, low):
    rows = left.shape[0]
    top, rest = split(left)
    first = dot(jnp.concatenate([top, rest], axis=0), high[...])
    return first[0:rows] + first[rows : 2 * rows] + dot(top, low[...])


def chain_kernel(devices, place, *refs):
    act_blocks, mixed_blocks = refs[:devices], refs[devices : 2 * devices]
    momentum, weights, act_out, grad_out, moment_out, weight_out = refs[2 * devices : 2 * devices + 6]
    bands, full, act_high, act_low, high, low, mid_high, mid_low = refs[2 * devices + 6 :]
    block, feat = momentum.shape
    width = act_blocks[0].shape[1]
    mine = place[0]
    own = pl.ds(pl.multiple_of(mine * block, block), block)
    here = [pl.ds(pl.multiple_of((mine ^ k) * block, block), block) for k in range(devices)]
    for k in range(devices):
        bands[here[k], :] = act_blocks[k][...]
    unfold(bands, full)
    act_out[...] = full[own, :]
    act_damp, act_alpha = damping(full)
    top, rest = split(full[...])
    act_high[...] = top
    act_low[...] = rest
    for k in range(devices):
        bands[here[k], :] = mixed_blocks[k][:, 0:width]
    unfold(bands, full)
    rows = full[own, :]
    grad_out[...] = rows
    damp, alpha = damping(full)
    top, rest = split(full[...])
    high[...] = top
    low[...] = rest
    for k in range(devices):
        top, rest = split(mixed_blocks[k][:, width : width + feat])
        mid_high[here[k], :] = top
        mid_low[here[k], :] = rest
    lanes = lax.broadcasted_iota(jnp.int32, (block, feat), 1)
    sublanes = lax.broadcasted_iota(jnp.int32, (block, feat), 0)
    unit = jnp.where(lanes == sublanes + mine * block, 1.0, 0.0).astype(F32)
    rest_rows = unit - alpha * (rows + damp * unit)
    once = 2.0 * rest_rows - alpha * (times(rest_rows, high, low) + damp * rest_rows)
    left = alpha * (unit + rest_rows + once - alpha * (times(once, high, low) + damp * once))
    half_way = times(left, mid_high, mid_low)
    value = half_way
    for _ in range(3):
        value = half_way + value - act_alpha * (times(value, act_high, act_low) + act_damp * value)
    moment = 0.9 * momentum[...] + act_alpha * value
    moment_out[...] = moment
    weight_out[...] = weights[...] - 0.5 * moment


def chain(place, act_blocks, mixed_blocks, momentum, weights):
    devices = len(act_blocks)
    block, feat = momentum.shape
    width = act_blocks[0].shape[1]
    square = (feat, feat)
    return pl.pallas_call(
        functools.partial(chain_kernel, devices),
        out_shape=[jax.ShapeDtypeStruct((block, feat), F32)] * 4,
        in_specs=[pl.BlockSpec(memory_space=pltpu.SMEM)] + whole_in_vmem(2 * devices + 2),
        out_specs=whole_in_vmem(4),
        scratch_shapes=[pltpu.VMEM((feat, width), F32), pltpu.VMEM(square, F32)]
        + [pltpu.VMEM(square, BF16)] * 6,
        compiler_params=pltpu.CompilerParams(vmem_limit_bytes=VMEM_LIMIT),
    )(place, *act_blocks, *mixed_blocks, momentum, weights)


def swap(value, axis, step):
    size = lax.axis_size(axis)
    return lax.ppermute(value, axis, [(i, i ^ step) for i in range(size)])


def kept_rows(routes, counts, experts):
    samples = routes.shape[0]
    ids = jnp.arange(experts, dtype=jnp.int32)
    hit = jnp.sum((routes.T[None, :, :] == ids[:, None, None]).astype(jnp.int32), axis=1, dtype=jnp.int32)
    before = jnp.triu(jnp.ones((samples, samples), BF16), 1)
    rank = dot(hit.astype(BF16), before)
    return jnp.where(rank < counts[0].astype(F32)[:, None], hit, 0).astype(F32)


def on_device(acts, grads_out, routes, counts, old_act_factor, old_grad_factor, momentum, weights):
    devices, experts = lax.axis_size("dp"), lax.axis_size("expert")
    chips = devices // 2
    feat, block = acts.shape[1], weights.shape[1]
    width = feat // 2 + TILE
    mine = lax.axis_index("dp")
    place = jnp.stack([mine, lax.axis_index("expert")]).astype(jnp.int32)

    keep = kept_rows(routes, counts, experts)
    acts_far, grads_far = swap(acts, "expert", 1), swap(grads_out, "expert", 1)
    keep = jnp.concatenate([keep, swap(keep, "expert", 1)], axis=1)
    keep = jnp.concatenate([keep, swap(keep, "dp", 1)], axis=1)
    total = lax.psum(jnp.sum(keep[:, 0 : acts.shape[0]], axis=1), ("dp", "expert"))
    total = jnp.maximum(lax.dynamic_slice_in_dim(total, lax.axis_index("expert"), 1), 1.0)
    act_parts = (acts, acts_far, swap(acts, "dp", 1), swap(acts_far, "dp", 1))
    grad_parts = (grads_out, grads_far, swap(grads_out, "dp", 1), swap(grads_far, "dp", 1))

    def to_owners(bands):
        total = bands[0]
        for k in range(1, chips):
            total = total + swap(bands[k], "dp", 2 * k)
        return total

    def own_band(old):
        start = mine * block // TILE * TILE
        wide = jnp.concatenate([old[0], old[0][:, 0 : width - TILE]], axis=1)
        return lax.dynamic_slice_in_dim(wide, start, width, 1)

    def across(near, far):
        for number in range(far.shape[0]):
            near = near + swap(far[number], "expert", 2 * (number + 1))
        return near

    def to_all(value):
        blocks = []
        for k in range(chips):
            blocks.append(swap(value, "dp", 2 * k) if k else value)
            blocks.append(swap(blocks[-1], "dp", 1))
        return blocks

    turns = tuple(range(experts // 2))
    act_sums = to_owners(act_bands(turns, place, keep, act_parts, chips, block, width))
    far_sums = to_owners(grad_bands(turns[1:], place, keep, grad_parts, act_parts, chips, block, width))
    near_sums = to_owners(grad_bands(turns[:1], place, keep, grad_parts, act_parts, chips, block, width))
    act_band = 0.5 * own_band(old_act_factor) + 0.5 * (across(act_sums[0], act_sums[1:]) / total[0])
    mixed = across(near_sums[0], far_sums) / total[0]
    mixed = jnp.concatenate(
        [0.5 * own_band(old_grad_factor) + 0.5 * mixed[:, 0:width], mixed[:, width:]], axis=1
    )
    outs = chain(place, to_all(act_band), to_all(mixed), momentum[0], weights[0])
    return tuple(out[None] for out in outs)


def solution(mesh):
    rows = P(("dp", "expert"), None)
    matrix = P("expert", "dp", None)
    return jax.shard_map(
        on_device,
        mesh=mesh,
        in_specs=(rows,) * 4 + (matrix,) * 4,
        out_specs=(matrix,) * 4,
        check_vma=False,
    )
```

```python
import functools
import math

import jax
import jax.numpy as jnp
from jax import lax
from jax.experimental import pallas as pl
from jax.experimental.pallas import tpu as pltpu
from jax.sharding import PartitionSpec as P

F32 = jnp.float32
BF16 = jnp.bfloat16
TILE = 128
VMEM_LIMIT = 56 * 1024 * 1024


def split(value):
    high = value.astype(BF16)
    return high, (value - high.astype(F32)).astype(BF16)


def dot(left, right):
    return jnp.dot(left, right, preferred_element_type=F32)


def band_place(owner, block):
    per_tile = TILE // block
    if per_tile == 1:
        return pl.multiple_of(owner * TILE, TILE), 0
    return (
        pl.multiple_of(lax.div(owner, per_tile) * TILE, TILE),
        pl.multiple_of(lax.rem(owner, per_tile) * block, block),
    )


def split_rows(parts, high, low, feat):
    extra = high.shape[1] - feat
    for number, part in enumerate(parts):
        rows = part.shape[0]
        here = slice(number * rows, (number + 1) * rows)
        top, rest = split(part[...])
        high[here, 0:feat] = top
        low[here, 0:feat] = rest
        if extra:
            high[here, feat : feat + extra] = top[:, 0:extra]
            low[here, feat : feat + extra] = rest[:, 0:extra]


def left_rows(parts, turned, column, row, block):
    for number, part in enumerate(parts):
        rows = part.shape[0]
        turned[:, number * rows : (number + 1) * rows] = part[:, pl.ds(column, TILE)].T
    return turned[pl.ds(row, block), :]


def weighted(rows, weights, lanes):
    halves = [split(rows * weights[pl.ds(lane, 1), :]) for lane in lanes]
    tops = [half[0] for half in halves]
    return jnp.concatenate(tops + [half[1] for half in halves], axis=0), jnp.concatenate(tops, axis=0)


def three(both, tops, high, low):
    half = tops.shape[0]
    first = dot(both, high)
    return first[0:half] + first[half : 2 * half] + dot(tops, low)


def orders(chips):
    bits = list(range(chips.bit_length() - 1))
    return bits, bits[1:] + bits[:1]


def held_and_sent(chips, order):
    if not order:
        return [0], []
    held = [k for k in range(chips) if not (k >> order[0]) & 1]
    return held, [k | (1 << order[0]) for k in held]


def slots(chips):
    places = {}
    for half, order in enumerate(orders(chips)):
        for which, group in enumerate(held_and_sent(chips, order)):
            for position, k in enumerate(group):
                places[k, half] = (2 * half + which, position)
    return places


def store(outs, seeds, place, number, columns, value):
    output, position = place
    if seeds:
        value = value + seeds[output][position, number, :, columns]
    outs[output][position, number, :, columns] = value


def act_kernel(turns, block, chips, seeded, place, weights, *refs):
    parts, refs = refs[:2], refs[2:]
    seeds, refs = (refs[:4], refs[4:]) if seeded else ((), refs)
    outs, (high, low, turned) = refs[:4], refs[4:]
    feat = parts[0].shape[1]
    width = outs[0].shape[3]
    mine, expert = place[0], place[1]
    split_rows(parts, high, low, feat)
    lanes = [expert ^ (2 * turn) for turn in turns]
    places = slots(chips)
    rows = lax.broadcasted_iota(jnp.int32, (block, width), 0)
    columns = lax.broadcasted_iota(jnp.int32, (block, width), 1)
    corner = jnp.logical_and(rows == block - 1, columns == 0)
    for k in range(chips):
        column, row = band_place(mine ^ (2 * k), block)
        both, tops = weighted(left_rows(parts, turned, column, row, block), weights, lanes)
        total = three(both, tops, high[:, pl.ds(column, width)], low[:, pl.ds(column, width)])
        for number, lane in enumerate(lanes):
            count = jnp.sum(weights[pl.ds(lane, 1), :], axis=1, keepdims=True)
            value = jnp.where(corner, count, total[number * block : (number + 1) * block])
            for half in range(2):
                here = value[half * (block // 2) : (half + 1) * (block // 2)]
                store(outs, seeds, places[k, half], number, slice(0, width), here)


def grad_kernel(turns, block, chips, seeded, place, weights, *refs):
    grads, acts, refs = refs[:2], refs[2:4], refs[4:]
    seeds, refs = (refs[:4], refs[4:]) if seeded else ((), refs)
    outs, (high, low, act_high, act_low, turned) = refs[:4], refs[4:]
    feat = grads[0].shape[1]
    width = outs[0].shape[3] - feat
    mine, expert = place[0], place[1]
    split_rows(grads, high, low, feat)
    split_rows(acts, act_high, act_low, feat)
    lanes = [expert ^ (2 * turn) for turn in turns]
    places = slots(chips)
    for k in range(chips):
        column, row = band_place(mine ^ (2 * k), block)
        both, tops = weighted(left_rows(grads, turned, column, row, block), weights, lanes)
        total = three(both, tops, high[:, pl.ds(column, width)], low[:, pl.ds(column, width)])
        mixed = three(both, tops, act_high[...], act_low[...])
        for number in range(len(lanes)):
            for half in range(2):
                first = number * block + half * (block // 2)
                here = slice(first, first + block // 2)
                store(outs, seeds, places[k, half], number, slice(0, width), total[here])
                store(outs, seeds, places[k, half], number, slice(width, width + feat), mixed[here])


def whole_in_vmem(count):
    return [pl.BlockSpec(memory_space=pltpu.VMEM)] * count


def cost(flops, *arrays):
    size = sum(4 * math.prod(array.shape) for array in arrays)
    return pl.CostEstimate(flops=flops, bytes_accessed=size, transcendentals=0)


def bands(body, turns, place, weights, parts, seeds, chips, block, width):
    rows, feat = parts[0].shape
    extended = pltpu.VMEM((2 * rows, feat + feat // 2), BF16)
    plain = pltpu.VMEM((2 * rows, feat), BF16)
    scratch = [extended, extended] + ([plain, plain] if len(parts) > 2 else [])
    shapes = [
        jax.ShapeDtypeStruct((len(group), len(turns), block // 2, width), F32)
        for order in orders(chips)
        for group in held_and_sent(chips, order)
    ]
    operands = (weights, *parts, *seeds)
    return pl.pallas_call(
        functools.partial(body, turns, block, chips, bool(seeds)),
        out_shape=shapes,
        in_specs=[pl.BlockSpec(memory_space=pltpu.SMEM)] + whole_in_vmem(len(operands)),
        out_specs=whole_in_vmem(4),
        scratch_shapes=scratch + [pltpu.VMEM((TILE, 2 * rows), F32)],
        cost_estimate=cost(12 * rows * chips * block * width * len(turns), *operands, *shapes),
        compiler_params=pltpu.CompilerParams(vmem_limit_bytes=VMEM_LIMIT),
    )(place, *operands)


def unfold(bands, full):
    tiles = full.shape[0] // TILE
    first_column = lax.broadcasted_iota(jnp.int32, (TILE, TILE), 1) == 0
    for i in range(tiles):
        for step in range(tiles // 2 + 1):
            j = (i + step) % tiles
            here = bands[i * TILE : (i + 1) * TILE, step * TILE : (step + 1) * TILE]
            if step == 0:
                here = jnp.where(first_column, here.T, here)
            full[i * TILE : (i + 1) * TILE, j * TILE : (j + 1) * TILE] = here
            if 0 < step < tiles // 2:
                full[j * TILE : (j + 1) * TILE, i * TILE : (i + 1) * TILE] = here.T


def damping(full):
    size = full.shape[0]
    value = full[...]
    lanes = lax.broadcasted_iota(jnp.int32, (size, size), 1)
    sublanes = lax.broadcasted_iota(jnp.int32, (size, size), 0)
    trace = jnp.sum(jnp.sum(jnp.where(lanes == sublanes, value, 0.0), axis=0, keepdims=True), axis=1, keepdims=True)
    largest = jnp.max(jnp.sum(jnp.abs(value), axis=0, keepdims=True), axis=1, keepdims=True)
    damp = trace * (0.1 / size)
    return damp, 1.0 / (largest + damp)


def times(left, high, low):
    rows = left.shape[0]
    top, rest = split(left)
    first = dot(jnp.concatenate([top, rest], axis=0), high[...])
    return first[0:rows] + first[rows : 2 * rows] + dot(top, low[...])


def chain_kernel(devices, place, *refs):
    pieces = 2 * devices
    act_blocks, mixed_blocks = refs[:pieces], refs[pieces : 2 * pieces]
    momentum, weights, act_out, grad_out, moment_out, weight_out = refs[2 * pieces : 2 * pieces + 6]
    bands, full, act_high, act_low, high, low, mid_high, mid_low = refs[2 * pieces + 6 :]
    block, feat = momentum.shape
    width = act_blocks[0].shape[1]
    mine = place[0]
    own = pl.ds(pl.multiple_of(mine * block, block), block)
    step = block // 2
    here = [
        pl.ds(pl.multiple_of((mine ^ k) * block + half * step, step), step)
        for k in range(devices)
        for half in range(2)
    ]
    for k in range(pieces):
        bands[here[k], :] = act_blocks[k][...]
    unfold(bands, full)
    act_out[...] = full[own, :]
    act_damp, act_alpha = damping(full)
    top, rest = split(full[...])
    act_high[...] = top
    act_low[...] = rest
    for k in range(pieces):
        bands[here[k], :] = mixed_blocks[k][:, 0:width]
    unfold(bands, full)
    rows = full[own, :]
    grad_out[...] = rows
    damp, alpha = damping(full)
    top, rest = split(full[...])
    high[...] = top
    low[...] = rest
    for k in range(pieces):
        top, rest = split(mixed_blocks[k][:, width : width + feat])
        mid_high[here[k], :] = top
        mid_low[here[k], :] = rest
    lanes = lax.broadcasted_iota(jnp.int32, (block, feat), 1)
    sublanes = lax.broadcasted_iota(jnp.int32, (block, feat), 0)
    unit = jnp.where(lanes == sublanes + mine * block, 1.0, 0.0).astype(F32)
    rest_rows = unit - alpha * (rows + damp * unit)
    once = 2.0 * rest_rows - alpha * (times(rest_rows, high, low) + damp * rest_rows)
    left = alpha * (unit + rest_rows + once - alpha * (times(once, high, low) + damp * once))
    half_way = times(left, mid_high, mid_low)
    value = half_way
    for _ in range(3):
        value = half_way + value - act_alpha * (times(value, act_high, act_low) + act_damp * value)
    moment = 0.9 * momentum[...] + act_alpha * value
    moment_out[...] = moment
    weight_out[...] = weights[...] - 0.5 * moment


def chain(place, act_blocks, mixed_blocks, momentum, weights):
    devices = len(act_blocks) // 2
    block, feat = momentum.shape
    width = act_blocks[0].shape[1]
    square = (feat, feat)
    return pl.pallas_call(
        functools.partial(chain_kernel, devices),
        out_shape=[jax.ShapeDtypeStruct((block, feat), F32)] * 4,
        in_specs=[pl.BlockSpec(memory_space=pltpu.SMEM)] + whole_in_vmem(4 * devices + 2),
        out_specs=whole_in_vmem(4),
        scratch_shapes=[pltpu.VMEM((feat, width), F32), pltpu.VMEM(square, F32)]
        + [pltpu.VMEM(square, BF16)] * 6,
        cost_estimate=cost(36 * block * feat * feat, *act_blocks, *mixed_blocks),
        compiler_params=pltpu.CompilerParams(vmem_limit_bytes=VMEM_LIMIT),
    )(place, *act_blocks, *mixed_blocks, momentum, weights)


def swap(value, axis, step):
    size = lax.axis_size(axis)
    return lax.ppermute(value, axis, [(i, i ^ step) for i in range(size)])


def kept_rows(routes, counts, experts):
    samples = routes.shape[0]
    ids = jnp.arange(experts, dtype=jnp.int32)
    hit = jnp.sum((routes.T[None, :, :] == ids[:, None, None]).astype(jnp.int32), axis=1, dtype=jnp.int32)
    before = jnp.triu(jnp.ones((samples, samples), BF16), 1)
    rank = dot(hit.astype(BF16), before)
    return jnp.where(rank < counts[0].astype(F32)[:, None], hit, 0).astype(F32)


def to_owner(pieces, chips):
    results = []
    for half, order in enumerate(orders(chips)):
        keep, leave = pieces[2 * half], pieces[2 * half + 1]
        held, _ = held_and_sent(chips, order)
        got = swap(leave, "dp", 2 << order[0])
        sums = {k: keep[i] + got[i] for i, k in enumerate(held)}
        for bit in order[1:]:
            low = [k for k in sums if not (k >> bit) & 1]
            high = [sums[k | (1 << bit)] for k in low]
            got = swap(jnp.stack(high), "dp", 2 << bit)
            sums = {k: sums[k] + got[i] for i, k in enumerate(low)}
        results.append(sums[0])
    return results


def across(near, far):
    for number in range(far.shape[0]):
        near = near + swap(far[number], "expert", 2 * (number + 1))
    return near


def to_all(halves, chips):
    pieces = {}
    for half, order in enumerate(orders(chips)):
        held = {0: halves[half]}
        for bit in order:
            for k in list(held):
                held[k | (1 << bit)] = swap(held[k], "dp", 2 << bit)
        for k in range(chips):
            pieces[2 * k, half] = held[k]
            pieces[2 * k + 1, half] = swap(held[k], "dp", 1)
    return [pieces[k, half] for k in range(2 * chips) for half in range(2)]


def on_device(acts, grads_out, routes, counts, old_act_factor, old_grad_factor, momentum, weights):
    devices, experts = lax.axis_size("dp"), lax.axis_size("expert")
    chips = devices // 2
    feat, block = acts.shape[1], weights.shape[1]
    width = feat // 2 + TILE
    mine = lax.axis_index("dp")
    place = jnp.stack([mine, lax.axis_index("expert")]).astype(jnp.int32)

    acts_far = swap(acts, "expert", 1)
    keep = kept_rows(routes, counts, experts)
    grads_out, keep = lax.optimization_barrier((grads_out, keep))
    keep_far = swap(keep, "expert", 1)
    grads_far = swap(grads_out, "expert", 1)
    near_keep = jnp.concatenate([keep, swap(keep, "dp", 1)], axis=1)
    far_keep = jnp.concatenate([keep_far, swap(keep_far, "dp", 1)], axis=1)
    near_acts = (acts, swap(acts, "dp", 1))
    near_grads = (grads_out, swap(grads_out, "dp", 1))

    def own_band(old):
        start = mine * block // TILE * TILE
        wide = jnp.concatenate([old[0], old[0][:, 0 : width - TILE]], axis=1)
        return 0.5 * lax.dynamic_slice_in_dim(wide, start, width, 1)

    old_act, old_grad = own_band(old_act_factor), own_band(old_grad_factor)
    turns = tuple(range(experts // 2))
    size = (chips, block, width)
    mixed_size = (chips, block, width + feat)
    act_seeds = bands(act_kernel, turns, place, near_keep, near_acts, (), *size)
    grad_parts = near_grads + near_acts
    far_seeds = bands(grad_kernel, turns[1:], place, near_keep, grad_parts, (), *mixed_size)
    near_seeds = bands(grad_kernel, turns[:1], place, near_keep, grad_parts, (), *mixed_size)

    far_acts = (acts_far, swap(acts_far, "dp", 1))
    act_pieces = bands(act_kernel, turns, place, far_keep, far_acts, act_seeds, *size)
    grads_far, act_pieces = lax.optimization_barrier((grads_far, act_pieces))
    grad_parts = (grads_far, swap(grads_far, "dp", 1)) + far_acts
    far_pieces = bands(grad_kernel, turns[1:], place, far_keep, grad_parts, far_seeds, *mixed_size)
    near_seeds, far_pieces = lax.optimization_barrier((near_seeds, far_pieces))
    near_pieces = bands(grad_kernel, turns[:1], place, far_keep, grad_parts, near_seeds, *mixed_size)

    act_sums = [across(total[0], total[1:]) for total in to_owner(act_pieces, chips)]
    far_sums = to_owner(far_pieces, chips)
    near_sums = to_owner(near_pieces, chips)
    total = jnp.maximum(act_sums[1][-1:, 0:1], 1.0)
    step = block // 2
    act_halves, mixed_halves = [], []
    for half in range(2):
        here = slice(half * step, (half + 1) * step)
        act_halves.append(old_act[here] + 0.5 * (act_sums[half] / total))
        mixed = across(near_sums[half][0], far_sums[half]) / total
        mixed = jnp.concatenate([old_grad[here] + 0.5 * mixed[:, 0:width], mixed[:, width:]], axis=1)
        mixed_halves.append(mixed)
    outs = chain(place, to_all(act_halves, chips), to_all(mixed_halves, chips), momentum[0], weights[0])
    return tuple(out[None] for out in outs)


def solution(mesh):
    rows = P(("dp", "expert"), None)
    matrix = P("expert", "dp", None)
    return jax.shard_map(
        on_device,
        mesh=mesh,
        in_specs=(rows,) * 4 + (matrix,) * 4,
        out_specs=(matrix,) * 4,
        check_vma=False,
    )
```

```python
import functools

import jax
import jax.numpy as jnp
from jax import lax
from jax.experimental import pallas as pl
from jax.experimental.pallas import tpu as pltpu
from jax.sharding import PartitionSpec as P

F32 = jnp.float32
BF16 = jnp.bfloat16
TILE = 128
VMEM_LIMIT = 56 * 1024 * 1024


def split(value):
    high = value.astype(BF16)
    return high, (value - high.astype(F32)).astype(BF16)


def dot(left, right):
    return jnp.dot(left, right, preferred_element_type=F32)


def band_place(owner, block):
    per_tile = TILE // block
    if per_tile == 1:
        return pl.multiple_of(owner * TILE, TILE), 0
    return (
        pl.multiple_of(lax.div(owner, per_tile) * TILE, TILE),
        pl.multiple_of(lax.rem(owner, per_tile) * block, block),
    )


def split_rows(parts, samples, high, low, feat):
    extra = high.shape[1] - feat
    for number, part in enumerate(parts):
        here = slice(number * samples, (number + 1) * samples)
        top, rest = split(part[0:samples, :])
        high[here, 0:feat] = top
        low[here, 0:feat] = rest
        if extra:
            high[here, feat : feat + extra] = top[:, 0:extra]
            low[here, feat : feat + extra] = rest[:, 0:extra]


def left_rows(parts, samples, turned, column, row, block):
    for number, part in enumerate(parts):
        here = slice(number * samples, (number + 1) * samples)
        turned[:, here] = part[0:samples, pl.ds(column, TILE)].T
    return turned[pl.ds(row, block), :]


def keep_place(expert, samples, feat):
    per_row = feat // samples
    return lax.div(expert, per_row), pl.multiple_of(lax.rem(expert, per_row) * samples, TILE)


def keep_row(parts, samples, expert):
    row, column = keep_place(expert, samples, parts[0].shape[1])
    return jnp.concatenate([part[pl.ds(samples + row, 1), pl.ds(column, samples)] for part in parts], axis=1)


def weighted(rows, keeps):
    halves = [split(rows * keep) for keep in keeps]
    tops = [half[0] for half in halves]
    return jnp.concatenate(tops + [half[1] for half in halves], axis=0), jnp.concatenate(tops, axis=0)


def three(both, tops, high, low):
    half = tops.shape[0]
    first = dot(both, high)
    return first[0:half] + first[half : 2 * half] + dot(tops, low)


def orders(chips):
    bits = list(range(chips.bit_length() - 1))
    return bits, bits[1:] + bits[:1]


def held_and_sent(chips, order):
    if not order:
        return [0], []
    held = [k for k in range(chips) if not (k >> order[0]) & 1]
    return held, [k | (1 << order[0]) for k in held]


def slots(chips):
    places = {}
    for half, order in enumerate(orders(chips)):
        for which, group in enumerate(held_and_sent(chips, order)):
            for position, k in enumerate(group):
                places[k, half] = (2 * half + which, position)
    return places


def store(outs, seeds, place, number, columns, value):
    output, position = place
    for out in outs[0::4]:
        if number < out.shape[1]:
            break
        output, number = output + 4, number - out.shape[1]
    if seeds:
        value = value + seeds[output][position, number, :, columns]
    outs[output][position, number, :, columns] = value


def prepare_kernel(routes, counts, acts, out):
    samples, feat = acts.shape
    experts = counts.shape[1]
    out[0:samples, :] = acts[...]
    out[samples:, :] = jnp.zeros((out.shape[0] - samples, feat), F32)
    hits = []
    for expert in range(experts):
        same = [jnp.where(routes[k : k + 1, :] == expert, 1.0, 0.0) for k in range(routes.shape[0])]
        hits.append(sum(same[1:], same[0]))
    hit = jnp.concatenate(hits, axis=0)
    first = lax.broadcasted_iota(jnp.int32, (samples, samples), 0)
    second = lax.broadcasted_iota(jnp.int32, (samples, samples), 1)
    rank = dot(hit.astype(BF16), jnp.where(first < second, 1.0, 0.0).astype(BF16))
    per_row = feat // samples
    for expert in range(experts):
        limit = counts[0, expert].astype(F32)
        keep = jnp.where(rank[expert : expert + 1, :] < limit, hits[expert], 0.0)
        row, column = samples + expert // per_row, expert % per_row * samples
        out[row : row + 1, column : column + samples] = keep


def act_kernel(turns, block, chips, seeded, samples, place, *refs):
    parts, refs = refs[:2], refs[2:]
    refs, (high, low, turned) = refs[:-3], refs[-3:]
    seeds, outs = (refs[: len(refs) // 2], refs[len(refs) // 2 :]) if seeded else ((), refs)
    feat = parts[0].shape[1]
    width = outs[0].shape[3]
    mine, expert = place[0], place[1]
    split_rows(parts, samples, high, low, feat)
    keeps = [keep_row(parts, samples, expert ^ (2 * turn)) for turn in turns]
    places = slots(chips)
    rows = lax.broadcasted_iota(jnp.int32, (block, width), 0)
    columns = lax.broadcasted_iota(jnp.int32, (block, width), 1)
    corner = jnp.logical_and(rows == block - 1, columns == 0)
    for k in range(chips):
        column, row = band_place(mine ^ (2 * k), block)
        both, tops = weighted(left_rows(parts, samples, turned, column, row, block), keeps)
        total = three(both, tops, high[:, pl.ds(column, width)], low[:, pl.ds(column, width)])
        for number, keep in enumerate(keeps):
            count = jnp.sum(keep, axis=1, keepdims=True)
            value = jnp.where(corner, count, total[number * block : (number + 1) * block])
            for half in range(2):
                here = value[half * (block // 2) : (half + 1) * (block // 2)]
                store(outs, seeds, places[k, half], number, slice(0, width), here)


def grad_kernel(turns, block, chips, seeded, samples, place, *refs):
    grads, acts, refs = refs[:2], refs[2:4], refs[4:]
    refs, (high, low, act_high, act_low, turned) = refs[:-5], refs[-5:]
    seeds, outs = (refs[: len(refs) // 2], refs[len(refs) // 2 :]) if seeded else ((), refs)
    feat = grads[0].shape[1]
    width = outs[0].shape[3] - feat
    mine, expert = place[0], place[1]
    split_rows(grads, samples, high, low, feat)
    split_rows(acts, samples, act_high, act_low, feat)
    keeps = [keep_row(acts, samples, expert ^ (2 * turn)) for turn in turns]
    places = slots(chips)
    for k in range(chips):
        column, row = band_place(mine ^ (2 * k), block)
        both, tops = weighted(left_rows(grads, samples, turned, column, row, block), keeps)
        total = three(both, tops, high[:, pl.ds(column, width)], low[:, pl.ds(column, width)])
        mixed = three(both, tops, act_high[...], act_low[...])
        for number in range(len(keeps)):
            for half in range(2):
                first = number * block + half * (block // 2)
                here = slice(first, first + block // 2)
                store(outs, seeds, places[k, half], number, slice(0, width), total[here])
                store(outs, seeds, places[k, half], number, slice(width, width + feat), mixed[here])


def whole_in_vmem(count):
    return [pl.BlockSpec(memory_space=pltpu.VMEM)] * count


def prepare(routes, counts, acts):
    samples, feat = acts.shape
    rows = samples + 8 * -(-counts.shape[1] * samples // (8 * feat))
    return pl.pallas_call(
        prepare_kernel,
        out_shape=jax.ShapeDtypeStruct((rows, feat), F32),
        in_specs=[
            pl.BlockSpec(memory_space=pltpu.VMEM),
            pl.BlockSpec(memory_space=pltpu.SMEM),
            pl.BlockSpec(memory_space=pltpu.VMEM),
        ],
        out_specs=pl.BlockSpec(memory_space=pltpu.VMEM),
        compiler_params=pltpu.CompilerParams(vmem_limit_bytes=VMEM_LIMIT),
    )(routes.T, counts, acts)


def bands(body, groups, place, parts, seeds, samples, chips, block, width):
    turns = tuple(range(sum(groups)))
    feat = parts[0].shape[1]
    extended = pltpu.VMEM((2 * samples, feat + feat // 2), BF16)
    plain = pltpu.VMEM((2 * samples, feat), BF16)
    scratch = [extended, extended] + ([plain, plain] if len(parts) > 2 else [])
    shapes = [
        jax.ShapeDtypeStruct((len(group), count, block // 2, width), F32)
        for count in groups
        for order in orders(chips)
        for group in held_and_sent(chips, order)
    ]
    operands = (*parts, *seeds)
    return pl.pallas_call(
        functools.partial(body, turns, block, chips, bool(seeds), samples),
        out_shape=shapes,
        in_specs=[pl.BlockSpec(memory_space=pltpu.SMEM)] + whole_in_vmem(len(operands)),
        out_specs=whole_in_vmem(len(shapes)),
        scratch_shapes=scratch + [pltpu.VMEM((TILE, 2 * samples), F32)],
        compiler_params=pltpu.CompilerParams(vmem_limit_bytes=VMEM_LIMIT),
    )(place, *operands)


def unfold(bands, full):
    tiles = full.shape[0] // TILE
    first_column = lax.broadcasted_iota(jnp.int32, (TILE, TILE), 1) == 0
    for i in range(tiles):
        for step in range(tiles // 2 + 1):
            j = (i + step) % tiles
            here = bands[i * TILE : (i + 1) * TILE, step * TILE : (step + 1) * TILE]
            if step == 0:
                here = jnp.where(first_column, here.T, here)
            full[i * TILE : (i + 1) * TILE, j * TILE : (j + 1) * TILE] = here
            if 0 < step < tiles // 2:
                full[j * TILE : (j + 1) * TILE, i * TILE : (i + 1) * TILE] = here.T


def damping(full):
    size = full.shape[0]
    value = full[...]
    lanes = lax.broadcasted_iota(jnp.int32, (size, size), 1)
    sublanes = lax.broadcasted_iota(jnp.int32, (size, size), 0)
    trace = jnp.sum(jnp.sum(jnp.where(lanes == sublanes, value, 0.0), axis=0, keepdims=True), axis=1, keepdims=True)
    largest = jnp.max(jnp.sum(jnp.abs(value), axis=0, keepdims=True), axis=1, keepdims=True)
    damp = trace * (0.1 / size)
    return damp, 1.0 / (largest + damp)


def times(left, high, low):
    rows = left.shape[0]
    top, rest = split(left)
    first = dot(jnp.concatenate([top, rest], axis=0), high[...])
    return first[0:rows] + first[rows : 2 * rows] + dot(top, low[...])


def chain_kernel(devices, place, *refs):
    pieces = 2 * devices
    act_blocks, mixed_blocks = refs[:pieces], refs[pieces : 2 * pieces]
    momentum, weights, act_out, grad_out, moment_out, weight_out = refs[2 * pieces : 2 * pieces + 6]
    bands, full, act_high, act_low, high, low, mid_high, mid_low = refs[2 * pieces + 6 :]
    block, feat = momentum.shape
    width = act_blocks[0].shape[1]
    mine = place[0]
    own = pl.ds(pl.multiple_of(mine * block, block), block)
    step = block // 2
    here = [
        pl.ds(pl.multiple_of((mine ^ k) * block + half * step, step), step)
        for k in range(devices)
        for half in range(2)
    ]
    for k in range(pieces):
        bands[here[k], :] = act_blocks[k][...]
    unfold(bands, full)
    act_out[...] = full[own, :]
    act_damp, act_alpha = damping(full)
    top, rest = split(full[...])
    act_high[...] = top
    act_low[...] = rest
    for k in range(pieces):
        bands[here[k], :] = mixed_blocks[k][:, 0:width]
    unfold(bands, full)
    rows = full[own, :]
    grad_out[...] = rows
    damp, alpha = damping(full)
    top, rest = split(full[...])
    high[...] = top
    low[...] = rest
    for k in range(pieces):
        top, rest = split(mixed_blocks[k][:, width : width + feat])
        mid_high[here[k], :] = top
        mid_low[here[k], :] = rest
    lanes = lax.broadcasted_iota(jnp.int32, (block, feat), 1)
    sublanes = lax.broadcasted_iota(jnp.int32, (block, feat), 0)
    unit = jnp.where(lanes == sublanes + mine * block, 1.0, 0.0).astype(F32)
    rest_rows = unit - alpha * (rows + damp * unit)
    once = 2.0 * rest_rows - alpha * (times(rest_rows, high, low) + damp * rest_rows)
    left = alpha * (unit + rest_rows + once - alpha * (times(once, high, low) + damp * once))
    half_way = times(left, mid_high, mid_low)
    value = half_way
    for _ in range(3):
        value = half_way + value - act_alpha * (times(value, act_high, act_low) + act_damp * value)
    moment = 0.9 * momentum[...] + act_alpha * value
    moment_out[...] = moment
    weight_out[...] = weights[...] - 0.5 * moment


def chain(place, act_blocks, mixed_blocks, momentum, weights):
    devices = len(act_blocks) // 2
    block, feat = momentum.shape
    width = act_blocks[0].shape[1]
    square = (feat, feat)
    return pl.pallas_call(
        functools.partial(chain_kernel, devices),
        out_shape=[jax.ShapeDtypeStruct((block, feat), F32)] * 4,
        in_specs=[pl.BlockSpec(memory_space=pltpu.SMEM)] + whole_in_vmem(4 * devices + 2),
        out_specs=whole_in_vmem(4),
        scratch_shapes=[pltpu.VMEM((feat, width), F32), pltpu.VMEM(square, F32)]
        + [pltpu.VMEM(square, BF16)] * 6,
        compiler_params=pltpu.CompilerParams(vmem_limit_bytes=VMEM_LIMIT),
    )(place, *act_blocks, *mixed_blocks, momentum, weights)


def swap(value, axis, step):
    size = lax.axis_size(axis)
    return lax.ppermute(value, axis, [(i, i ^ step) for i in range(size)])


class PlaneSum:
    def __init__(self, pieces, chips):
        self.steps = [list(order) for order in orders(chips)]
        self.offsets = [held_and_sent(chips, order)[0] for order in self.steps]
        self.held, self.leaving = list(pieces[0::2]), list(pieces[1::2])

    def send(self):
        self.got = [swap(value, "dp", 2 << order[0]) for value, order in zip(self.leaving, self.steps)]

    def add(self):
        self.leaving = []
        for half, order in enumerate(self.steps):
            offsets = self.offsets[half]
            sums = {k: self.held[half][i] + self.got[half][i] for i, k in enumerate(offsets)}
            order.pop(0)
            if order:
                offsets = [k for k in offsets if not (k >> order[0]) & 1]
                self.leaving.append(jnp.stack([sums[k | (1 << order[0])] for k in offsets]))
            self.offsets[half] = offsets
            self.held[half] = [sums[k] for k in offsets]

    def finish(self):
        while self.steps[0]:
            self.send()
            self.add()
        return [held[0] for held in self.held]


def across(far):
    return [swap(far[number], "expert", 2 * (number + 1)) for number in range(far.shape[0])]


def to_all(halves, chips):
    pieces = {}
    for half, order in enumerate(orders(chips)):
        held = {0: halves[half]}
        for bit in order:
            for k in list(held):
                held[k | (1 << bit)] = swap(held[k], "dp", 2 << bit)
        for k in range(chips):
            pieces[2 * k, half] = held[k]
            pieces[2 * k + 1, half] = swap(held[k], "dp", 1)
    return [pieces[k, half] for k in range(2 * chips) for half in range(2)]


def together(*values):
    return lax.optimization_barrier(values)


def on_device(acts, grads_out, routes, counts, old_act_factor, old_grad_factor, momentum, weights):
    devices, experts = lax.axis_size("dp"), lax.axis_size("expert")
    chips = devices // 2
    samples, feat, block = acts.shape[0], acts.shape[1], weights.shape[1]
    width = feat // 2 + TILE
    mine = lax.axis_index("dp")
    place = jnp.stack([mine, lax.axis_index("expert")]).astype(jnp.int32)

    def own_band(old):
        start = mine * block // TILE * TILE
        wide = jnp.concatenate([old[0], old[0][:, 0 : width - TILE]], axis=1)
        return 0.5 * lax.dynamic_slice_in_dim(wide, start, width, 1)

    turns = experts // 2
    size = (samples, chips, block, width)
    mixed_size = (samples, chips, block, width + feat)

    acts = prepare(routes, counts, acts)
    acts_far = swap(acts, "expert", 1)
    near_acts = (acts, swap(acts, "dp", 1))
    act_seeds = bands(act_kernel, (turns,), place, near_acts, (), *size)
    grads_out, act_seeds = together(grads_out, act_seeds)
    grads_far = swap(grads_out, "expert", 1)
    grad_parts = (grads_out, swap(grads_out, "dp", 1)) + near_acts
    grad_seeds = bands(grad_kernel, (1, turns - 1), place, grad_parts, (), *mixed_size)
    old_act, old_grad = own_band(old_act_factor), own_band(old_grad_factor)
    acts_far, grad_seeds, old_act, old_grad = together(acts_far, grad_seeds, old_act, old_grad)

    far_acts = (acts_far, swap(acts_far, "dp", 1))
    act_sum = PlaneSum(bands(act_kernel, (turns,), place, far_acts, act_seeds, *size), chips)
    act_sum.send()
    grads_far, act_sum.held = together(grads_far, act_sum.held)
    grad_parts = (grads_far, swap(grads_far, "dp", 1)) + far_acts
    act_sum.add()
    grad_seeds, act_sum.leaving = together(grad_seeds, act_sum.leaving)
    act_sum.send()
    pieces = bands(grad_kernel, (1, turns - 1), place, grad_parts, grad_seeds, *mixed_size)

    near_sum, far_sum = PlaneSum(pieces[:4], chips), PlaneSum(pieces[4:], chips)
    far_sum.send()
    act_sum.held, far_sum.held = together(act_sum.held, far_sum.held)
    act_sum.add()
    act_sums = act_sum.finish()
    act_across = [across(total[1:]) for total in act_sums]
    far_sum.add()
    far_sum.leaving, act_across = together(far_sum.leaving, act_across)
    far_sums = far_sum.finish()
    far_sums, near_sum.leaving = together(far_sums, near_sum.leaving)
    far_across = [across(total) for total in far_sums]
    near_sum.send()
    near_sum.add()

    step = block // 2
    act_totals = [sum(there, total[0]) for total, there in zip(act_sums, act_across)]
    total = jnp.maximum(act_totals[1][-1:, 0:1], 1.0)
    act_halves, mixed_halves = [], []
    for half in range(2):
        here = slice(half * step, (half + 1) * step)
        act_halves.append(old_act[here] + 0.5 * (act_totals[half] / total))
    near_sum.leaving, act_halves = together(near_sum.leaving, act_halves)
    near_sums = near_sum.finish()
    act_blocks = to_all(act_halves, chips)
    for half in range(2):
        here = slice(half * step, (half + 1) * step)
        mixed = sum(far_across[half], near_sums[half][0]) / total
        mixed = jnp.concatenate([old_grad[here] + 0.5 * mixed[:, 0:width], mixed[:, width:]], axis=1)
        mixed_halves.append(mixed)
    outs = chain(place, act_blocks, to_all(mixed_halves, chips), momentum[0], weights[0])
    return tuple(out[None] for out in outs)


def solution(mesh):
    rows = P(("dp", "expert"), None)
    matrix = P("expert", "dp", None)
    return jax.shard_map(
        on_device,
        mesh=mesh,
        in_specs=(rows,) * 4 + (matrix,) * 4,
        out_specs=(matrix,) * 4,
        check_vma=False,
    )
```

```python
import functools

import jax
import jax.numpy as jnp
from jax import lax
from jax.experimental import pallas as pl
from jax.experimental.pallas import tpu as pltpu
from jax.sharding import PartitionSpec as P

F32 = jnp.float32
BF16 = jnp.bfloat16
TILE = 128
MIB = 1024 * 1024


def split(value):
    high = value.astype(BF16)
    return high, (value - high.astype(F32)).astype(BF16)


def dot(left, right):
    return jnp.dot(left, right, preferred_element_type=F32)


def band_place(owner, block):
    per_tile = TILE // block
    if per_tile == 1:
        return pl.multiple_of(owner * TILE, TILE), 0
    return (
        pl.multiple_of(lax.div(owner, per_tile) * TILE, TILE),
        pl.multiple_of(lax.rem(owner, per_tile) * block, block),
    )


def split_rows(parts, samples, high, low, feat):
    extra = high.shape[1] - feat
    for number, part in enumerate(parts):
        here = slice(number * samples, (number + 1) * samples)
        top, rest = split(part[0:samples, :])
        high[here, 0:feat] = top
        low[here, 0:feat] = rest
        if extra:
            high[here, feat : feat + extra] = top[:, 0:extra]
            low[here, feat : feat + extra] = rest[:, 0:extra]


def left_rows(parts, samples, turned, column, row, block):
    for number, part in enumerate(parts):
        here = slice(number * samples, (number + 1) * samples)
        turned[:, here] = part[0:samples, pl.ds(column, TILE)].T
    return turned[pl.ds(row, block), :]


def keep_place(expert, samples, feat):
    per_row = feat // samples
    return lax.div(expert, per_row), pl.multiple_of(lax.rem(expert, per_row) * samples, TILE)


def keep_row(parts, samples, expert):
    row, column = keep_place(expert, samples, parts[0].shape[1])
    return jnp.concatenate([part[pl.ds(samples + row, 1), pl.ds(column, samples)] for part in parts], axis=1)


def weighted(rows, keeps):
    halves = [split(rows * keep) for keep in keeps]
    tops = [half[0] for half in halves]
    return jnp.concatenate(tops + [half[1] for half in halves], axis=0), jnp.concatenate(tops, axis=0)


def three(both, tops, high, low):
    half = tops.shape[0]
    first = dot(both, high)
    return first[0:half] + first[half : 2 * half] + dot(tops, low)


def orders(chips):
    bits = list(range(chips.bit_length() - 1))
    return bits, bits[1:] + bits[:1]


def held_and_sent(chips, order):
    if not order:
        return [0], []
    held = [k for k in range(chips) if not (k >> order[0]) & 1]
    return held, [k | (1 << order[0]) for k in held]


def slots(chips):
    places = {}
    for half, order in enumerate(orders(chips)):
        for which, group in enumerate(held_and_sent(chips, order)):
            for position, k in enumerate(group):
                places[k, half] = (2 * half + which, position)
    return places


def store(outs, seeds, place, number, columns, value):
    output, position = place
    for out in outs[0::4]:
        if number < out.shape[1]:
            break
        output, number = output + 4, number - out.shape[1]
    if seeds:
        value = value + seeds[output][position, number, :, columns]
    outs[output][position, number, :, columns] = value


def prepare_kernel(routes, counts, acts, out):
    samples, feat = acts.shape
    experts = counts.shape[1]
    out[0:samples, :] = acts[...]
    out[samples:, :] = jnp.zeros((out.shape[0] - samples, feat), F32)
    hits = []
    for expert in range(experts):
        same = [jnp.where(routes[k : k + 1, :] == expert, 1.0, 0.0) for k in range(routes.shape[0])]
        hits.append(sum(same[1:], same[0]))
    hit = jnp.concatenate(hits, axis=0)
    first = lax.broadcasted_iota(jnp.int32, (samples, samples), 0)
    second = lax.broadcasted_iota(jnp.int32, (samples, samples), 1)
    rank = dot(hit.astype(BF16), jnp.where(first < second, 1.0, 0.0).astype(BF16))
    per_row = feat // samples
    for expert in range(experts):
        limit = counts[0, expert].astype(F32)
        keep = jnp.where(rank[expert : expert + 1, :] < limit, hits[expert], 0.0)
        row, column = samples + expert // per_row, expert % per_row * samples
        out[row : row + 1, column : column + samples] = keep


def act_kernel(turns, block, chips, seeded, samples, place, *refs):
    parts, refs = refs[:2], refs[2:]
    refs, (high, low, turned) = refs[:-3], refs[-3:]
    seeds, outs = (refs[: len(refs) // 2], refs[len(refs) // 2 :]) if seeded else ((), refs)
    feat = parts[0].shape[1]
    width = outs[0].shape[3]
    mine, expert = place[0], place[1]
    split_rows(parts, samples, high, low, feat)
    keeps = [keep_row(parts, samples, expert ^ (2 * turn)) for turn in turns]
    places = slots(chips)
    rows = lax.broadcasted_iota(jnp.int32, (block, width), 0)
    columns = lax.broadcasted_iota(jnp.int32, (block, width), 1)
    corner = jnp.logical_and(rows == block - 1, columns == 0)
    for k in range(chips):
        column, row = band_place(mine ^ (2 * k), block)
        both, tops = weighted(left_rows(parts, samples, turned, column, row, block), keeps)
        total = three(both, tops, high[:, pl.ds(column, width)], low[:, pl.ds(column, width)])
        for number, keep in enumerate(keeps):
            count = jnp.sum(keep, axis=1, keepdims=True)
            value = jnp.where(corner, count, total[number * block : (number + 1) * block])
            for half in range(2):
                here = value[half * (block // 2) : (half + 1) * (block // 2)]
                store(outs, seeds, places[k, half], number, slice(0, width), here)


def grad_kernel(turns, block, chips, seeded, samples, place, *refs):
    grads, acts, refs = refs[:2], refs[2:4], refs[4:]
    refs, (high, low, act_high, act_low, turned) = refs[:-5], refs[-5:]
    seeds, outs = (refs[: len(refs) // 2], refs[len(refs) // 2 :]) if seeded else ((), refs)
    feat = grads[0].shape[1]
    width = outs[0].shape[3] - feat
    mine, expert = place[0], place[1]
    split_rows(grads, samples, high, low, feat)
    split_rows(acts, samples, act_high, act_low, feat)
    keeps = [keep_row(acts, samples, expert ^ (2 * turn)) for turn in turns]
    places = slots(chips)
    for k in range(chips):
        column, row = band_place(mine ^ (2 * k), block)
        both, tops = weighted(left_rows(grads, samples, turned, column, row, block), keeps)
        total = three(both, tops, high[:, pl.ds(column, width)], low[:, pl.ds(column, width)])
        mixed = three(both, tops, act_high[...], act_low[...])
        for number in range(len(keeps)):
            for half in range(2):
                first = number * block + half * (block // 2)
                here = slice(first, first + block // 2)
                store(outs, seeds, places[k, half], number, slice(0, width), total[here])
                store(outs, seeds, places[k, half], number, slice(width, width + feat), mixed[here])


def whole_in_vmem(count):
    return [pl.BlockSpec(memory_space=pltpu.VMEM)] * count


def prepare(routes, counts, acts):
    samples, feat = acts.shape
    rows = samples + 8 * -(-counts.shape[1] * samples // (8 * feat))
    return pl.pallas_call(
        prepare_kernel,
        out_shape=jax.ShapeDtypeStruct((rows, feat), F32),
        in_specs=[
            pl.BlockSpec(memory_space=pltpu.VMEM),
            pl.BlockSpec(memory_space=pltpu.SMEM),
            pl.BlockSpec(memory_space=pltpu.VMEM),
        ],
        out_specs=pl.BlockSpec(memory_space=pltpu.VMEM),
        compiler_params=pltpu.CompilerParams(vmem_limit_bytes=16 * MIB),
    )(routes.T, counts, acts)


def bands(body, groups, place, parts, seeds, samples, chips, block, width):
    turns = tuple(range(sum(groups)))
    feat = parts[0].shape[1]
    extended = pltpu.VMEM((2 * samples, feat + feat // 2), BF16)
    plain = pltpu.VMEM((2 * samples, feat), BF16)
    scratch = [extended, extended] + ([plain, plain] if len(parts) > 2 else [])
    shapes = [
        jax.ShapeDtypeStruct((len(group), count, block // 2, width), F32)
        for count in groups
        for order in orders(chips)
        for group in held_and_sent(chips, order)
    ]
    operands = (*parts, *seeds)
    limit = 36 if len(parts) > 2 else 20
    return pl.pallas_call(
        functools.partial(body, turns, block, chips, bool(seeds), samples),
        out_shape=shapes,
        in_specs=[pl.BlockSpec(memory_space=pltpu.SMEM)] + whole_in_vmem(len(operands)),
        out_specs=whole_in_vmem(len(shapes)),
        scratch_shapes=scratch + [pltpu.VMEM((TILE, 2 * samples), F32)],
        compiler_params=pltpu.CompilerParams(vmem_limit_bytes=limit * MIB),
    )(place, *operands)


def unfold(bands, full):
    tiles = full.shape[0] // TILE
    first_column = lax.broadcasted_iota(jnp.int32, (TILE, TILE), 1) == 0
    for i in range(tiles):
        for step in range(tiles // 2 + 1):
            j = (i + step) % tiles
            here = bands[i * TILE : (i + 1) * TILE, step * TILE : (step + 1) * TILE]
            if step == 0:
                here = jnp.where(first_column, here.T, here)
            full[i * TILE : (i + 1) * TILE, j * TILE : (j + 1) * TILE] = here
            if 0 < step < tiles // 2:
                full[j * TILE : (j + 1) * TILE, i * TILE : (i + 1) * TILE] = here.T


def damping(full):
    size = full.shape[0]
    value = full[...]
    lanes = lax.broadcasted_iota(jnp.int32, (size, size), 1)
    sublanes = lax.broadcasted_iota(jnp.int32, (size, size), 0)
    trace = jnp.sum(jnp.sum(jnp.where(lanes == sublanes, value, 0.0), axis=0, keepdims=True), axis=1, keepdims=True)
    largest = jnp.max(jnp.sum(jnp.abs(value), axis=0, keepdims=True), axis=1, keepdims=True)
    damp = trace * (0.1 / size)
    return damp, 1.0 / (largest + damp)


def times(left, high, low):
    rows = left.shape[0]
    top, rest = split(left)
    first = dot(jnp.concatenate([top, rest], axis=0), high[...])
    return first[0:rows] + first[rows : 2 * rows] + dot(top, low[...])


def row_pieces(place, block, count):
    step = block // 2
    return [
        pl.ds(pl.multiple_of((place[0] ^ (number // 2)) * block + number % 2 * step, step), step)
        for number in range(count)
    ]


def factor_rows(place, block, blocks, bands, full):
    for here, value in zip(row_pieces(place, block, len(blocks)), blocks):
        bands[here, :] = value[...]
    unfold(bands, full)
    return full[pl.ds(pl.multiple_of(place[0] * block, block), block), :]


def act_factor_kernel(place, *refs):
    blocks, (factor, scales, high, low), (bands, full) = refs[:-6], refs[-6:-2], refs[-2:]
    factor[...] = factor_rows(place, factor.shape[0], blocks, bands, full)
    damp, alpha = damping(full)
    scales[0:1, :] = jnp.broadcast_to(damp, (1, TILE))
    scales[1:2, :] = jnp.broadcast_to(alpha, (1, TILE))
    high[...], low[...] = split(full[...])


def grad_factor_kernel(place, *refs):
    blocks, (factor, inverse), (bands, full, high, low) = refs[:-6], refs[-6:-4], refs[-4:]
    block, feat = factor.shape
    rows = factor_rows(place, block, blocks, bands, full)
    factor[...] = rows
    damp, alpha = damping(full)
    high[...], low[...] = split(full[...])
    lanes = lax.broadcasted_iota(jnp.int32, (block, feat), 1)
    sublanes = lax.broadcasted_iota(jnp.int32, (block, feat), 0)
    unit = jnp.where(lanes == sublanes + place[0] * block, 1.0, 0.0).astype(F32)
    rest_rows = unit - alpha * (rows + damp * unit)
    once = 2.0 * rest_rows - alpha * (times(rest_rows, high, low) + damp * rest_rows)
    inverse[...] = alpha * (unit + rest_rows + once - alpha * (times(once, high, low) + damp * once))


def update_kernel(place, *refs):
    blocks = refs[:-9]
    inverse, scales, act_high, act_low, momentum, weights, moment_out, weight_out, full = refs[-9:]
    for here, value in zip(row_pieces(place, momentum.shape[0], len(blocks)), blocks):
        full[here, :] = value[...]
    damp, alpha = scales[0:1, 0:1], scales[1:2, 0:1]
    half_way = times(inverse[...], *split(full[...]))
    value = half_way
    for _ in range(3):
        value = half_way + value - alpha * (times(value, act_high[...], act_low[...]) + damp * value)
    moment = 0.9 * momentum[...] + alpha * value
    moment_out[...] = moment
    weight_out[...] = weights[...] - 0.5 * moment


def on_core(body, place, operands, shapes, scratch, limit):
    return pl.pallas_call(
        body,
        out_shape=shapes,
        in_specs=[pl.BlockSpec(memory_space=pltpu.SMEM)] + whole_in_vmem(len(operands)),
        out_specs=whole_in_vmem(len(shapes)),
        scratch_shapes=scratch,
        compiler_params=pltpu.CompilerParams(vmem_limit_bytes=limit * MIB),
    )(place, *operands)


def act_factor_rows(place, blocks, block, feat):
    shapes = [((block, feat), F32), ((8, TILE), F32), ((feat, feat), BF16), ((feat, feat), BF16)]
    shapes = [jax.ShapeDtypeStruct(*shape) for shape in shapes]
    scratch = [pltpu.VMEM((feat, blocks[0].shape[1]), F32), pltpu.VMEM((feat, feat), F32)]
    return on_core(act_factor_kernel, place, blocks, shapes, scratch, 32)


def grad_factor_rows(place, blocks, block, feat):
    shapes = [jax.ShapeDtypeStruct((block, feat), F32)] * 2
    scratch = [pltpu.VMEM((feat, blocks[0].shape[1]), F32), pltpu.VMEM((feat, feat), F32)]
    scratch += [pltpu.VMEM((feat, feat), BF16)] * 2
    return on_core(grad_factor_kernel, place, blocks, shapes, scratch, 32)


def update_rows(place, blocks, inverse, scales, high, low, momentum, weights):
    block, feat = momentum.shape
    operands = (*blocks, inverse, scales, high, low, momentum, weights)
    shapes = [jax.ShapeDtypeStruct((block, feat), F32)] * 2
    return on_core(update_kernel, place, operands, shapes, [pltpu.VMEM((feat, feat), F32)], 32)


def swap(value, axis, step):
    size = lax.axis_size(axis)
    return lax.ppermute(value, axis, [(i, i ^ step) for i in range(size)])


class PlaneSum:
    def __init__(self, pieces, chips):
        self.steps = [list(order) for order in orders(chips)]
        self.offsets = [held_and_sent(chips, order)[0] for order in self.steps]
        self.held, self.leaving = list(pieces[0::2]), list(pieces[1::2])

    def send(self):
        self.got = [swap(value, "dp", 2 << order[0]) for value, order in zip(self.leaving, self.steps)]

    def add(self):
        self.leaving = []
        for half, order in enumerate(self.steps):
            offsets = self.offsets[half]
            sums = {k: self.held[half][i] + self.got[half][i] for i, k in enumerate(offsets)}
            order.pop(0)
            if order:
                offsets = [k for k in offsets if not (k >> order[0]) & 1]
                self.leaving.append(jnp.stack([sums[k | (1 << order[0])] for k in offsets]))
            self.offsets[half] = offsets
            self.held[half] = [sums[k] for k in offsets]

    def finish(self):
        while self.steps[0]:
            self.send()
            self.add()
        return [held[0] for held in self.held]


def across(far):
    return [swap(far[number], "expert", 2 * (number + 1)) for number in range(far.shape[0])]


class Gather:
    def __init__(self, halves, chips):
        self.chips, self.orders = chips, orders(chips)
        self.held = [{0: value} for value in halves]

    def step(self, half, bit):
        held = self.held[half]
        for k in list(held):
            held[k | (1 << bit)] = swap(held[k], "dp", 2 << bit)

    def begin(self):
        for half, order in enumerate(self.orders):
            for bit in order[:1]:
                self.step(half, bit)
        return [held[max(held)] for held in self.held]

    def relay(self):
        for half, order in enumerate(self.orders):
            for bit in order[1:]:
                self.step(half, bit)

    def finish(self, *before):
        pieces = {}
        for half in range(2):
            last = self.chips - 1
            self.held[half][last], before = together(self.held[half][last], before)
            for k in range(self.chips):
                pieces[2 * k, half] = self.held[half][k]
                pieces[2 * k + 1, half] = swap(self.held[half][k], "dp", 1)
        return [pieces[k, half] for k in range(2 * self.chips) for half in range(2)]


def together(*values):
    return lax.optimization_barrier(values)


def on_device(acts, grads_out, routes, counts, old_act_factor, old_grad_factor, momentum, weights):
    devices, experts = lax.axis_size("dp"), lax.axis_size("expert")
    chips = devices // 2
    samples, feat, block = acts.shape[0], acts.shape[1], weights.shape[1]
    width = feat // 2 + TILE
    mine = lax.axis_index("dp")
    place = jnp.stack([mine, lax.axis_index("expert")]).astype(jnp.int32)

    def own_band(old):
        start = mine * block // TILE * TILE
        wide = jnp.concatenate([old[0], old[0][:, 0 : width - TILE]], axis=1)
        return 0.5 * lax.dynamic_slice_in_dim(wide, start, width, 1)

    turns = experts // 2
    size = (samples, chips, block, width)
    mixed_size = (samples, chips, block, width + feat)

    acts = prepare(routes, counts, acts)
    acts_far = swap(acts, "expert", 1)
    near_acts = (acts, swap(acts, "dp", 1))
    act_seeds = bands(act_kernel, (turns,), place, near_acts, (), *size)
    grads_far = swap(grads_out, "expert", 1)
    grad_parts = (grads_out, swap(grads_out, "dp", 1)) + near_acts
    grad_seeds = bands(grad_kernel, (1, turns - 1), place, grad_parts, (), *mixed_size)
    old_act, old_grad = own_band(old_act_factor), own_band(old_grad_factor)
    early = (act_seeds, grad_seeds, old_act, old_grad)
    acts_far, (act_seeds, grad_seeds, old_act, old_grad) = together(acts_far, early)

    far_acts = (acts_far, swap(acts_far, "dp", 1))
    act_sum = PlaneSum(bands(act_kernel, (turns,), place, far_acts, act_seeds, *size), chips)
    act_sum.send()
    grads_far, act_sum.held = together(grads_far, act_sum.held)
    grad_parts = (grads_far, swap(grads_far, "dp", 1)) + far_acts
    act_sum.add()
    grad_seeds, act_sum.leaving = together(grad_seeds, act_sum.leaving)
    act_sum.send()
    pieces = bands(grad_kernel, (1, turns - 1), place, grad_parts, grad_seeds, *mixed_size)

    near_sum, far_sum = PlaneSum(pieces[:4], chips), PlaneSum(pieces[4:], chips)
    far_sum.send()
    act_sum.held, far_sum.held = together(act_sum.held, far_sum.held)
    act_sum.add()
    act_sums = act_sum.finish()
    act_across = [across(total[1:]) for total in act_sums]
    far_sum.add()
    far_sum.leaving, act_across = together(far_sum.leaving, act_across)
    far_sums = far_sum.finish()

    step = block // 2
    parts = [slice(half * step, (half + 1) * step) for half in range(2)]
    act_totals = [sum(there, total[0]) for total, there in zip(act_sums, act_across)]
    total = jnp.maximum(act_totals[1][-1:, 0:1], 1.0)
    act_halves = [old_act[here] + 0.5 * (value / total) for here, value in zip(parts, act_totals)]
    far_sums, act_halves = together(far_sums, act_halves)
    across_grad = across(jnp.stack([value[:, :, 0:width] for value in far_sums], axis=1))
    far_mixed = [value[:, :, width:] for value in far_sums]
    act_gather = Gather(act_halves, chips)
    act_gather.begin()
    act_gather.relay()
    early = (act_gather.held, across_grad, far_mixed)
    near_sum.leaving, (act_gather.held, across_grad, far_mixed) = together(near_sum.leaving, early)
    across_mixed = [across(value) for value in far_mixed]
    near_sum.send()
    act_out, *act_square = act_factor_rows(place, act_gather.finish(), block, feat)
    near_sum.held, across_mixed[0] = together(near_sum.held, across_mixed[0])
    near_sum.add()
    near_sum.send()
    near_sum.held, across_mixed[1], act_square = together(near_sum.held, across_mixed[1], act_square)
    near_sum.add()
    near_sums = near_sum.finish()

    grad_stats = [
        sum((there[half] for there in across_grad), value[0, :, 0:width]) / total
        for half, value in enumerate(near_sums)
    ]
    mixed = [sum(there, value[0, :, width:]) / total for value, there in zip(near_sums, across_mixed)]
    grad_halves = [old_grad[here] + 0.5 * value for here, value in zip(parts, grad_stats)]
    grad_gather = Gather(grad_halves, chips)
    arrived = grad_gather.begin()
    mixed, arrived = together(mixed, arrived)
    mixed_gather = Gather(mixed, chips)
    mixed_gather.begin()
    grad_gather.relay()
    mixed_gather.relay()
    grad_out, inverse = grad_factor_rows(place, grad_gather.finish(), block, feat)
    mixed_blocks = mixed_gather.finish(inverse)
    outs = update_rows(place, mixed_blocks, inverse, *act_square, momentum[0], weights[0])
    return tuple(out[None] for out in (act_out, grad_out, *outs))


def solution(mesh):
    rows = P(("dp", "expert"), None)
    matrix = P("expert", "dp", None)
    return jax.shard_map(
        on_device,
        mesh=mesh,
        in_specs=(rows,) * 4 + (matrix,) * 4,
        out_specs=(matrix,) * 4,
        check_vma=False,
    )
```

```python
import functools

import jax
import jax.numpy as jnp
from jax import lax
from jax.experimental import pallas as pl
from jax.experimental.pallas import tpu as pltpu
from jax.sharding import PartitionSpec as P

F32 = jnp.float32
BF16 = jnp.bfloat16
TILE = 128
MIB = 1024 * 1024


def split(value):
    high = value.astype(BF16)
    return high, (value - high.astype(F32)).astype(BF16)


def dot(left, right):
    return jnp.dot(left, right, preferred_element_type=F32)


def band_place(owner, block):
    per_tile = TILE // block
    if per_tile == 1:
        return pl.multiple_of(owner * TILE, TILE), 0
    return (
        pl.multiple_of(lax.div(owner, per_tile) * TILE, TILE),
        pl.multiple_of(lax.rem(owner, per_tile) * block, block),
    )


def split_rows(parts, samples, high, low, feat):
    extra = high.shape[1] - feat
    for number, part in enumerate(parts):
        here = slice(number * samples, (number + 1) * samples)
        top, rest = split(part[0:samples, :])
        high[here, 0:feat] = top
        low[here, 0:feat] = rest
        if extra:
            high[here, feat : feat + extra] = top[:, 0:extra]
            low[here, feat : feat + extra] = rest[:, 0:extra]


def left_rows(parts, samples, turned, column, row, block):
    for number, part in enumerate(parts):
        here = slice(number * samples, (number + 1) * samples)
        turned[:, here] = part[0:samples, pl.ds(column, TILE)].T
    return turned[pl.ds(row, block), :]


def keep_place(expert, samples, feat):
    per_row = feat // samples
    return lax.div(expert, per_row), pl.multiple_of(lax.rem(expert, per_row) * samples, TILE)


def keep_row(parts, samples, expert):
    row, column = keep_place(expert, samples, parts[0].shape[1])
    return jnp.concatenate([part[pl.ds(samples + row, 1), pl.ds(column, samples)] for part in parts], axis=1)


def weighted(rows, keeps):
    halves = [split(rows * keep) for keep in keeps]
    tops = [half[0] for half in halves]
    return jnp.concatenate(tops + [half[1] for half in halves], axis=0), jnp.concatenate(tops, axis=0)


def three(both, tops, high, low):
    half = tops.shape[0]
    first = dot(both, high)
    return first[0:half] + first[half : 2 * half] + dot(tops, low)


def orders(chips):
    bits = list(range(chips.bit_length() - 1))
    return bits, bits[1:] + bits[:1]


def held_and_sent(chips, order):
    if not order:
        return [0], []
    held = [k for k in range(chips) if not (k >> order[0]) & 1]
    return held, [k | (1 << order[0]) for k in held]


def slots(chips):
    places = {}
    for half, order in enumerate(orders(chips)):
        for which, group in enumerate(held_and_sent(chips, order)):
            for position, k in enumerate(group):
                places[k, half] = (2 * half + which, position)
    return places


def store(outs, seeds, place, number, columns, value):
    output, position = place
    for out in outs[0::4]:
        if number < out.shape[1]:
            break
        output, number = output + 4, number - out.shape[1]
    if seeds:
        value = value + seeds[output][position, number, :, columns]
    outs[output][position, number, :, columns] = value


def prepare_kernel(routes, counts, acts, out):
    samples, feat = acts.shape
    experts = counts.shape[1]
    out[0:samples, :] = acts[...]
    out[samples:, :] = jnp.zeros((out.shape[0] - samples, feat), F32)
    hits = []
    for expert in range(experts):
        same = [jnp.where(routes[k : k + 1, :] == expert, 1.0, 0.0) for k in range(routes.shape[0])]
        hits.append(sum(same[1:], same[0]))
    hit = jnp.concatenate(hits, axis=0)
    first = lax.broadcasted_iota(jnp.int32, (samples, samples), 0)
    second = lax.broadcasted_iota(jnp.int32, (samples, samples), 1)
    rank = dot(hit.astype(BF16), jnp.where(first < second, 1.0, 0.0).astype(BF16))
    per_row = feat // samples
    for expert in range(experts):
        limit = counts[0, expert].astype(F32)
        keep = jnp.where(rank[expert : expert + 1, :] < limit, hits[expert], 0.0)
        row, column = samples + expert // per_row, expert % per_row * samples
        out[row : row + 1, column : column + samples] = keep


def act_kernel(turns, block, chips, seeded, samples, place, *refs):
    parts, refs = refs[:2], refs[2:]
    refs, (high, low, turned) = refs[:-3], refs[-3:]
    seeds, outs = (refs[: len(refs) // 2], refs[len(refs) // 2 :]) if seeded else ((), refs)
    feat = parts[0].shape[1]
    width = outs[0].shape[3]
    mine, expert = place[0], place[1]
    split_rows(parts, samples, high, low, feat)
    keeps = [keep_row(parts, samples, expert ^ (2 * turn)) for turn in turns]
    places = slots(chips)
    rows = lax.broadcasted_iota(jnp.int32, (block, width), 0)
    columns = lax.broadcasted_iota(jnp.int32, (block, width), 1)
    corner = jnp.logical_and(rows == block - 1, columns == 0)
    for k in range(chips):
        column, row = band_place(mine ^ (2 * k), block)
        both, tops = weighted(left_rows(parts, samples, turned, column, row, block), keeps)
        total = three(both, tops, high[:, pl.ds(column, width)], low[:, pl.ds(column, width)])
        for number, keep in enumerate(keeps):
            count = jnp.sum(keep, axis=1, keepdims=True)
            value = jnp.where(corner, count, total[number * block : (number + 1) * block])
            for half in range(2):
                here = value[half * (block // 2) : (half + 1) * (block // 2)]
                store(outs, seeds, places[k, half], number, slice(0, width), here)


def grad_kernel(turns, block, chips, seeded, samples, place, *refs):
    grads, acts, refs = refs[:2], refs[2:4], refs[4:]
    refs, (high, low, act_high, act_low, turned) = refs[:-5], refs[-5:]
    seeds, outs = (refs[: len(refs) // 2], refs[len(refs) // 2 :]) if seeded else ((), refs)
    feat = grads[0].shape[1]
    width = outs[0].shape[3] - feat
    mine, expert = place[0], place[1]
    split_rows(grads, samples, high, low, feat)
    split_rows(acts, samples, act_high, act_low, feat)
    keeps = [keep_row(acts, samples, expert ^ (2 * turn)) for turn in turns]
    places = slots(chips)
    for k in range(chips):
        column, row = band_place(mine ^ (2 * k), block)
        both, tops = weighted(left_rows(grads, samples, turned, column, row, block), keeps)
        total = three(both, tops, high[:, pl.ds(column, width)], low[:, pl.ds(column, width)])
        mixed = three(both, tops, act_high[...], act_low[...])
        for number in range(len(keeps)):
            for half in range(2):
                first = number * block + half * (block // 2)
                here = slice(first, first + block // 2)
                store(outs, seeds, places[k, half], number, slice(0, width), total[here])
                store(outs, seeds, places[k, half], number, slice(width, width + feat), mixed[here])


def whole_in_vmem(count):
    return [pl.BlockSpec(memory_space=pltpu.VMEM)] * count


def prepare(routes, counts, acts):
    samples, feat = acts.shape
    rows = samples + 8 * -(-counts.shape[1] * samples // (8 * feat))
    return pl.pallas_call(
        prepare_kernel,
        out_shape=jax.ShapeDtypeStruct((rows, feat), F32),
        in_specs=[
            pl.BlockSpec(memory_space=pltpu.VMEM),
            pl.BlockSpec(memory_space=pltpu.SMEM),
            pl.BlockSpec(memory_space=pltpu.VMEM),
        ],
        out_specs=pl.BlockSpec(memory_space=pltpu.VMEM),
        compiler_params=pltpu.CompilerParams(vmem_limit_bytes=16 * MIB),
    )(routes.T, counts, acts)


def bands(body, groups, place, parts, seeds, samples, chips, block, width):
    turns = tuple(range(sum(groups)))
    feat = parts[0].shape[1]
    extended = pltpu.VMEM((2 * samples, feat + feat // 2), BF16)
    plain = pltpu.VMEM((2 * samples, feat), BF16)
    scratch = [extended, extended] + ([plain, plain] if len(parts) > 2 else [])
    shapes = [
        jax.ShapeDtypeStruct((len(group), count, block // 2, width), F32)
        for count in groups
        for order in orders(chips)
        for group in held_and_sent(chips, order)
    ]
    operands = (*parts, *seeds)
    limit = 36 if len(parts) > 2 else 20
    return pl.pallas_call(
        functools.partial(body, turns, block, chips, bool(seeds), samples),
        out_shape=shapes,
        in_specs=[pl.BlockSpec(memory_space=pltpu.SMEM)] + whole_in_vmem(len(operands)),
        out_specs=whole_in_vmem(len(shapes)),
        scratch_shapes=scratch + [pltpu.VMEM((TILE, 2 * samples), F32)],
        compiler_params=pltpu.CompilerParams(vmem_limit_bytes=limit * MIB),
    )(place, *operands)


def unfold(bands, full):
    tiles = full.shape[0] // TILE
    first_column = lax.broadcasted_iota(jnp.int32, (TILE, TILE), 1) == 0
    for i in range(tiles):
        for step in range(tiles // 2 + 1):
            j = (i + step) % tiles
            here = bands[i * TILE : (i + 1) * TILE, step * TILE : (step + 1) * TILE]
            if step == 0:
                here = jnp.where(first_column, here.T, here)
            full[i * TILE : (i + 1) * TILE, j * TILE : (j + 1) * TILE] = here
            if 0 < step < tiles // 2:
                full[j * TILE : (j + 1) * TILE, i * TILE : (i + 1) * TILE] = here.T


def damping(full):
    size = full.shape[0]
    value = full[...]
    lanes = lax.broadcasted_iota(jnp.int32, (size, size), 1)
    sublanes = lax.broadcasted_iota(jnp.int32, (size, size), 0)
    trace = jnp.sum(jnp.sum(jnp.where(lanes == sublanes, value, 0.0), axis=0, keepdims=True), axis=1, keepdims=True)
    largest = jnp.max(jnp.sum(jnp.abs(value), axis=0, keepdims=True), axis=1, keepdims=True)
    damp = trace * (0.1 / size)
    return damp, 1.0 / (largest + damp)


def times(left, high, low):
    rows = left.shape[0]
    top, rest = split(left)
    first = dot(jnp.concatenate([top, rest], axis=0), high[...])
    return first[0:rows] + first[rows : 2 * rows] + dot(top, low[...])


def gather_order(order):
    offsets = [0]
    for bit in order:
        offsets += [k | (1 << bit) for k in offsets]
    return offsets


def row_pieces(place, block, blocks):
    step = block // 2
    chips = len(blocks) // 2
    pieces = []
    for number, value in enumerate(blocks):
        core, position = number // chips, number % chips
        for half, order in enumerate(orders(chips)):
            owner = place[0] ^ (2 * gather_order(order)[position] + core)
            here = pl.ds(pl.multiple_of(owner * block + half * step, step), step)
            pieces.append((here, value[half * step : (half + 1) * step, :]))
    return pieces


def factor_rows(place, block, blocks, bands, full):
    for here, value in row_pieces(place, block, blocks):
        bands[here, :] = value
    unfold(bands, full)
    return full[pl.ds(pl.multiple_of(place[0] * block, block), block), :]


def act_factor_kernel(place, *refs):
    blocks, (factor, scales, high, low), (bands, full) = refs[:-6], refs[-6:-2], refs[-2:]
    factor[...] = factor_rows(place, factor.shape[0], blocks, bands, full)
    damp, alpha = damping(full)
    scales[0:1, :] = jnp.broadcast_to(damp, (1, TILE))
    scales[1:2, :] = jnp.broadcast_to(alpha, (1, TILE))
    high[...], low[...] = split(full[...])


def grad_factor_kernel(place, *refs):
    blocks, (factor, inverse), (bands, full, high, low) = refs[:-6], refs[-6:-4], refs[-4:]
    block, feat = factor.shape
    rows = factor_rows(place, block, blocks, bands, full)
    factor[...] = rows
    damp, alpha = damping(full)
    high[...], low[...] = split(full[...])
    lanes = lax.broadcasted_iota(jnp.int32, (block, feat), 1)
    sublanes = lax.broadcasted_iota(jnp.int32, (block, feat), 0)
    unit = jnp.where(lanes == sublanes + place[0] * block, 1.0, 0.0).astype(F32)
    rest_rows = unit - alpha * (rows + damp * unit)
    once = 2.0 * rest_rows - alpha * (times(rest_rows, high, low) + damp * rest_rows)
    inverse[...] = alpha * (unit + rest_rows + once - alpha * (times(once, high, low) + damp * once))


def update_kernel(place, *refs):
    blocks = refs[:-9]
    inverse, scales, act_high, act_low, momentum, weights, moment_out, weight_out, full = refs[-9:]
    for here, value in row_pieces(place, momentum.shape[0], blocks):
        full[here, :] = value
    damp, alpha = scales[0:1, 0:1], scales[1:2, 0:1]
    half_way = times(inverse[...], *split(full[...]))
    value = half_way
    for _ in range(3):
        value = half_way + value - alpha * (times(value, act_high[...], act_low[...]) + damp * value)
    moment = 0.9 * momentum[...] + alpha * value
    moment_out[...] = moment
    weight_out[...] = weights[...] - 0.5 * moment


def on_core(body, place, operands, shapes, scratch, limit):
    return pl.pallas_call(
        body,
        out_shape=shapes,
        in_specs=[pl.BlockSpec(memory_space=pltpu.SMEM)] + whole_in_vmem(len(operands)),
        out_specs=whole_in_vmem(len(shapes)),
        scratch_shapes=scratch,
        compiler_params=pltpu.CompilerParams(vmem_limit_bytes=limit * MIB),
    )(place, *operands)


def act_factor_rows(place, blocks, block, feat):
    shapes = [((block, feat), F32), ((8, TILE), F32), ((feat, feat), BF16), ((feat, feat), BF16)]
    shapes = [jax.ShapeDtypeStruct(*shape) for shape in shapes]
    scratch = [pltpu.VMEM((feat, blocks[0].shape[1]), F32), pltpu.VMEM((feat, feat), F32)]
    return on_core(act_factor_kernel, place, blocks, shapes, scratch, 32)


def grad_factor_rows(place, blocks, block, feat):
    shapes = [jax.ShapeDtypeStruct((block, feat), F32)] * 2
    scratch = [pltpu.VMEM((feat, blocks[0].shape[1]), F32), pltpu.VMEM((feat, feat), F32)]
    scratch += [pltpu.VMEM((feat, feat), BF16)] * 2
    return on_core(grad_factor_kernel, place, blocks, shapes, scratch, 32)


def update_rows(place, blocks, inverse, scales, high, low, momentum, weights):
    block, feat = momentum.shape
    operands = (*blocks, inverse, scales, high, low, momentum, weights)
    shapes = [jax.ShapeDtypeStruct((block, feat), F32)] * 2
    return on_core(update_kernel, place, operands, shapes, [pltpu.VMEM((feat, feat), F32)], 32)


def swap(value, axis, step):
    size = lax.axis_size(axis)
    return lax.ppermute(value, axis, [(i, i ^ step) for i in range(size)])


class PlaneSum:
    def __init__(self, pieces, chips):
        self.steps = [list(order) for order in orders(chips)]
        self.offsets = [held_and_sent(chips, order)[0] for order in self.steps]
        self.held, self.leaving = list(pieces[0::2]), list(pieces[1::2])

    def send(self):
        self.got = [swap(value, "dp", 2 << order[0]) for value, order in zip(self.leaving, self.steps)]

    def add(self):
        self.leaving = []
        for half, order in enumerate(self.steps):
            offsets = self.offsets[half]
            sums = {k: self.held[half][i] + self.got[half][i] for i, k in enumerate(offsets)}
            order.pop(0)
            if order:
                offsets = [k for k in offsets if not (k >> order[0]) & 1]
                self.leaving.append(jnp.stack([sums[k | (1 << order[0])] for k in offsets]))
            self.offsets[half] = offsets
            self.held[half] = [sums[k] for k in offsets]

    def finish(self):
        while self.steps[0]:
            self.send()
            self.add()
        return [held[0] for held in self.held]


def across(far):
    return [swap(far[number], "expert", 2 * (number + 1)) for number in range(far.shape[0])]


class Gather:
    def __init__(self, halves, chips):
        self.chips, self.orders = chips, orders(chips)
        self.held = [[value] for value in halves]

    def begin(self):
        for held, order in zip(self.held, self.orders):
            held += [swap(held[0], "dp", 2 << bit) for bit in order[:1]]

    def relay(self):
        for held, order in zip(self.held, self.orders):
            for bit in order[1:]:
                held += [swap(value, "dp", 2 << bit) for value in held]

    def finish(self, *before):
        mine = [jnp.concatenate(pair, axis=0) for pair in zip(*self.held)]
        mine[-1], before = together(mine[-1], before)
        return mine + [swap(value, "dp", 1) for value in mine]


def together(*values):
    return lax.optimization_barrier(values)


def on_device(acts, grads_out, routes, counts, old_act_factor, old_grad_factor, momentum, weights):
    devices, experts = lax.axis_size("dp"), lax.axis_size("expert")
    chips = devices // 2
    samples, feat, block = acts.shape[0], acts.shape[1], weights.shape[1]
    width = feat // 2 + TILE
    mine = lax.axis_index("dp")
    place = jnp.stack([mine, lax.axis_index("expert")]).astype(jnp.int32)

    def own_band(old):
        start = mine * block // TILE * TILE
        wide = jnp.concatenate([old[0], old[0][:, 0 : width - TILE]], axis=1)
        return 0.5 * lax.dynamic_slice_in_dim(wide, start, width, 1)

    turns = experts // 2
    size = (samples, chips, block, width)
    mixed_size = (samples, chips, block, width + feat)

    acts = prepare(routes, counts, acts)
    acts_far = swap(acts, "expert", 1)
    near_acts = (acts, swap(acts, "dp", 1))
    act_seeds = bands(act_kernel, (turns,), place, near_acts, (), *size)
    grads_far = swap(grads_out, "expert", 1)
    grad_parts = (grads_out, swap(grads_out, "dp", 1)) + near_acts
    grad_seeds = bands(grad_kernel, (1, turns - 1), place, grad_parts, (), *mixed_size)
    old_act, old_grad = own_band(old_act_factor), own_band(old_grad_factor)
    early = (act_seeds, grad_seeds, old_act, old_grad)
    acts_far, (act_seeds, grad_seeds, old_act, old_grad) = together(acts_far, early)

    far_acts = (acts_far, swap(acts_far, "dp", 1))
    act_sum = PlaneSum(bands(act_kernel, (turns,), place, far_acts, act_seeds, *size), chips)
    act_sum.send()
    grads_far, act_sum.held = together(grads_far, act_sum.held)
    grad_parts = (grads_far, swap(grads_far, "dp", 1)) + far_acts
    act_sum.add()
    grad_seeds, act_sum.leaving = together(grad_seeds, act_sum.leaving)
    act_sum.send()
    pieces = bands(grad_kernel, (1, turns - 1), place, grad_parts, grad_seeds, *mixed_size)

    near_sum, far_sum = PlaneSum(pieces[:4], chips), PlaneSum(pieces[4:], chips)
    far_sum.send()
    act_sum.held, far_sum.held = together(act_sum.held, far_sum.held)
    act_sum.add()
    act_sums = act_sum.finish()
    act_across = [across(total[1:]) for total in act_sums]
    far_sum.add()
    far_sum.leaving, act_across = together(far_sum.leaving, act_across)
    far_sum.send()

    step = block // 2
    parts = [slice(half * step, (half + 1) * step) for half in range(2)]
    act_totals = [sum(there, total[0]) for total, there in zip(act_sums, act_across)]
    total = jnp.maximum(act_totals[1][-1:, 0:1], 1.0)
    act_halves = [old_act[here] + 0.5 * (value / total) for here, value in zip(parts, act_totals)]
    act_gather = Gather(act_halves, chips)
    act_gather.begin()
    far_sum.add()
    far_sums = far_sum.finish()
    far_sums, near_sum.leaving = together(far_sums, near_sum.leaving)
    across_grad = across(jnp.stack([value[:, :, 0:width] for value in far_sums], axis=1))
    across_mixed = [across(value[:, :, width:]) for value in far_sums]
    near_sum.send()
    early = (across_grad, across_mixed[0])
    near_sum.held, (across_grad, across_mixed[0]) = together(near_sum.held, early)
    near_sum.add()
    near_sum.send()
    near_sum.add()
    near_sums, act_gather.held = together(near_sum.finish(), act_gather.held)
    act_gather.relay()

    def of_near(half, far, columns):
        return sum(far, near_sums[half][0, :, columns]) / total

    grad_halves = [
        old_grad[here] + 0.5 * of_near(half, [there[half] for there in across_grad], slice(0, width))
        for half, here in enumerate(parts)
    ]
    grad_gather = Gather(grad_halves, chips)
    grad_gather.begin()
    mixed_gather = Gather([of_near(half, across_mixed[half], slice(width, None)) for half in range(2)], chips)
    mixed_gather.begin()
    grad_gather.relay()
    mixed_gather.relay()
    act_out, *act_square = act_factor_rows(place, act_gather.finish(), block, feat)
    grad_blocks, act_square = together(grad_gather.finish(), act_square)
    grad_out, inverse = grad_factor_rows(place, grad_blocks, block, feat)
    mixed_blocks = mixed_gather.finish(inverse)
    outs = update_rows(place, mixed_blocks, inverse, *act_square, momentum[0], weights[0])
    return tuple(out[None] for out in (act_out, grad_out, *outs))


def solution(mesh):
    rows = P(("dp", "expert"), None)
    matrix = P("expert", "dp", None)
    return jax.shard_map(
        on_device,
        mesh=mesh,
        in_specs=(rows,) * 4 + (matrix,) * 4,
        out_specs=(matrix,) * 4,
        check_vma=False,
    )
```

```python
import functools

import jax
import jax.numpy as jnp
from jax import lax
from jax.experimental import pallas as pl
from jax.experimental.pallas import tpu as pltpu
from jax.sharding import PartitionSpec as P

F32 = jnp.float32
BF16 = jnp.bfloat16
TILE = 128
MIB = 1024 * 1024


def split(value):
    high = value.astype(BF16)
    return high, (value - high.astype(F32)).astype(BF16)


def dot(left, right):
    return jnp.dot(left, right, preferred_element_type=F32)


def band_place(owner, block):
    per_tile = TILE // block
    if per_tile == 1:
        return pl.multiple_of(owner * TILE, TILE), 0
    return (
        pl.multiple_of(lax.div(owner, per_tile) * TILE, TILE),
        pl.multiple_of(lax.rem(owner, per_tile) * block, block),
    )


def split_rows(parts, samples, high, low, feat):
    extra = high.shape[1] - feat
    for number, part in enumerate(parts):
        here = slice(number * samples, (number + 1) * samples)
        top, rest = split(part[0:samples, :])
        high[here, 0:feat] = top
        low[here, 0:feat] = rest
        if extra:
            high[here, feat : feat + extra] = top[:, 0:extra]
            low[here, feat : feat + extra] = rest[:, 0:extra]


def left_rows(parts, samples, turned, column, row, block):
    for number, part in enumerate(parts):
        here = slice(number * samples, (number + 1) * samples)
        turned[:, here] = part[0:samples, pl.ds(column, TILE)].T
    return turned[pl.ds(row, block), :]


def keep_place(expert, samples, feat):
    per_row = feat // samples
    return lax.div(expert, per_row), pl.multiple_of(lax.rem(expert, per_row) * samples, TILE)


def keep_row(parts, samples, expert):
    row, column = keep_place(expert, samples, parts[0].shape[1])
    return jnp.concatenate([part[pl.ds(samples + row, 1), pl.ds(column, samples)] for part in parts], axis=1)


def weighted(rows, keeps):
    halves = [split(rows * keep) for keep in keeps]
    tops = [half[0] for half in halves]
    return jnp.concatenate(tops + [half[1] for half in halves], axis=0), jnp.concatenate(tops, axis=0)


def three(both, tops, high, low):
    half = tops.shape[0]
    first = dot(both, high)
    return first[0:half] + first[half : 2 * half] + dot(tops, low)


def orders(chips):
    bits = list(range(chips.bit_length() - 1))
    return bits, bits[1:] + bits[:1]


def held_and_sent(chips, order):
    if not order:
        return [0], []
    held = [k for k in range(chips) if not (k >> order[0]) & 1]
    return held, [k | (1 << order[0]) for k in held]


def slots(chips):
    places = {}
    for half, order in enumerate(orders(chips)):
        for which, group in enumerate(held_and_sent(chips, order)):
            for position, k in enumerate(group):
                places[k, half] = (2 * half + which, position)
    return places


def store(outs, seeds, place, number, columns, value):
    output, position = place
    for out in outs[0::4]:
        if number < out.shape[1]:
            break
        output, number = output + 4, number - out.shape[1]
    if seeds:
        value = value + seeds[output][position, number, :, columns]
    outs[output][position, number, :, columns] = value


def prepare_kernel(routes, counts, acts, out):
    samples, feat = acts.shape
    experts = counts.shape[1]
    out[0:samples, :] = acts[...]
    out[samples:, :] = jnp.zeros((out.shape[0] - samples, feat), F32)
    hits = []
    for expert in range(experts):
        same = [jnp.where(routes[k : k + 1, :] == expert, 1.0, 0.0) for k in range(routes.shape[0])]
        hits.append(sum(same[1:], same[0]))
    hit = jnp.concatenate(hits, axis=0)
    first = lax.broadcasted_iota(jnp.int32, (samples, samples), 0)
    second = lax.broadcasted_iota(jnp.int32, (samples, samples), 1)
    rank = dot(hit.astype(BF16), jnp.where(first < second, 1.0, 0.0).astype(BF16))
    per_row = feat // samples
    for expert in range(experts):
        limit = counts[0, expert].astype(F32)
        keep = jnp.where(rank[expert : expert + 1, :] < limit, hits[expert], 0.0)
        row, column = samples + expert // per_row, expert % per_row * samples
        out[row : row + 1, column : column + samples] = keep


def act_kernel(turns, block, chips, seeded, samples, place, *refs):
    parts, refs = refs[:2], refs[2:]
    refs, (high, low, turned) = refs[:-3], refs[-3:]
    seeds, outs = (refs[: len(refs) // 2], refs[len(refs) // 2 :]) if seeded else ((), refs)
    feat = parts[0].shape[1]
    width = outs[0].shape[3]
    mine, expert = place[0], place[1]
    split_rows(parts, samples, high, low, feat)
    keeps = [keep_row(parts, samples, expert ^ (2 * turn)) for turn in turns]
    places = slots(chips)
    rows = lax.broadcasted_iota(jnp.int32, (block, width), 0)
    columns = lax.broadcasted_iota(jnp.int32, (block, width), 1)
    corner = jnp.logical_and(rows == block - 1, columns == 0)
    for k in range(chips):
        column, row = band_place(mine ^ (2 * k), block)
        both, tops = weighted(left_rows(parts, samples, turned, column, row, block), keeps)
        total = three(both, tops, high[:, pl.ds(column, width)], low[:, pl.ds(column, width)])
        for number, keep in enumerate(keeps):
            count = jnp.sum(keep, axis=1, keepdims=True)
            value = jnp.where(corner, count, total[number * block : (number + 1) * block])
            for half in range(2):
                here = value[half * (block // 2) : (half + 1) * (block // 2)]
                store(outs, seeds, places[k, half], number, slice(0, width), here)


def grad_kernel(turns, block, chips, seeded, samples, place, *refs):
    grads, acts, refs = refs[:2], refs[2:4], refs[4:]
    refs, (high, low, act_high, act_low, turned) = refs[:-5], refs[-5:]
    seeds, outs = (refs[: len(refs) // 2], refs[len(refs) // 2 :]) if seeded else ((), refs)
    feat = grads[0].shape[1]
    width = outs[0].shape[3] - feat
    mine, expert = place[0], place[1]
    split_rows(grads, samples, high, low, feat)
    split_rows(acts, samples, act_high, act_low, feat)
    keeps = [keep_row(acts, samples, expert ^ (2 * turn)) for turn in turns]
    places = slots(chips)
    for k in range(chips):
        column, row = band_place(mine ^ (2 * k), block)
        both, tops = weighted(left_rows(grads, samples, turned, column, row, block), keeps)
        total = three(both, tops, high[:, pl.ds(column, width)], low[:, pl.ds(column, width)])
        mixed = three(both, tops, act_high[...], act_low[...])
        for number in range(len(keeps)):
            for half in range(2):
                first = number * block + half * (block // 2)
                here = slice(first, first + block // 2)
                store(outs, seeds, places[k, half], number, slice(0, width), total[here])
                store(outs, seeds, places[k, half], number, slice(width, width + feat), mixed[here])


def whole_in_vmem(count):
    return [pl.BlockSpec(memory_space=pltpu.VMEM)] * count


def prepare(routes, counts, acts):
    samples, feat = acts.shape
    rows = samples + 8 * -(-counts.shape[1] * samples // (8 * feat))
    return pl.pallas_call(
        prepare_kernel,
        out_shape=jax.ShapeDtypeStruct((rows, feat), F32),
        in_specs=[
            pl.BlockSpec(memory_space=pltpu.VMEM),
            pl.BlockSpec(memory_space=pltpu.SMEM),
            pl.BlockSpec(memory_space=pltpu.VMEM),
        ],
        out_specs=pl.BlockSpec(memory_space=pltpu.VMEM),
        compiler_params=pltpu.CompilerParams(vmem_limit_bytes=16 * MIB),
    )(routes.T, counts, acts)


def bands(body, groups, place, parts, seeds, samples, chips, block, width):
    turns = tuple(range(sum(groups)))
    feat = parts[0].shape[1]
    extended = pltpu.VMEM((2 * samples, feat + feat // 2), BF16)
    plain = pltpu.VMEM((2 * samples, feat), BF16)
    scratch = [extended, extended] + ([plain, plain] if len(parts) > 2 else [])
    shapes = [
        jax.ShapeDtypeStruct((len(group), count, block // 2, width), F32)
        for count in groups
        for order in orders(chips)
        for group in held_and_sent(chips, order)
    ]
    operands = (*parts, *seeds)
    limit = 36 if len(parts) > 2 else 20
    return pl.pallas_call(
        functools.partial(body, turns, block, chips, bool(seeds), samples),
        out_shape=shapes,
        in_specs=[pl.BlockSpec(memory_space=pltpu.SMEM)] + whole_in_vmem(len(operands)),
        out_specs=whole_in_vmem(len(shapes)),
        scratch_shapes=scratch + [pltpu.VMEM((TILE, 2 * samples), F32)],
        compiler_params=pltpu.CompilerParams(vmem_limit_bytes=limit * MIB),
    )(place, *operands)


def unfold(bands, full):
    tiles = full.shape[0] // TILE
    first_column = lax.broadcasted_iota(jnp.int32, (TILE, TILE), 1) == 0
    for i in range(tiles):
        for step in range(tiles // 2 + 1):
            j = (i + step) % tiles
            here = bands[i * TILE : (i + 1) * TILE, step * TILE : (step + 1) * TILE]
            if step == 0:
                here = jnp.where(first_column, here.T, here)
            full[i * TILE : (i + 1) * TILE, j * TILE : (j + 1) * TILE] = here
            if 0 < step < tiles // 2:
                full[j * TILE : (j + 1) * TILE, i * TILE : (i + 1) * TILE] = here.T


def damping(full):
    size = full.shape[0]
    value = full[...]
    lanes = lax.broadcasted_iota(jnp.int32, (size, size), 1)
    sublanes = lax.broadcasted_iota(jnp.int32, (size, size), 0)
    trace = jnp.sum(jnp.sum(jnp.where(lanes == sublanes, value, 0.0), axis=0, keepdims=True), axis=1, keepdims=True)
    largest = jnp.max(jnp.sum(jnp.abs(value), axis=0, keepdims=True), axis=1, keepdims=True)
    damp = trace * (0.1 / size)
    return damp, 1.0 / (largest + damp)


def times(left, high, low):
    rows = left.shape[0]
    top, rest = split(left)
    first = dot(jnp.concatenate([top, rest], axis=0), high[...])
    return first[0:rows] + first[rows : 2 * rows] + dot(top, low[...])


def gather_order(order):
    offsets = [0]
    for bit in order:
        offsets += [k | (1 << bit) for k in offsets]
    return offsets


def row_pieces(place, block, blocks):
    step = block // 2
    chips = len(blocks) // 2
    pieces = []
    for number, value in enumerate(blocks):
        core, position = number // chips, number % chips
        for half, order in enumerate(orders(chips)):
            owner = place[0] ^ (2 * gather_order(order)[position] + core)
            here = pl.ds(pl.multiple_of(owner * block + half * step, step), step)
            pieces.append((here, value[half * step : (half + 1) * step, :]))
    return pieces


def factor_rows(place, block, blocks, bands, full):
    for here, value in row_pieces(place, block, blocks):
        bands[here, :] = value
    unfold(bands, full)
    return full[pl.ds(pl.multiple_of(place[0] * block, block), block), :]


def act_factor_kernel(place, *refs):
    blocks, (factor, scales, high, low), (bands, full) = refs[:-6], refs[-6:-2], refs[-2:]
    factor[...] = factor_rows(place, factor.shape[0], blocks, bands, full)
    damp, alpha = damping(full)
    scales[0:1, :] = jnp.broadcast_to(damp, (1, TILE))
    scales[1:2, :] = jnp.broadcast_to(alpha, (1, TILE))
    high[...], low[...] = split(full[...])


def grad_factor_kernel(place, *refs):
    blocks, (factor, inverse), (bands, full, high, low) = refs[:-6], refs[-6:-4], refs[-4:]
    block, feat = factor.shape
    rows = factor_rows(place, block, blocks, bands, full)
    factor[...] = rows
    damp, alpha = damping(full)
    high[...], low[...] = split(full[...])
    lanes = lax.broadcasted_iota(jnp.int32, (block, feat), 1)
    sublanes = lax.broadcasted_iota(jnp.int32, (block, feat), 0)
    unit = jnp.where(lanes == sublanes + place[0] * block, 1.0, 0.0).astype(F32)
    rest_rows = unit - alpha * (rows + damp * unit)
    once = 2.0 * rest_rows - alpha * (times(rest_rows, high, low) + damp * rest_rows)
    inverse[...] = alpha * (unit + rest_rows + once - alpha * (times(once, high, low) + damp * once))


def update_kernel(place, *refs):
    blocks = refs[:-9]
    inverse, scales, act_high, act_low, momentum, weights, moment_out, weight_out, full = refs[-9:]
    for here, value in row_pieces(place, momentum.shape[0], blocks):
        full[here, :] = value
    damp, alpha = scales[0:1, 0:1], scales[1:2, 0:1]
    half_way = times(inverse[...], *split(full[...]))
    value = half_way
    for _ in range(3):
        value = half_way + value - alpha * (times(value, act_high[...], act_low[...]) + damp * value)
    moment = 0.9 * momentum[...] + alpha * value
    moment_out[...] = moment
    weight_out[...] = weights[...] - 0.5 * moment


def on_core(body, place, operands, shapes, scratch, limit):
    return pl.pallas_call(
        body,
        out_shape=shapes,
        in_specs=[pl.BlockSpec(memory_space=pltpu.SMEM)] + whole_in_vmem(len(operands)),
        out_specs=whole_in_vmem(len(shapes)),
        scratch_shapes=scratch,
        compiler_params=pltpu.CompilerParams(vmem_limit_bytes=limit * MIB),
    )(place, *operands)


def act_factor_rows(place, blocks, block, feat):
    shapes = [((block, feat), F32), ((8, TILE), F32), ((feat, feat), BF16), ((feat, feat), BF16)]
    shapes = [jax.ShapeDtypeStruct(*shape) for shape in shapes]
    scratch = [pltpu.VMEM((feat, blocks[0].shape[1]), F32), pltpu.VMEM((feat, feat), F32)]
    return on_core(act_factor_kernel, place, blocks, shapes, scratch, 32)


def grad_factor_rows(place, blocks, block, feat):
    shapes = [jax.ShapeDtypeStruct((block, feat), F32)] * 2
    scratch = [pltpu.VMEM((feat, blocks[0].shape[1]), F32), pltpu.VMEM((feat, feat), F32)]
    scratch += [pltpu.VMEM((feat, feat), BF16)] * 2
    return on_core(grad_factor_kernel, place, blocks, shapes, scratch, 32)


def update_rows(place, blocks, inverse, scales, high, low, momentum, weights):
    block, feat = momentum.shape
    operands = (*blocks, inverse, scales, high, low, momentum, weights)
    shapes = [jax.ShapeDtypeStruct((block, feat), F32)] * 2
    return on_core(update_kernel, place, operands, shapes, [pltpu.VMEM((feat, feat), F32)], 32)


def swap(value, axis, step):
    size = lax.axis_size(axis)
    return lax.ppermute(value, axis, [(i, i ^ step) for i in range(size)])


class PlaneSum:
    def __init__(self, pieces, chips):
        self.steps = [list(order) for order in orders(chips)]
        self.offsets = [held_and_sent(chips, order)[0] for order in self.steps]
        self.held, self.leaving = list(pieces[0::2]), list(pieces[1::2])

    def send(self):
        self.got = [swap(value, "dp", 2 << order[0]) for value, order in zip(self.leaving, self.steps)]

    def add(self):
        self.leaving = []
        for half, order in enumerate(self.steps):
            offsets = self.offsets[half]
            sums = {k: self.held[half][i] + self.got[half][i] for i, k in enumerate(offsets)}
            order.pop(0)
            if order:
                offsets = [k for k in offsets if not (k >> order[0]) & 1]
                self.leaving.append(jnp.stack([sums[k | (1 << order[0])] for k in offsets]))
            self.offsets[half] = offsets
            self.held[half] = [sums[k] for k in offsets]

    def finish(self):
        while self.steps[0]:
            self.send()
            self.add()
        return [held[0] for held in self.held]


def across(far):
    return [swap(far[number], "expert", 2 * (number + 1)) for number in range(far.shape[0])]


class Gather:
    def __init__(self, halves, chips):
        self.chips, self.orders = chips, orders(chips)
        self.halves, self.whole = halves, {}

    def begin(self):
        block = jnp.concatenate(self.halves, axis=0)
        self.whole = {order[0]: swap(block, "dp", 2 << order[0]) for order in self.orders}

    def relay(self):
        step = self.halves[0].shape[0]
        self.held = []
        for half, order in enumerate(self.orders):
            held = [self.halves[half]]
            for bit in order:
                came = [swap(value, "dp", 2 << bit) for value in held[1:]]
                if bit in self.whole:
                    own = self.whole[bit][half * step : (half + 1) * step]
                else:
                    own = swap(held[0], "dp", 2 << bit)
                held += [own] + came
            self.held.append(held)

    def finish(self, *before):
        mine = [jnp.concatenate(pair, axis=0) for pair in zip(*self.held)]
        mine[-1], before = together(mine[-1], before)
        return mine + [swap(value, "dp", 1) for value in mine]


def together(*values):
    return lax.optimization_barrier(values)


def on_device(acts, grads_out, routes, counts, old_act_factor, old_grad_factor, momentum, weights):
    devices, experts = lax.axis_size("dp"), lax.axis_size("expert")
    chips = devices // 2
    samples, feat, block = acts.shape[0], acts.shape[1], weights.shape[1]
    width = feat // 2 + TILE
    mine = lax.axis_index("dp")
    place = jnp.stack([mine, lax.axis_index("expert")]).astype(jnp.int32)

    def own_band(old):
        start = mine * block // TILE * TILE
        wide = jnp.concatenate([old[0], old[0][:, 0 : width - TILE]], axis=1)
        return 0.5 * lax.dynamic_slice_in_dim(wide, start, width, 1)

    turns = experts // 2
    size = (samples, chips, block, width)
    mixed_size = (samples, chips, block, width + feat)

    acts = prepare(routes, counts, acts)
    acts_far = swap(acts, "expert", 1)
    near_acts = (acts, swap(acts, "dp", 1))
    act_seeds = bands(act_kernel, (turns,), place, near_acts, (), *size)
    grads_far = swap(grads_out, "expert", 1)
    grad_parts = (grads_out, swap(grads_out, "dp", 1)) + near_acts
    grad_seeds = bands(grad_kernel, (1, turns - 1), place, grad_parts, (), *mixed_size)
    old_act, old_grad = own_band(old_act_factor), own_band(old_grad_factor)
    early = (act_seeds, grad_seeds, old_act, old_grad)
    acts_far, (act_seeds, grad_seeds, old_act, old_grad) = together(acts_far, early)

    far_acts = (acts_far, swap(acts_far, "dp", 1))
    act_sum = PlaneSum(bands(act_kernel, (turns,), place, far_acts, act_seeds, *size), chips)
    act_sum.send()
    grads_far, act_sum.held = together(grads_far, act_sum.held)
    grad_parts = (grads_far, swap(grads_far, "dp", 1)) + far_acts
    act_sum.add()
    grad_seeds, act_sum.leaving = together(grad_seeds, act_sum.leaving)
    act_sum.send()
    pieces = bands(grad_kernel, (1, turns - 1), place, grad_parts, grad_seeds, *mixed_size)

    near_sum, far_sum = PlaneSum(pieces[:4], chips), PlaneSum(pieces[4:], chips)
    far_sum.send()
    act_sum.held, far_sum.held = together(act_sum.held, far_sum.held)
    act_sum.add()
    act_sums = act_sum.finish()
    act_across = across(jnp.stack([value[1:] for value in act_sums], axis=1))
    near_sum.leaving, act_across = together(near_sum.leaving, act_across)
    near_sum.send()
    far_sum.add()
    far_sum.leaving, act_across = together(far_sum.leaving, act_across)
    far_sum.send()
    near_sum.add()
    near_sum.send()
    far_sum.add()
    far_sums = far_sum.finish()

    step = block // 2
    parts = [slice(half * step, (half + 1) * step) for half in range(2)]
    act_totals = [
        sum((there[half] for there in act_across), value[0]) for half, value in enumerate(act_sums)
    ]
    total = jnp.maximum(act_totals[1][-1:, 0:1], 1.0)
    act_halves = [old_act[here] + 0.5 * (value / total) for here, value in zip(parts, act_totals)]
    far_sums, act_halves = together(far_sums, act_halves)
    across_grad = across(jnp.stack([value[:, :, 0:width] for value in far_sums], axis=1))
    across_mixed = across(jnp.stack([value[:, :, width:] for value in far_sums], axis=1))
    act_gather = Gather(act_halves, chips)
    act_gather.begin()
    near_sum.held, across_grad = together(near_sum.held, across_grad)
    near_sum.add()
    near_sums = near_sum.finish()

    def of_near(half, far, columns):
        return sum((there[half] for there in far), near_sums[half][0, :, columns]) / total

    grad_halves = [
        old_grad[here] + 0.5 * of_near(half, across_grad, slice(0, width))
        for half, here in enumerate(parts)
    ]
    grad_gather = Gather(grad_halves, chips)
    grad_gather.begin()
    across_mixed, grad_gather.whole = together(across_mixed, grad_gather.whole)
    act_gather.relay()
    grad_gather.relay()
    act_out, *act_square = act_factor_rows(place, act_gather.finish(), block, feat)
    mixed_gather = Gather([of_near(half, across_mixed, slice(width, None)) for half in range(2)], chips)
    mixed_gather.relay()
    grad_blocks, act_square = together(grad_gather.finish(), act_square)
    grad_out, inverse = grad_factor_rows(place, grad_blocks, block, feat)
    mixed_blocks = mixed_gather.finish(inverse)
    outs = update_rows(place, mixed_blocks, inverse, *act_square, momentum[0], weights[0])
    return tuple(out[None] for out in (act_out, grad_out, *outs))


def solution(mesh):
    rows = P(("dp", "expert"), None)
    matrix = P("expert", "dp", None)
    return jax.shard_map(
        on_device,
        mesh=mesh,
        in_specs=(rows,) * 4 + (matrix,) * 4,
        out_specs=(matrix,) * 4,
        check_vma=False,
    )
```

```python
import functools

import jax
import jax.numpy as jnp
from jax import lax
from jax.experimental import pallas as pl
from jax.experimental.pallas import tpu as pltpu
from jax.sharding import PartitionSpec as P

F32 = jnp.float32
BF16 = jnp.bfloat16
TILE = 128
MIB = 1024 * 1024


def split(value):
    high = value.astype(BF16)
    return high, (value - high.astype(F32)).astype(BF16)


def dot(left, right):
    return jnp.dot(left, right, preferred_element_type=F32)


def band_place(owner, block):
    per_tile = TILE // block
    if per_tile == 1:
        return pl.multiple_of(owner * TILE, TILE), 0
    return (
        pl.multiple_of(lax.div(owner, per_tile) * TILE, TILE),
        pl.multiple_of(lax.rem(owner, per_tile) * block, block),
    )


def split_rows(parts, samples, high, low, feat):
    extra = high.shape[1] - feat
    for number, part in enumerate(parts):
        here = slice(number * samples, (number + 1) * samples)
        top, rest = split(part[0:samples, :])
        high[here, 0:feat] = top
        low[here, 0:feat] = rest
        if extra:
            high[here, feat : feat + extra] = top[:, 0:extra]
            low[here, feat : feat + extra] = rest[:, 0:extra]


def left_rows(parts, samples, turned, column, row, block):
    for number, part in enumerate(parts):
        here = slice(number * samples, (number + 1) * samples)
        turned[:, here] = part[0:samples, pl.ds(column, TILE)].T
    return turned[pl.ds(row, block), :]


def keep_place(expert, samples, feat):
    per_row = feat // samples
    return lax.div(expert, per_row), pl.multiple_of(lax.rem(expert, per_row) * samples, TILE)


def keep_row(parts, samples, expert):
    row, column = keep_place(expert, samples, parts[0].shape[1])
    return jnp.concatenate([part[pl.ds(samples + row, 1), pl.ds(column, samples)] for part in parts], axis=1)


def weighted(rows, keeps):
    halves = [split(rows * keep) for keep in keeps]
    tops = [half[0] for half in halves]
    return jnp.concatenate(tops + [half[1] for half in halves], axis=0), jnp.concatenate(tops, axis=0)


def three(both, tops, high, low):
    half = tops.shape[0]
    first = dot(both, high)
    return first[0:half] + first[half : 2 * half] + dot(tops, low)


def orders(chips):
    bits = list(range(chips.bit_length() - 1))
    return bits, bits[1:] + bits[:1]


def held_and_sent(chips, order):
    if not order:
        return [0], []
    held = [k for k in range(chips) if not (k >> order[0]) & 1]
    return held, [k | (1 << order[0]) for k in held]


def slots(chips):
    places = {}
    for half, order in enumerate(orders(chips)):
        for which, group in enumerate(held_and_sent(chips, order)):
            for position, k in enumerate(group):
                places[k, half] = (2 * half + which, position)
    return places


def store(outs, seeds, group, place, number, columns, value):
    output, position = 4 * group + place[0], place[1]
    if seeds:
        value = value + seeds[output][position, number, :, columns]
    outs[output][position, number, :, columns] = value


def prepare_kernel(routes, counts, acts, out):
    samples, feat = acts.shape
    experts = counts.shape[1]
    out[0:samples, :] = acts[...]
    out[samples:, :] = jnp.zeros((out.shape[0] - samples, feat), F32)
    hits = []
    for expert in range(experts):
        same = [jnp.where(routes[k : k + 1, :] == expert, 1.0, 0.0) for k in range(routes.shape[0])]
        hits.append(sum(same[1:], same[0]))
    hit = jnp.concatenate(hits, axis=0)
    first = lax.broadcasted_iota(jnp.int32, (samples, samples), 0)
    second = lax.broadcasted_iota(jnp.int32, (samples, samples), 1)
    rank = dot(hit.astype(BF16), jnp.where(first < second, 1.0, 0.0).astype(BF16))
    per_row = feat // samples
    for expert in range(experts):
        limit = counts[0, expert].astype(F32)
        keep = jnp.where(rank[expert : expert + 1, :] < limit, hits[expert], 0.0)
        row, column = samples + expert // per_row, expert % per_row * samples
        out[row : row + 1, column : column + samples] = keep


def act_kernel(turns, block, chips, seeded, samples, place, *refs):
    parts, refs = refs[:2], refs[2:]
    refs, (high, low, turned) = refs[:-3], refs[-3:]
    seeds, outs = (refs[: len(refs) // 2], refs[len(refs) // 2 :]) if seeded else ((), refs)
    feat = parts[0].shape[1]
    width = outs[0].shape[3]
    mine, expert = place[0], place[1]
    split_rows(parts, samples, high, low, feat)
    keeps = [keep_row(parts, samples, expert ^ (2 * turn)) for turn in turns]
    places = slots(chips)
    rows = lax.broadcasted_iota(jnp.int32, (block, width), 0)
    columns = lax.broadcasted_iota(jnp.int32, (block, width), 1)
    corner = jnp.logical_and(rows == block - 1, columns == 0)
    for k in range(chips):
        column, row = band_place(mine ^ (2 * k), block)
        both, tops = weighted(left_rows(parts, samples, turned, column, row, block), keeps)
        total = three(both, tops, high[:, pl.ds(column, width)], low[:, pl.ds(column, width)])
        for number, keep in enumerate(keeps):
            count = jnp.sum(keep, axis=1, keepdims=True)
            value = jnp.where(corner, count, total[number * block : (number + 1) * block])
            for half in range(2):
                here = value[half * (block // 2) : (half + 1) * (block // 2)]
                store(outs, seeds, 0, places[k, half], number, slice(0, width), here)


def grad_kernel(turns, block, chips, seeded, samples, place, *refs):
    grads, acts, refs = refs[:2], refs[2:4], refs[4:]
    refs, (high, low, act_high, act_low, turned) = refs[:-5], refs[-5:]
    seeds, outs = (refs[: len(refs) // 2], refs[len(refs) // 2 :]) if seeded else ((), refs)
    feat = grads[0].shape[1]
    width = outs[0].shape[3]
    mine, expert = place[0], place[1]
    split_rows(grads, samples, high, low, feat)
    split_rows(acts, samples, act_high, act_low, feat)
    keeps = [keep_row(acts, samples, expert ^ (2 * turn)) for turn in turns]
    places = slots(chips)
    for k in range(chips):
        column, row = band_place(mine ^ (2 * k), block)
        both, tops = weighted(left_rows(grads, samples, turned, column, row, block), keeps)
        total = three(both, tops, high[:, pl.ds(column, width)], low[:, pl.ds(column, width)])
        mixed = three(both, tops, act_high[...], act_low[...])
        for number in range(len(keeps)):
            for half in range(2):
                first = number * block + half * (block // 2)
                here = slice(first, first + block // 2)
                place = places[k, half]
                if number:
                    store(outs, seeds, 2, place, number - 1, slice(0, width), total[here])
                    store(outs, seeds, 2, place, number - 1, slice(width, width + feat), mixed[here])
                else:
                    store(outs, seeds, 0, place, 0, slice(0, width), total[here])
                    store(outs, seeds, 1, place, 0, slice(0, feat), mixed[here])


def whole_in_vmem(count):
    return [pl.BlockSpec(memory_space=pltpu.VMEM)] * count


def prepare(routes, counts, acts):
    samples, feat = acts.shape
    rows = samples + 8 * -(-counts.shape[1] * samples // (8 * feat))
    return pl.pallas_call(
        prepare_kernel,
        out_shape=jax.ShapeDtypeStruct((rows, feat), F32),
        in_specs=[
            pl.BlockSpec(memory_space=pltpu.VMEM),
            pl.BlockSpec(memory_space=pltpu.SMEM),
            pl.BlockSpec(memory_space=pltpu.VMEM),
        ],
        out_specs=pl.BlockSpec(memory_space=pltpu.VMEM),
        compiler_params=pltpu.CompilerParams(vmem_limit_bytes=16 * MIB),
    )(routes.T, counts, acts)


def bands(body, turns, groups, place, parts, seeds, samples, chips, block):
    feat = parts[0].shape[1]
    extended = pltpu.VMEM((2 * samples, feat + feat // 2), BF16)
    plain = pltpu.VMEM((2 * samples, feat), BF16)
    scratch = [extended, extended] + ([plain, plain] if len(parts) > 2 else [])
    shapes = [
        jax.ShapeDtypeStruct((len(group), count, block // 2, width), F32)
        for count, width in groups
        for order in orders(chips)
        for group in held_and_sent(chips, order)
    ]
    operands = (*parts, *seeds)
    limit = 36 if len(parts) > 2 else 20
    return pl.pallas_call(
        functools.partial(body, range(turns), block, chips, bool(seeds), samples),
        out_shape=shapes,
        in_specs=[pl.BlockSpec(memory_space=pltpu.SMEM)] + whole_in_vmem(len(operands)),
        out_specs=whole_in_vmem(len(shapes)),
        scratch_shapes=scratch + [pltpu.VMEM((TILE, 2 * samples), F32)],
        compiler_params=pltpu.CompilerParams(vmem_limit_bytes=limit * MIB),
    )(place, *operands)


def unfold(bands, full):
    tiles = full.shape[0] // TILE
    first_column = lax.broadcasted_iota(jnp.int32, (TILE, TILE), 1) == 0
    for i in range(tiles):
        for step in range(tiles // 2 + 1):
            j = (i + step) % tiles
            here = bands[i * TILE : (i + 1) * TILE, step * TILE : (step + 1) * TILE]
            if step == 0:
                here = jnp.where(first_column, here.T, here)
            full[i * TILE : (i + 1) * TILE, j * TILE : (j + 1) * TILE] = here
            if 0 < step < tiles // 2:
                full[j * TILE : (j + 1) * TILE, i * TILE : (i + 1) * TILE] = here.T


def damping(full):
    size = full.shape[0]
    value = full[...]
    lanes = lax.broadcasted_iota(jnp.int32, (size, size), 1)
    sublanes = lax.broadcasted_iota(jnp.int32, (size, size), 0)
    trace = jnp.sum(jnp.sum(jnp.where(lanes == sublanes, value, 0.0), axis=0, keepdims=True), axis=1, keepdims=True)
    largest = jnp.max(jnp.sum(jnp.abs(value), axis=0, keepdims=True), axis=1, keepdims=True)
    damp = trace * (0.1 / size)
    return damp, 1.0 / (largest + damp)


def times(left, high, low):
    rows = left.shape[0]
    top, rest = split(left)
    first = dot(jnp.concatenate([top, rest], axis=0), high[...])
    return first[0:rows] + first[rows : 2 * rows] + dot(top, low[...])


def gather_order(order):
    offsets = [0]
    for bit in order:
        offsets += [k | (1 << bit) for k in offsets]
    return offsets


def row_pieces(place, block, blocks):
    step = block // 2
    chips = len(blocks) // 2
    pieces = []
    for number, value in enumerate(blocks):
        core, position = number // chips, number % chips
        for half, order in enumerate(orders(chips)):
            owner = place[0] ^ (2 * gather_order(order)[position] + core)
            here = pl.ds(pl.multiple_of(owner * block + half * step, step), step)
            pieces.append((here, value[half * step : (half + 1) * step, :]))
    return pieces


def factor_rows(place, block, blocks, bands, full):
    for here, value in row_pieces(place, block, blocks):
        bands[here, :] = value
    unfold(bands, full)
    return full[pl.ds(pl.multiple_of(place[0] * block, block), block), :]


def act_factor_kernel(place, *refs):
    blocks, (factor, scales, high, low), (bands, full) = refs[:-6], refs[-6:-2], refs[-2:]
    factor[...] = factor_rows(place, factor.shape[0], blocks, bands, full)
    damp, alpha = damping(full)
    scales[0:1, :] = jnp.broadcast_to(damp, (1, TILE))
    scales[1:2, :] = jnp.broadcast_to(alpha, (1, TILE))
    high[...], low[...] = split(full[...])


def grad_factor_kernel(place, *refs):
    blocks, (factor, inverse), (bands, full, high, low) = refs[:-6], refs[-6:-4], refs[-4:]
    block, feat = factor.shape
    rows = factor_rows(place, block, blocks, bands, full)
    factor[...] = rows
    damp, alpha = damping(full)
    high[...], low[...] = split(full[...])
    lanes = lax.broadcasted_iota(jnp.int32, (block, feat), 1)
    sublanes = lax.broadcasted_iota(jnp.int32, (block, feat), 0)
    unit = jnp.where(lanes == sublanes + place[0] * block, 1.0, 0.0).astype(F32)
    rest_rows = unit - alpha * (rows + damp * unit)
    once = 2.0 * rest_rows - alpha * (times(rest_rows, high, low) + damp * rest_rows)
    inverse[...] = alpha * (unit + rest_rows + once - alpha * (times(once, high, low) + damp * once))


def update_kernel(place, *refs):
    blocks = refs[:-9]
    inverse, scales, act_high, act_low, momentum, weights, moment_out, weight_out, full = refs[-9:]
    for here, value in row_pieces(place, momentum.shape[0], blocks):
        full[here, :] = value
    damp, alpha = scales[0:1, 0:1], scales[1:2, 0:1]
    half_way = times(inverse[...], *split(full[...]))
    value = half_way
    for _ in range(3):
        value = half_way + value - alpha * (times(value, act_high[...], act_low[...]) + damp * value)
    moment = 0.9 * momentum[...] + alpha * value
    moment_out[...] = moment
    weight_out[...] = weights[...] - 0.5 * moment


def on_core(body, place, operands, shapes, scratch, limit):
    return pl.pallas_call(
        body,
        out_shape=shapes,
        in_specs=[pl.BlockSpec(memory_space=pltpu.SMEM)] + whole_in_vmem(len(operands)),
        out_specs=whole_in_vmem(len(shapes)),
        scratch_shapes=scratch,
        compiler_params=pltpu.CompilerParams(vmem_limit_bytes=limit * MIB),
    )(place, *operands)


def act_factor_rows(place, blocks, block, feat):
    shapes = [((block, feat), F32), ((8, TILE), F32), ((feat, feat), BF16), ((feat, feat), BF16)]
    shapes = [jax.ShapeDtypeStruct(*shape) for shape in shapes]
    scratch = [pltpu.VMEM((feat, blocks[0].shape[1]), F32), pltpu.VMEM((feat, feat), F32)]
    return on_core(act_factor_kernel, place, blocks, shapes, scratch, 32)


def grad_factor_rows(place, blocks, block, feat):
    shapes = [jax.ShapeDtypeStruct((block, feat), F32)] * 2
    scratch = [pltpu.VMEM((feat, blocks[0].shape[1]), F32), pltpu.VMEM((feat, feat), F32)]
    scratch += [pltpu.VMEM((feat, feat), BF16)] * 2
    return on_core(grad_factor_kernel, place, blocks, shapes, scratch, 32)


def update_rows(place, blocks, inverse, scales, high, low, momentum, weights):
    block, feat = momentum.shape
    operands = (*blocks, inverse, scales, high, low, momentum, weights)
    shapes = [jax.ShapeDtypeStruct((block, feat), F32)] * 2
    return on_core(update_kernel, place, operands, shapes, [pltpu.VMEM((feat, feat), F32)], 32)


def swap(value, axis, step):
    size = lax.axis_size(axis)
    return lax.ppermute(value, axis, [(i, i ^ step) for i in range(size)])


class PlaneSum:
    def __init__(self, pieces, chips):
        self.steps = [list(order) for order in orders(chips)]
        self.offsets = [held_and_sent(chips, order)[0] for order in self.steps]
        self.held, self.leaving = list(pieces[0::2]), list(pieces[1::2])

    def send(self):
        self.got = [swap(value, "dp", 2 << order[0]) for value, order in zip(self.leaving, self.steps)]

    def add(self):
        self.leaving = []
        for half, order in enumerate(self.steps):
            offsets = self.offsets[half]
            sums = {k: self.held[half][i] + self.got[half][i] for i, k in enumerate(offsets)}
            order.pop(0)
            if order:
                offsets = [k for k in offsets if not (k >> order[0]) & 1]
                self.leaving.append(jnp.stack([sums[k | (1 << order[0])] for k in offsets]))
            self.offsets[half] = offsets
            self.held[half] = [sums[k] for k in offsets]

    def finish(self):
        while self.steps[0]:
            self.send()
            self.add()
        return [held[0] for held in self.held]


def across(far):
    return [swap(far[number], "expert", 2 * (number + 1)) for number in range(far.shape[0])]


class Gather:
    def __init__(self, halves, chips):
        self.chips, self.orders = chips, orders(chips)
        self.halves, self.whole = halves, {}

    def begin(self):
        block = jnp.concatenate(self.halves, axis=0)
        self.whole = {order[0]: swap(block, "dp", 2 << order[0]) for order in self.orders}

    def relay(self):
        step = self.halves[0].shape[0]
        self.held = []
        for half, order in enumerate(self.orders):
            held = [self.halves[half]]
            for bit in order:
                came = [swap(value, "dp", 2 << bit) for value in held[1:]]
                if bit in self.whole:
                    own = self.whole[bit][half * step : (half + 1) * step]
                else:
                    own = swap(held[0], "dp", 2 << bit)
                held += [own] + came
            self.held.append(held)

    def finish(self, *before):
        mine = [jnp.concatenate(pair, axis=0) for pair in zip(*self.held)]
        if before:
            mine[-1], before = together(mine[-1], before)
        else:
            mine = list(together(*mine))
        return mine + [swap(value, "dp", 1) for value in mine]


def together(*values):
    return lax.optimization_barrier(values)


def on_device(acts, grads_out, routes, counts, old_act_factor, old_grad_factor, momentum, weights):
    devices, experts = lax.axis_size("dp"), lax.axis_size("expert")
    chips = devices // 2
    samples, feat, block = acts.shape[0], acts.shape[1], weights.shape[1]
    width = feat // 2 + TILE
    mine = lax.axis_index("dp")
    place = jnp.stack([mine, lax.axis_index("expert")]).astype(jnp.int32)

    def own_band(old):
        start = mine * block // TILE * TILE
        wide = jnp.concatenate([old[0], old[0][:, 0 : width - TILE]], axis=1)
        return 0.5 * lax.dynamic_slice_in_dim(wide, start, width, 1)

    turns = experts // 2
    size = (samples, chips, block)
    act_groups = ((turns, width),)
    grad_groups = ((1, width), (1, feat), (turns - 1, width + feat))

    acts = prepare(routes, counts, acts)
    acts_far = swap(acts, "expert", 1)
    near_acts = (acts, swap(acts, "dp", 1))
    act_seeds = bands(act_kernel, turns, act_groups, place, near_acts, (), *size)
    grads_far = swap(grads_out, "expert", 1)
    grad_parts = (grads_out, swap(grads_out, "dp", 1)) + near_acts
    grad_seeds = bands(grad_kernel, turns, grad_groups, place, grad_parts, (), *size)
    old_act, old_grad = own_band(old_act_factor), own_band(old_grad_factor)
    early = (act_seeds, grad_seeds, old_act, old_grad)
    acts_far, (act_seeds, grad_seeds, old_act, old_grad) = together(acts_far, early)

    far_acts = (acts_far, swap(acts_far, "dp", 1))
    act_sum = PlaneSum(bands(act_kernel, turns, act_groups, place, far_acts, act_seeds, *size), chips)
    act_sum.send()
    grads_far, act_sum.held = together(grads_far, act_sum.held)
    grad_parts = (grads_far, swap(grads_far, "dp", 1)) + far_acts
    act_sum.add()
    grad_seeds, act_sum.leaving = together(grad_seeds, act_sum.leaving)
    act_sum.send()
    pieces = bands(grad_kernel, turns, grad_groups, place, grad_parts, grad_seeds, *size)

    grad_sum, mixed_sum, far_sum = [PlaneSum(pieces[first : first + 4], chips) for first in (0, 4, 8)]
    far_sum.send()
    act_sum.held, far_sum.held = together(act_sum.held, far_sum.held)
    act_sum.add()
    act_sums = act_sum.finish()
    act_across = across(jnp.stack([value[1:] for value in act_sums], axis=1))
    grad_sum.leaving, far_sum.got = together(grad_sum.leaving, far_sum.got)
    grad_sum.send()
    far_sum.add()
    far_sum.leaving, act_across = together(far_sum.leaving, act_across)
    far_sum.send()
    grad_sum.add()
    mixed_sum.leaving, grad_sum.leaving = together(mixed_sum.leaving, grad_sum.leaving)
    mixed_sum.send()
    grad_sum.send()
    far_sum.add()
    far_sums = far_sum.finish()

    step = block // 2
    parts = [slice(half * step, (half + 1) * step) for half in range(2)]
    act_totals = [
        sum((there[half] for there in act_across), value[0]) for half, value in enumerate(act_sums)
    ]
    total = jnp.maximum(act_totals[1][-1:, 0:1], 1.0)
    act_halves = [old_act[here] + 0.5 * (value / total) for here, value in zip(parts, act_totals)]
    across_grad = across(jnp.stack([value[:, :, 0:width] for value in far_sums], axis=1))
    far_mixed = jnp.stack([value[:, :, width:] for value in far_sums], axis=1)
    grad_sum.add()
    grad_sums = grad_sum.finish()
    mixed_sum.held, across_grad = together(mixed_sum.held, across_grad)
    mixed_sum.add()
    mixed_sum.leaving, far_mixed = together(mixed_sum.leaving, far_mixed)
    mixed_sum.send()
    across_mixed = across(far_mixed)

    def both(near, far):
        return [sum((there[half] for there in far), value[0]) / total for half, value in enumerate(near)]

    grad_halves = [old_grad[here] + 0.5 * value for here, value in zip(parts, both(grad_sums, across_grad))]
    grad_gather = Gather(grad_halves, chips)
    grad_gather.begin()
    early = (grad_gather.whole, mixed_sum.got)
    act_halves, (grad_gather.whole, mixed_sum.got) = together(act_halves, early)
    mixed_sum.add()
    mixed_sums = mixed_sum.finish()
    act_gather = Gather(act_halves, chips)
    act_gather.begin()
    across_mixed, act_gather.whole = together(across_mixed, act_gather.whole)
    act_gather.relay()
    grad_gather.relay()
    act_out, *act_square = act_factor_rows(place, act_gather.finish(), block, feat)
    mixed_gather = Gather(both(mixed_sums, across_mixed), chips)
    mixed_gather.begin()
    mixed_gather.relay()
    grad_blocks, act_square = together(grad_gather.finish(), act_square)
    grad_out, inverse = grad_factor_rows(place, grad_blocks, block, feat)
    mixed_blocks = mixed_gather.finish(inverse)
    outs = update_rows(place, mixed_blocks, inverse, *act_square, momentum[0], weights[0])
    return tuple(out[None] for out in (act_out, grad_out, *outs))


def solution(mesh):
    rows = P(("dp", "expert"), None)
    matrix = P("expert", "dp", None)
    return jax.shard_map(
        on_device,
        mesh=mesh,
        in_specs=(rows,) * 4 + (matrix,) * 4,
        out_specs=(matrix,) * 4,
        check_vma=False,
    )
```

```python
import functools

import jax
import jax.numpy as jnp
from jax import lax
from jax.experimental import pallas as pl
from jax.experimental.pallas import tpu as pltpu
from jax.sharding import PartitionSpec as P

F32 = jnp.float32
BF16 = jnp.bfloat16
TILE = 128
MIB = 1024 * 1024


def split(value):
    high = value.astype(BF16)
    return high, (value - high.astype(F32)).astype(BF16)


def dot(left, right):
    return jnp.dot(left, right, preferred_element_type=F32)


def band_place(owner, block):
    per_tile = TILE // block
    if per_tile == 1:
        return pl.multiple_of(owner * TILE, TILE), 0
    return (
        pl.multiple_of(lax.div(owner, per_tile) * TILE, TILE),
        pl.multiple_of(lax.rem(owner, per_tile) * block, block),
    )


def split_rows(parts, samples, high, low, feat):
    extra = high.shape[1] - feat
    for number, part in enumerate(parts):
        here = slice(number * samples, (number + 1) * samples)
        top, rest = split(part[0:samples, :])
        high[here, 0:feat] = top
        low[here, 0:feat] = rest
        if extra:
            high[here, feat : feat + extra] = top[:, 0:extra]
            low[here, feat : feat + extra] = rest[:, 0:extra]


def left_rows(parts, samples, turned, column, row, block):
    for number, part in enumerate(parts):
        here = slice(number * samples, (number + 1) * samples)
        turned[:, here] = part[0:samples, pl.ds(column, TILE)].T
    return turned[pl.ds(row, block), :]


def keep_place(expert, samples, feat):
    per_row = feat // samples
    return lax.div(expert, per_row), pl.multiple_of(lax.rem(expert, per_row) * samples, TILE)


def keep_row(parts, samples, expert):
    row, column = keep_place(expert, samples, parts[0].shape[1])
    return jnp.concatenate([part[pl.ds(samples + row, 1), pl.ds(column, samples)] for part in parts], axis=1)


def weighted(rows, keeps):
    halves = [split(rows * keep) for keep in keeps]
    tops = [half[0] for half in halves]
    return jnp.concatenate(tops + [half[1] for half in halves], axis=0), jnp.concatenate(tops, axis=0)


def three(both, tops, high, low):
    half = tops.shape[0]
    first = dot(both, high)
    return first[0:half] + first[half : 2 * half] + dot(tops, low)


def orders(chips):
    bits = list(range(chips.bit_length() - 1))
    return bits, bits[1:] + bits[:1]


def held_and_sent(chips, order):
    if not order:
        return [0], []
    held = [k for k in range(chips) if not (k >> order[0]) & 1]
    return held, [k | (1 << order[0]) for k in held]


def slots(chips):
    places = {}
    for half, order in enumerate(orders(chips)):
        for which, group in enumerate(held_and_sent(chips, order)):
            for position, k in enumerate(group):
                places[k, half] = (2 * half + which, position)
    return places


def store(outs, seeds, group, place, number, columns, value):
    output, position = 4 * group + place[0], place[1]
    if seeds:
        value = value + seeds[output][position, number, :, columns]
    outs[output][position, number, :, columns] = value


def prepare_kernel(routes_ref, counts_ref, acts, out, routes, counts, sems):
    samples, feat = acts.shape
    experts = counts.shape[1]
    copies = [
        pltpu.make_async_copy(routes_ref, routes, sems.at[0]),
        pltpu.make_async_copy(counts_ref, counts, sems.at[1]),
        pltpu.make_async_copy(acts, out.at[pl.ds(0, samples), :], sems.at[2]),
    ]
    for copy in copies:
        copy.start()
    out[samples:, :] = jnp.zeros((out.shape[0] - samples, feat), F32)
    for copy in copies[:2]:
        copy.wait()
    hits = []
    for expert in range(experts):
        same = [jnp.where(routes[k : k + 1, :] == expert, 1.0, 0.0) for k in range(routes.shape[0])]
        hits.append(sum(same[1:], same[0]))
    hit = jnp.concatenate(hits, axis=0)
    first = lax.broadcasted_iota(jnp.int32, (samples, samples), 0)
    second = lax.broadcasted_iota(jnp.int32, (samples, samples), 1)
    rank = dot(hit.astype(BF16), jnp.where(first < second, 1.0, 0.0).astype(BF16))
    per_row = feat // samples
    for expert in range(experts):
        limit = counts[0, expert].astype(F32)
        keep = jnp.where(rank[expert : expert + 1, :] < limit, hits[expert], 0.0)
        row, column = samples + expert // per_row, expert % per_row * samples
        out[row : row + 1, column : column + samples] = keep
    copies[2].wait()


def act_kernel(turns, block, chips, seeded, samples, place, *refs):
    parts, refs = refs[:2], refs[2:]
    refs, (high, low, turned) = refs[:-3], refs[-3:]
    seeds, outs = (refs[: len(refs) // 2], refs[len(refs) // 2 :]) if seeded else ((), refs)
    feat = parts[0].shape[1]
    width = outs[0].shape[3]
    mine, expert = place[0], place[1]
    split_rows(parts, samples, high, low, feat)
    keeps = [keep_row(parts, samples, expert ^ (2 * turn)) for turn in turns]
    places = slots(chips)
    rows = lax.broadcasted_iota(jnp.int32, (block, width), 0)
    columns = lax.broadcasted_iota(jnp.int32, (block, width), 1)
    corner = jnp.logical_and(rows == block - 1, columns == 0)
    for k in range(chips):
        column, row = band_place(mine ^ (2 * k), block)
        both, tops = weighted(left_rows(parts, samples, turned, column, row, block), keeps)
        total = three(both, tops, high[:, pl.ds(column, width)], low[:, pl.ds(column, width)])
        for number, keep in enumerate(keeps):
            count = jnp.sum(keep, axis=1, keepdims=True)
            value = jnp.where(corner, count, total[number * block : (number + 1) * block])
            for half in range(2):
                here = value[half * (block // 2) : (half + 1) * (block // 2)]
                store(outs, seeds, 0, places[k, half], number, slice(0, width), here)


def grad_kernel(turns, block, chips, seeded, samples, place, *refs):
    grads, acts, refs = refs[:2], refs[2:4], refs[4:]
    refs, (high, low, act_high, act_low, turned) = refs[:-5], refs[-5:]
    seeds, outs = (refs[: len(refs) // 2], refs[len(refs) // 2 :]) if seeded else ((), refs)
    feat = grads[0].shape[1]
    width = outs[0].shape[3]
    mine, expert = place[0], place[1]
    split_rows(grads, samples, high, low, feat)
    split_rows(acts, samples, act_high, act_low, feat)
    keeps = [keep_row(acts, samples, expert ^ (2 * turn)) for turn in turns]
    places = slots(chips)
    for k in range(chips):
        column, row = band_place(mine ^ (2 * k), block)
        both, tops = weighted(left_rows(grads, samples, turned, column, row, block), keeps)
        total = three(both, tops, high[:, pl.ds(column, width)], low[:, pl.ds(column, width)])
        mixed = three(both, tops, act_high[...], act_low[...])
        for number in range(len(keeps)):
            for half in range(2):
                first = number * block + half * (block // 2)
                here = slice(first, first + block // 2)
                place = places[k, half]
                if number:
                    store(outs, seeds, 2, place, number - 1, slice(0, width), total[here])
                    store(outs, seeds, 2, place, number - 1, slice(width, width + feat), mixed[here])
                else:
                    store(outs, seeds, 0, place, 0, slice(0, width), total[here])
                    store(outs, seeds, 1, place, 0, slice(0, feat), mixed[here])


def whole_in_vmem(count):
    return [pl.BlockSpec(memory_space=pltpu.VMEM)] * count


def prepare(routes, counts, acts):
    samples, feat = acts.shape
    rows = samples + 8 * -(-counts.shape[1] * samples // (8 * feat))
    return pl.pallas_call(
        prepare_kernel,
        out_shape=jax.ShapeDtypeStruct((rows, feat), F32),
        in_specs=[pl.BlockSpec(memory_space=pltpu.HBM)] * 3,
        out_specs=pl.BlockSpec(memory_space=pltpu.VMEM),
        scratch_shapes=[
            pltpu.VMEM(routes.shape[::-1], jnp.int32),
            pltpu.SMEM(counts.shape, jnp.int32),
            pltpu.SemaphoreType.DMA((3,)),
        ],
        compiler_params=pltpu.CompilerParams(vmem_limit_bytes=16 * MIB),
    )(routes.T, counts, acts)


def bands(body, turns, groups, place, parts, seeds, samples, chips, block):
    feat = parts[0].shape[1]
    extended = pltpu.VMEM((2 * samples, feat + feat // 2), BF16)
    plain = pltpu.VMEM((2 * samples, feat), BF16)
    scratch = [extended, extended] + ([plain, plain] if len(parts) > 2 else [])
    shapes = [
        jax.ShapeDtypeStruct((len(group), count, block // 2, width), F32)
        for count, width in groups
        for order in orders(chips)
        for group in held_and_sent(chips, order)
    ]
    operands = (*parts, *seeds)
    limit = 36 if len(parts) > 2 else 20
    return pl.pallas_call(
        functools.partial(body, range(turns), block, chips, bool(seeds), samples),
        out_shape=shapes,
        in_specs=[pl.BlockSpec(memory_space=pltpu.SMEM)] + whole_in_vmem(len(operands)),
        out_specs=whole_in_vmem(len(shapes)),
        scratch_shapes=scratch + [pltpu.VMEM((TILE, 2 * samples), F32)],
        compiler_params=pltpu.CompilerParams(vmem_limit_bytes=limit * MIB),
    )(place, *operands)


def unfold(bands, full):
    tiles = full.shape[0] // TILE
    first_column = lax.broadcasted_iota(jnp.int32, (TILE, TILE), 1) == 0
    for i in range(tiles):
        for step in range(tiles // 2 + 1):
            j = (i + step) % tiles
            here = bands[i * TILE : (i + 1) * TILE, step * TILE : (step + 1) * TILE]
            if step == 0:
                here = jnp.where(first_column, here.T, here)
            full[i * TILE : (i + 1) * TILE, j * TILE : (j + 1) * TILE] = here
            if 0 < step < tiles // 2:
                full[j * TILE : (j + 1) * TILE, i * TILE : (i + 1) * TILE] = here.T


def damping(full):
    size = full.shape[0]
    value = full[...]
    lanes = lax.broadcasted_iota(jnp.int32, (size, size), 1)
    sublanes = lax.broadcasted_iota(jnp.int32, (size, size), 0)
    trace = jnp.sum(jnp.sum(jnp.where(lanes == sublanes, value, 0.0), axis=0, keepdims=True), axis=1, keepdims=True)
    largest = jnp.max(jnp.sum(jnp.abs(value), axis=0, keepdims=True), axis=1, keepdims=True)
    damp = trace * (0.1 / size)
    return damp, 1.0 / (largest + damp)


def times(left, high, low):
    rows = left.shape[0]
    top, rest = split(left)
    first = dot(jnp.concatenate([top, rest], axis=0), high[...])
    return first[0:rows] + first[rows : 2 * rows] + dot(top, low[...])


def gather_order(order):
    offsets = [0]
    for bit in order:
        offsets += [k | (1 << bit) for k in offsets]
    return offsets


def row_pieces(place, block, chips, arrays):
    step = block // 2
    blocks = [
        value[first : first + block, :] for value in arrays for first in range(0, value.shape[0], block)
    ]
    pieces = []
    for number, value in enumerate(blocks):
        core, position = number // chips, number % chips
        for half, order in enumerate(orders(chips)):
            owner = place[0] ^ (2 * gather_order(order)[position] + core)
            here = pl.ds(pl.multiple_of(owner * block + half * step, step), step)
            pieces.append((here, value[half * step : (half + 1) * step, :]))
    return pieces


def factor_rows(place, block, blocks, bands, full):
    for here, value in row_pieces(place, block, bands.shape[0] // (2 * block), blocks):
        bands[here, :] = value
    unfold(bands, full)
    return full[pl.ds(pl.multiple_of(place[0] * block, block), block), :]


def act_factor_kernel(place, *refs):
    blocks, (factor, scales, high, low), (bands, full) = refs[:-6], refs[-6:-2], refs[-2:]
    factor[...] = factor_rows(place, factor.shape[0], blocks, bands, full)
    damp, alpha = damping(full)
    scales[0:1, :] = jnp.broadcast_to(damp, (1, TILE))
    scales[1:2, :] = jnp.broadcast_to(alpha, (1, TILE))
    high[...], low[...] = split(full[...])


def grad_factor_kernel(place, *refs):
    blocks, (factor, inverse), (bands, full, high, low) = refs[:-6], refs[-6:-4], refs[-4:]
    block, feat = factor.shape
    rows = factor_rows(place, block, blocks, bands, full)
    factor[...] = rows
    damp, alpha = damping(full)
    high[...], low[...] = split(full[...])
    lanes = lax.broadcasted_iota(jnp.int32, (block, feat), 1)
    sublanes = lax.broadcasted_iota(jnp.int32, (block, feat), 0)
    unit = jnp.where(lanes == sublanes + place[0] * block, 1.0, 0.0).astype(F32)
    rest_rows = unit - alpha * (rows + damp * unit)
    once = 2.0 * rest_rows - alpha * (times(rest_rows, high, low) + damp * rest_rows)
    inverse[...] = alpha * (unit + rest_rows + once - alpha * (times(once, high, low) + damp * once))


def update_kernel(place, *refs):
    blocks = refs[:-9]
    inverse, scales, act_high, act_low, momentum, weights, moment_out, weight_out, full = refs[-9:]
    block = momentum.shape[0]
    for here, value in row_pieces(place, block, full.shape[0] // (2 * block), blocks):
        full[here, :] = value
    damp, alpha = scales[0:1, 0:1], scales[1:2, 0:1]
    half_way = times(inverse[...], *split(full[...]))
    value = half_way
    for _ in range(3):
        value = half_way + value - alpha * (times(value, act_high[...], act_low[...]) + damp * value)
    moment = 0.9 * momentum[...] + alpha * value
    moment_out[...] = moment
    weight_out[...] = weights[...] - 0.5 * moment


def on_core(body, place, operands, shapes, scratch, limit):
    return pl.pallas_call(
        body,
        out_shape=shapes,
        in_specs=[pl.BlockSpec(memory_space=pltpu.SMEM)] + whole_in_vmem(len(operands)),
        out_specs=whole_in_vmem(len(shapes)),
        scratch_shapes=scratch,
        compiler_params=pltpu.CompilerParams(vmem_limit_bytes=limit * MIB),
    )(place, *operands)


def act_factor_rows(place, blocks, block, feat):
    shapes = [((block, feat), F32), ((8, TILE), F32), ((feat, feat), BF16), ((feat, feat), BF16)]
    shapes = [jax.ShapeDtypeStruct(*shape) for shape in shapes]
    scratch = [pltpu.VMEM((feat, blocks[0].shape[1]), F32), pltpu.VMEM((feat, feat), F32)]
    return on_core(act_factor_kernel, place, blocks, shapes, scratch, 32)


def grad_factor_rows(place, blocks, block, feat):
    shapes = [jax.ShapeDtypeStruct((block, feat), F32)] * 2
    scratch = [pltpu.VMEM((feat, blocks[0].shape[1]), F32), pltpu.VMEM((feat, feat), F32)]
    scratch += [pltpu.VMEM((feat, feat), BF16)] * 2
    return on_core(grad_factor_kernel, place, blocks, shapes, scratch, 32)


def update_rows(place, blocks, inverse, scales, high, low, momentum, weights):
    block, feat = momentum.shape
    operands = (*blocks, inverse, scales, high, low, momentum, weights)
    shapes = [jax.ShapeDtypeStruct((block, feat), F32)] * 2
    return on_core(update_kernel, place, operands, shapes, [pltpu.VMEM((feat, feat), F32)], 32)


def swap(value, axis, step):
    size = lax.axis_size(axis)
    return lax.ppermute(value, axis, [(i, i ^ step) for i in range(size)])


class PlaneSum:
    def __init__(self, pieces, chips):
        self.steps = [list(order) for order in orders(chips)]
        self.offsets = [held_and_sent(chips, order)[0] for order in self.steps]
        self.held, self.leaving = list(pieces[0::2]), list(pieces[1::2])

    def send(self):
        self.got = [swap(value, "dp", 2 << order[0]) for value, order in zip(self.leaving, self.steps)]

    def add(self):
        self.leaving = []
        for half, order in enumerate(self.steps):
            offsets = self.offsets[half]
            sums = {k: self.held[half][i] + self.got[half][i] for i, k in enumerate(offsets)}
            order.pop(0)
            if order:
                offsets = [k for k in offsets if not (k >> order[0]) & 1]
                self.leaving.append(jnp.stack([sums[k | (1 << order[0])] for k in offsets]))
            self.offsets[half] = offsets
            self.held[half] = [sums[k] for k in offsets]

    def finish(self):
        while self.steps[0]:
            self.send()
            self.add()
        return [held[0] for held in self.held]


def across(far):
    return [swap(far[number], "expert", 2 * (number + 1)) for number in range(far.shape[0])]


class Gather:
    def __init__(self, halves, chips):
        self.chips, self.orders = chips, orders(chips)
        self.halves, self.whole = halves, {}

    def begin(self):
        block = jnp.concatenate(self.halves, axis=0)
        self.whole = {order[0]: swap(block, "dp", 2 << order[0]) for order in self.orders}

    def relay(self):
        step = self.halves[0].shape[0]
        self.held = []
        for half, order in enumerate(self.orders):
            held = [self.halves[half]]
            for bit in order:
                came = [swap(value, "dp", 2 << bit) for value in held[1:]]
                if bit in self.whole:
                    own = self.whole[bit][half * step : (half + 1) * step]
                else:
                    own = swap(held[0], "dp", 2 << bit)
                held += [own] + came
            self.held.append(held)

    def exchange(self, first=0, last=None):
        pairs = list(zip(*self.held))[first:last]
        mine = jnp.concatenate([value for pair in pairs for value in pair], axis=0)
        return mine, swap(mine, "dp", 1)


def together(*values):
    return lax.optimization_barrier(values)


def on_device(acts, grads_out, routes, counts, old_act_factor, old_grad_factor, momentum, weights):
    devices, experts = lax.axis_size("dp"), lax.axis_size("expert")
    chips = devices // 2
    samples, feat, block = acts.shape[0], acts.shape[1], weights.shape[1]
    width = feat // 2 + TILE
    mine = lax.axis_index("dp")
    place = jnp.stack([mine, lax.axis_index("expert")]).astype(jnp.int32)

    def own_band(old):
        start = mine * block // TILE * TILE
        wide = jnp.concatenate([old[0], old[0][:, 0 : width - TILE]], axis=1)
        return 0.5 * lax.dynamic_slice_in_dim(wide, start, width, 1)

    turns = experts // 2
    size = (samples, chips, block)
    act_groups = ((turns, width),)
    grad_groups = ((1, width), (1, feat), (turns - 1, width + feat))

    acts = prepare(routes, counts, acts)
    acts_far = swap(acts, "expert", 1)
    near_acts = (acts, swap(acts, "dp", 1))
    act_seeds = bands(act_kernel, turns, act_groups, place, near_acts, (), *size)
    grads_far = swap(grads_out, "expert", 1)
    grad_parts = (grads_out, swap(grads_out, "dp", 1)) + near_acts
    grad_seeds = bands(grad_kernel, turns, grad_groups, place, grad_parts, (), *size)
    old_act, old_grad = own_band(old_act_factor), own_band(old_grad_factor)
    early = (act_seeds, grad_seeds, old_act, old_grad)
    acts_far, (act_seeds, grad_seeds, old_act, old_grad) = together(acts_far, early)

    far_acts = (acts_far, swap(acts_far, "dp", 1))
    act_sum = PlaneSum(bands(act_kernel, turns, act_groups, place, far_acts, act_seeds, *size), chips)
    act_sum.send()
    grads_far, act_sum.held = together(grads_far, act_sum.held)
    grad_parts = (grads_far, swap(grads_far, "dp", 1)) + far_acts
    act_sum.add()
    grad_seeds, act_sum.leaving = together(grad_seeds, act_sum.leaving)
    act_sum.send()
    pieces = bands(grad_kernel, turns, grad_groups, place, grad_parts, grad_seeds, *size)

    grad_sum, mixed_sum, far_sum = [PlaneSum(pieces[first : first + 4], chips) for first in (0, 4, 8)]
    far_sum.send()
    act_sum.held, far_sum.held = together(act_sum.held, far_sum.held)
    act_sum.add()
    act_sums = act_sum.finish()
    act_across = across(jnp.stack([value[1:] for value in act_sums], axis=1))
    grad_sum.leaving, far_sum.got = together(grad_sum.leaving, far_sum.got)
    grad_sum.send()
    far_sum.add()
    far_sum.leaving, act_across = together(far_sum.leaving, act_across)
    far_sum.send()
    grad_sum.add()
    mixed_sum.leaving, grad_sum.leaving = together(mixed_sum.leaving, grad_sum.leaving)
    mixed_sum.send()
    grad_sum.send()
    far_sum.add()
    far_sums = far_sum.finish()

    step = block // 2
    parts = [slice(half * step, (half + 1) * step) for half in range(2)]
    act_totals = [
        sum((there[half] for there in act_across), value[0]) for half, value in enumerate(act_sums)
    ]
    total = jnp.maximum(act_totals[1][-1:, 0:1], 1.0)
    act_halves = [old_act[here] + 0.5 * (value / total) for here, value in zip(parts, act_totals)]
    across_grad = across(jnp.stack([value[:, :, 0:width] for value in far_sums], axis=1))
    far_mixed = jnp.stack([value[:, :, width:] for value in far_sums], axis=1)
    grad_sum.add()
    grad_sums = grad_sum.finish()
    mixed_sum.held, across_grad = together(mixed_sum.held, across_grad)
    mixed_sum.add()
    mixed_sum.leaving, far_mixed = together(mixed_sum.leaving, far_mixed)
    mixed_sum.send()
    across_mixed = across(far_mixed)

    def both(near, far):
        return [sum((there[half] for there in far), value[0]) / total for half, value in enumerate(near)]

    grad_halves = [old_grad[here] + 0.5 * value for here, value in zip(parts, both(grad_sums, across_grad))]
    grad_gather = Gather(grad_halves, chips)
    grad_gather.begin()
    early = (grad_gather.whole, mixed_sum.got)
    act_halves, (grad_gather.whole, mixed_sum.got) = together(act_halves, early)
    mixed_sum.add()
    mixed_sums = mixed_sum.finish()
    act_gather = Gather(act_halves, chips)
    act_gather.begin()
    grad_gather.relay()
    act_gather.relay()
    across_mixed, _ = together(across_mixed, act_gather.whole)
    act_out, *act_square = act_factor_rows(place, act_gather.exchange(), block, feat)
    mixed_gather = Gather(both(mixed_sums, across_mixed), chips)
    mixed_gather.begin()
    grad_blocks, act_square = together(grad_gather.exchange(), act_square)
    grad_out, inverse = grad_factor_rows(place, grad_blocks, block, feat)
    mixed_gather.whole, inverse = together(mixed_gather.whole, inverse)
    mixed_gather.relay()
    mine, theirs = mixed_gather.exchange(0, -1)
    my_last, their_last = mixed_gather.exchange(-1)
    mixed_blocks = (mine, my_last, theirs, their_last)
    outs = update_rows(place, mixed_blocks, inverse, *act_square, momentum[0], weights[0])
    return tuple(out[None] for out in (act_out, grad_out, *outs))


def solution(mesh):
    rows = P(("dp", "expert"), None)
    matrix = P("expert", "dp", None)
    return jax.shard_map(
        on_device,
        mesh=mesh,
        in_specs=(rows,) * 4 + (matrix,) * 4,
        out_specs=(matrix,) * 4,
        check_vma=False,
    )
```

```python
import functools

import jax
import jax.numpy as jnp
from jax import lax
from jax.experimental import pallas as pl
from jax.experimental.pallas import tpu as pltpu
from jax.sharding import PartitionSpec as P

F32 = jnp.float32
BF16 = jnp.bfloat16
TILE = 128
MIB = 1024 * 1024


def split(value):
    high = value.astype(BF16)
    return high, (value - high.astype(F32)).astype(BF16)


def dot(left, right):
    return jnp.dot(left, right, preferred_element_type=F32)


def band_place(owner, block):
    per_tile = TILE // block
    if per_tile == 1:
        return pl.multiple_of(owner * TILE, TILE), 0
    return (
        pl.multiple_of(lax.div(owner, per_tile) * TILE, TILE),
        pl.multiple_of(lax.rem(owner, per_tile) * block, block),
    )


def split_rows(parts, samples, high, low, feat):
    extra = high.shape[1] - feat
    for number, part in enumerate(parts):
        here = slice(number * samples, (number + 1) * samples)
        top, rest = split(part[0:samples, :])
        high[here, 0:feat] = top
        low[here, 0:feat] = rest
        if extra:
            high[here, feat : feat + extra] = top[:, 0:extra]
            low[here, feat : feat + extra] = rest[:, 0:extra]


def left_rows(parts, samples, turned, column, row, block):
    for number, part in enumerate(parts):
        here = slice(number * samples, (number + 1) * samples)
        turned[:, here] = part[0:samples, pl.ds(column, TILE)].T
    return turned[pl.ds(row, block), :]


def keep_place(expert, samples, feat):
    per_row = feat // samples
    return lax.div(expert, per_row), pl.multiple_of(lax.rem(expert, per_row) * samples, TILE)


def keep_row(parts, samples, expert):
    row, column = keep_place(expert, samples, parts[0].shape[1])
    return jnp.concatenate([part[pl.ds(samples + row, 1), pl.ds(column, samples)] for part in parts], axis=1)


def weighted(rows, keeps):
    halves = [split(rows * keep) for keep in keeps]
    tops = [half[0] for half in halves]
    return jnp.concatenate(tops + [half[1] for half in halves], axis=0), jnp.concatenate(tops, axis=0)


def three(both, tops, high, low):
    half = tops.shape[0]
    first = dot(both, high)
    return first[0:half] + first[half : 2 * half] + dot(tops, low)


def orders(chips):
    bits = list(range(chips.bit_length() - 1))
    return bits, bits[1:] + bits[:1]


def held_and_sent(chips, order):
    if not order:
        return [0], []
    held = [k for k in range(chips) if not (k >> order[0]) & 1]
    return held, [k | (1 << order[0]) for k in held]


def slots(chips):
    places = {}
    for half, order in enumerate(orders(chips)):
        for which, group in enumerate(held_and_sent(chips, order)):
            for position, k in enumerate(group):
                places[k, half] = (2 * half + which, position)
    return places


def store(outs, seeds, group, place, number, columns, value):
    output, position = 4 * group + place[0], place[1]
    if seeds:
        value = value + seeds[output][position, number, :, columns]
    outs[output][position, number, :, columns] = value


def prepare_kernel(routes_ref, counts_ref, acts, out, routes, counts, sems):
    samples, feat = acts.shape
    experts = counts.shape[1]
    copies = [
        pltpu.make_async_copy(routes_ref, routes, sems.at[0]),
        pltpu.make_async_copy(counts_ref, counts, sems.at[1]),
        pltpu.make_async_copy(acts, out.at[pl.ds(0, samples), :], sems.at[2]),
    ]
    for copy in copies:
        copy.start()
    out[samples:, :] = jnp.zeros((out.shape[0] - samples, feat), F32)
    for copy in copies[:2]:
        copy.wait()
    hits = []
    for expert in range(experts):
        same = [jnp.where(routes[k : k + 1, :] == expert, 1.0, 0.0) for k in range(routes.shape[0])]
        hits.append(sum(same[1:], same[0]))
    hit = jnp.concatenate(hits, axis=0)
    first = lax.broadcasted_iota(jnp.int32, (samples, samples), 0)
    second = lax.broadcasted_iota(jnp.int32, (samples, samples), 1)
    rank = dot(hit.astype(BF16), jnp.where(first < second, 1.0, 0.0).astype(BF16))
    per_row = feat // samples
    for expert in range(experts):
        limit = counts[0, expert].astype(F32)
        keep = jnp.where(rank[expert : expert + 1, :] < limit, hits[expert], 0.0)
        row, column = samples + expert // per_row, expert % per_row * samples
        out[row : row + 1, column : column + samples] = keep
    copies[2].wait()


def act_kernel(turns, block, chips, seeded, samples, place, *refs):
    parts, refs = refs[:2], refs[2:]
    refs, (high, low, turned) = refs[:-3], refs[-3:]
    seeds, outs = (refs[: len(refs) // 2], refs[len(refs) // 2 :]) if seeded else ((), refs)
    feat = parts[0].shape[1]
    width = outs[0].shape[3]
    mine, expert = place[0], place[1]
    split_rows(parts, samples, high, low, feat)
    keeps = [keep_row(parts, samples, expert ^ (2 * turn)) for turn in turns]
    places = slots(chips)
    rows = lax.broadcasted_iota(jnp.int32, (block, width), 0)
    columns = lax.broadcasted_iota(jnp.int32, (block, width), 1)
    corner = jnp.logical_and(rows == block - 1, columns == 0)
    for k in range(chips):
        column, row = band_place(mine ^ (2 * k), block)
        both, tops = weighted(left_rows(parts, samples, turned, column, row, block), keeps)
        total = three(both, tops, high[:, pl.ds(column, width)], low[:, pl.ds(column, width)])
        for number, keep in enumerate(keeps):
            count = jnp.sum(keep, axis=1, keepdims=True)
            value = jnp.where(corner, count, total[number * block : (number + 1) * block])
            for half in range(2):
                here = value[half * (block // 2) : (half + 1) * (block // 2)]
                store(outs, seeds, 0, places[k, half], number, slice(0, width), here)


def grad_kernel(turns, block, chips, seeded, samples, place, *refs):
    grads, acts, refs = refs[:2], refs[2:4], refs[4:]
    refs, (high, low, act_high, act_low, turned) = refs[:-5], refs[-5:]
    seeds, outs = (refs[: len(refs) // 2], refs[len(refs) // 2 :]) if seeded else ((), refs)
    feat = grads[0].shape[1]
    width = outs[0].shape[3]
    mine, expert = place[0], place[1]
    split_rows(grads, samples, high, low, feat)
    split_rows(acts, samples, act_high, act_low, feat)
    keeps = [keep_row(acts, samples, expert ^ (2 * turn)) for turn in turns]
    places = slots(chips)
    for k in range(chips):
        column, row = band_place(mine ^ (2 * k), block)
        both, tops = weighted(left_rows(grads, samples, turned, column, row, block), keeps)
        total = three(both, tops, high[:, pl.ds(column, width)], low[:, pl.ds(column, width)])
        mixed = three(both, tops, act_high[...], act_low[...])
        for number in range(len(keeps)):
            for half in range(2):
                first = number * block + half * (block // 2)
                here = slice(first, first + block // 2)
                place = places[k, half]
                if number:
                    store(outs, seeds, 2, place, number - 1, slice(0, width), total[here])
                    store(outs, seeds, 2, place, number - 1, slice(width, width + feat), mixed[here])
                else:
                    store(outs, seeds, 0, place, 0, slice(0, width), total[here])
                    store(outs, seeds, 1, place, 0, slice(0, feat), mixed[here])


def whole_in_vmem(count):
    return [pl.BlockSpec(memory_space=pltpu.VMEM)] * count


def prepare(routes, counts, acts):
    samples, feat = acts.shape
    rows = samples + 8 * -(-counts.shape[1] * samples // (8 * feat))
    return pl.pallas_call(
        prepare_kernel,
        out_shape=jax.ShapeDtypeStruct((rows, feat), F32),
        in_specs=[pl.BlockSpec(memory_space=pltpu.HBM)] * 3,
        out_specs=pl.BlockSpec(memory_space=pltpu.VMEM),
        scratch_shapes=[
            pltpu.VMEM(routes.shape[::-1], jnp.int32),
            pltpu.SMEM(counts.shape, jnp.int32),
            pltpu.SemaphoreType.DMA((3,)),
        ],
        compiler_params=pltpu.CompilerParams(vmem_limit_bytes=16 * MIB),
    )(routes.T, counts, acts)


def bands(body, turns, groups, place, parts, seeds, samples, chips, block):
    feat = parts[0].shape[1]
    extended = pltpu.VMEM((2 * samples, feat + feat // 2), BF16)
    plain = pltpu.VMEM((2 * samples, feat), BF16)
    scratch = [extended, extended] + ([plain, plain] if len(parts) > 2 else [])
    shapes = [
        jax.ShapeDtypeStruct((len(group), count, block // 2, width), F32)
        for count, width in groups
        for order in orders(chips)
        for group in held_and_sent(chips, order)
    ]
    operands = (*parts, *seeds)
    limit = 36 if len(parts) > 2 else 20
    return pl.pallas_call(
        functools.partial(body, range(turns), block, chips, bool(seeds), samples),
        out_shape=shapes,
        in_specs=[pl.BlockSpec(memory_space=pltpu.SMEM)] + whole_in_vmem(len(operands)),
        out_specs=whole_in_vmem(len(shapes)),
        scratch_shapes=scratch + [pltpu.VMEM((TILE, 2 * samples), F32)],
        compiler_params=pltpu.CompilerParams(vmem_limit_bytes=limit * MIB),
    )(place, *operands)


def unfold(bands, full):
    tiles = full.shape[0] // TILE
    first_column = lax.broadcasted_iota(jnp.int32, (TILE, TILE), 1) == 0
    for i in range(tiles):
        for step in range(tiles // 2 + 1):
            j = (i + step) % tiles
            here = bands[i * TILE : (i + 1) * TILE, step * TILE : (step + 1) * TILE]
            if step == 0:
                here = jnp.where(first_column, here.T, here)
            full[i * TILE : (i + 1) * TILE, j * TILE : (j + 1) * TILE] = here
            if 0 < step < tiles // 2:
                full[j * TILE : (j + 1) * TILE, i * TILE : (i + 1) * TILE] = here.T


def damping(full):
    size = full.shape[0]
    value = full[...]
    lanes = lax.broadcasted_iota(jnp.int32, (size, size), 1)
    sublanes = lax.broadcasted_iota(jnp.int32, (size, size), 0)
    trace = jnp.sum(jnp.sum(jnp.where(lanes == sublanes, value, 0.0), axis=0, keepdims=True), axis=1, keepdims=True)
    largest = jnp.max(jnp.sum(jnp.abs(value), axis=0, keepdims=True), axis=1, keepdims=True)
    damp = trace * (0.1 / size)
    return damp, 1.0 / (largest + damp)


def times(left, high, low):
    rows = left.shape[0]
    top, rest = split(left)
    first = dot(jnp.concatenate([top, rest], axis=0), high[...])
    return first[0:rows] + first[rows : 2 * rows] + dot(top, low[...])


def gather_order(order):
    offsets = [0]
    for bit in order:
        offsets += [k | (1 << bit) for k in offsets]
    return offsets


def row_pieces(place, block, chips, arrays):
    step = block // 2
    blocks = [
        value[first : first + block, :] for value in arrays for first in range(0, value.shape[0], block)
    ]
    pieces = []
    for number, value in enumerate(blocks):
        core, position = number // chips, number % chips
        for half, order in enumerate(orders(chips)):
            owner = place[0] ^ (2 * gather_order(order)[position] + core)
            here = pl.ds(pl.multiple_of(owner * block + half * step, step), step)
            pieces.append((here, value[half * step : (half + 1) * step, :]))
    return pieces


def factor_rows(place, block, blocks, bands, full):
    for here, value in row_pieces(place, block, bands.shape[0] // (2 * block), blocks):
        bands[here, :] = value
    unfold(bands, full)
    return full[pl.ds(pl.multiple_of(place[0] * block, block), block), :]


def act_factor_kernel(place, *refs):
    blocks, (factor, scales, high, low), (bands, full) = refs[:-6], refs[-6:-2], refs[-2:]
    factor[...] = factor_rows(place, factor.shape[0], blocks, bands, full)
    damp, alpha = damping(full)
    scales[0:1, :] = jnp.broadcast_to(damp, (1, TILE))
    scales[1:2, :] = jnp.broadcast_to(alpha, (1, TILE))
    high[...], low[...] = split(full[...])


def grad_factor_kernel(place, *refs):
    blocks, (factor, inverse), (bands, full, high, low) = refs[:-6], refs[-6:-4], refs[-4:]
    block, feat = factor.shape
    rows = factor_rows(place, block, blocks, bands, full)
    factor[...] = rows
    damp, alpha = damping(full)
    high[...], low[...] = split(full[...])
    lanes = lax.broadcasted_iota(jnp.int32, (block, feat), 1)
    sublanes = lax.broadcasted_iota(jnp.int32, (block, feat), 0)
    unit = jnp.where(lanes == sublanes + place[0] * block, 1.0, 0.0).astype(F32)
    rest_rows = unit - alpha * (rows + damp * unit)
    once = 2.0 * rest_rows - alpha * (times(rest_rows, high, low) + damp * rest_rows)
    inverse[...] = alpha * (unit + rest_rows + once - alpha * (times(once, high, low) + damp * once))


def update_kernel(place, *refs):
    blocks = refs[:-9]
    inverse, scales, act_high, act_low, momentum, weights, moment_out, weight_out, full = refs[-9:]
    block = momentum.shape[0]
    for here, value in row_pieces(place, block, full.shape[0] // (2 * block), blocks):
        full[here, :] = value
    damp, alpha = scales[0:1, 0:1], scales[1:2, 0:1]
    half_way = times(inverse[...], *split(full[...]))
    value = half_way
    for _ in range(3):
        value = half_way + value - alpha * (times(value, act_high[...], act_low[...]) + damp * value)
    moment = 0.9 * momentum[...] + alpha * value
    moment_out[...] = moment
    weight_out[...] = weights[...] - 0.5 * moment


def on_core(body, place, operands, shapes, scratch, limit):
    return pl.pallas_call(
        body,
        out_shape=shapes,
        in_specs=[pl.BlockSpec(memory_space=pltpu.SMEM)] + whole_in_vmem(len(operands)),
        out_specs=whole_in_vmem(len(shapes)),
        scratch_shapes=scratch,
        compiler_params=pltpu.CompilerParams(vmem_limit_bytes=limit * MIB),
    )(place, *operands)


def act_factor_rows(place, blocks, block, feat):
    shapes = [((block, feat), F32), ((8, TILE), F32), ((feat, feat), BF16), ((feat, feat), BF16)]
    shapes = [jax.ShapeDtypeStruct(*shape) for shape in shapes]
    scratch = [pltpu.VMEM((feat, blocks[0].shape[1]), F32), pltpu.VMEM((feat, feat), F32)]
    return on_core(act_factor_kernel, place, blocks, shapes, scratch, 32)


def grad_factor_rows(place, blocks, block, feat):
    shapes = [jax.ShapeDtypeStruct((block, feat), F32)] * 2
    scratch = [pltpu.VMEM((feat, blocks[0].shape[1]), F32), pltpu.VMEM((feat, feat), F32)]
    scratch += [pltpu.VMEM((feat, feat), BF16)] * 2
    return on_core(grad_factor_kernel, place, blocks, shapes, scratch, 32)


def update_rows(place, blocks, inverse, scales, high, low, momentum, weights):
    block, feat = momentum.shape
    operands = (*blocks, inverse, scales, high, low, momentum, weights)
    shapes = [jax.ShapeDtypeStruct((block, feat), F32)] * 2
    return on_core(update_kernel, place, operands, shapes, [pltpu.VMEM((feat, feat), F32)], 32)


def swap(value, axis, step):
    size = lax.axis_size(axis)
    return lax.ppermute(value, axis, [(i, i ^ step) for i in range(size)])


class PlaneSum:
    def __init__(self, pieces, chips):
        self.steps = [list(order) for order in orders(chips)]
        self.offsets = [held_and_sent(chips, order)[0] for order in self.steps]
        self.held, self.leaving = list(pieces[0::2]), list(pieces[1::2])

    def send(self):
        self.got = [swap(value, "dp", 2 << order[0]) for value, order in zip(self.leaving, self.steps)]

    def add(self):
        self.leaving = []
        for half, order in enumerate(self.steps):
            offsets = self.offsets[half]
            sums = {k: self.held[half][i] + self.got[half][i] for i, k in enumerate(offsets)}
            order.pop(0)
            if order:
                offsets = [k for k in offsets if not (k >> order[0]) & 1]
                self.leaving.append(jnp.stack([sums[k | (1 << order[0])] for k in offsets]))
            self.offsets[half] = offsets
            self.held[half] = [sums[k] for k in offsets]

    def finish(self):
        while self.steps[0]:
            self.send()
            self.add()
        return [held[0] for held in self.held]


def across(far):
    return [swap(far[number], "expert", 2 * (number + 1)) for number in range(far.shape[0])]


class Gather:
    def __init__(self, halves, chips):
        self.chips, self.orders = chips, orders(chips)
        self.halves, self.whole = halves, {}

    def begin(self):
        block = jnp.concatenate(self.halves, axis=0)
        self.whole = {order[0]: swap(block, "dp", 2 << order[0]) for order in self.orders}

    def relay(self):
        step = self.halves[0].shape[0]
        self.held = []
        for half, order in enumerate(self.orders):
            held = [self.halves[half]]
            for bit in order:
                came = [swap(value, "dp", 2 << bit) for value in held[1:]]
                if bit in self.whole:
                    own = self.whole[bit][half * step : (half + 1) * step]
                else:
                    own = swap(held[0], "dp", 2 << bit)
                held += [own] + came
            self.held.append(held)

    def hold_last(self, value):
        last, value = together([held[-1] for held in self.held], value)
        self.held = [held[:-1] + [block] for held, block in zip(self.held, last)]
        return value

    def exchange(self, first=0, last=None):
        pairs = list(zip(*self.held))[first:last]
        mine = jnp.concatenate([value for pair in pairs for value in pair], axis=0)
        return mine, swap(mine, "dp", 1)


def together(*values):
    return lax.optimization_barrier(values)


def on_device(acts, grads_out, routes, counts, old_act_factor, old_grad_factor, momentum, weights):
    devices, experts = lax.axis_size("dp"), lax.axis_size("expert")
    chips = devices // 2
    samples, feat, block = acts.shape[0], acts.shape[1], weights.shape[1]
    width = feat // 2 + TILE
    mine = lax.axis_index("dp")
    place = jnp.stack([mine, lax.axis_index("expert")]).astype(jnp.int32)

    def own_band(old):
        start = mine * block // TILE * TILE
        wide = jnp.concatenate([old[0], old[0][:, 0 : width - TILE]], axis=1)
        return 0.5 * lax.dynamic_slice_in_dim(wide, start, width, 1)

    turns = experts // 2
    size = (samples, chips, block)
    act_groups = ((turns, width),)
    grad_groups = ((1, width), (1, feat), (turns - 1, width + feat))

    acts = prepare(routes, counts, acts)
    acts_far = swap(acts, "expert", 1)
    near_acts = (acts, swap(acts, "dp", 1))
    act_seeds = bands(act_kernel, turns, act_groups, place, near_acts, (), *size)
    grads_far = swap(grads_out, "expert", 1)
    grad_parts = (grads_out, swap(grads_out, "dp", 1)) + near_acts
    grad_seeds = bands(grad_kernel, turns, grad_groups, place, grad_parts, (), *size)
    old_act, old_grad = own_band(old_act_factor), own_band(old_grad_factor)
    early = (act_seeds, grad_seeds, old_act, old_grad)
    acts_far, (act_seeds, grad_seeds, old_act, old_grad) = together(acts_far, early)

    far_acts = (acts_far, swap(acts_far, "dp", 1))
    act_sum = PlaneSum(bands(act_kernel, turns, act_groups, place, far_acts, act_seeds, *size), chips)
    act_sum.send()
    grads_far, act_sum.held = together(grads_far, act_sum.held)
    grad_parts = (grads_far, swap(grads_far, "dp", 1)) + far_acts
    act_sum.add()
    grad_seeds, act_sum.leaving = together(grad_seeds, act_sum.leaving)
    act_sum.send()
    pieces = bands(grad_kernel, turns, grad_groups, place, grad_parts, grad_seeds, *size)

    grad_sum, mixed_sum, far_sum = [PlaneSum(pieces[first : first + 4], chips) for first in (0, 4, 8)]
    far_sum.send()
    act_sum.held, far_sum.held = together(act_sum.held, far_sum.held)
    act_sum.add()
    act_sums = act_sum.finish()
    act_across = across(jnp.stack([value[1:] for value in act_sums], axis=1))
    grad_sum.leaving, far_sum.got = together(grad_sum.leaving, far_sum.got)
    grad_sum.send()
    far_sum.add()
    far_sum.leaving, act_across = together(far_sum.leaving, act_across)
    far_sum.send()
    grad_sum.add()
    mixed_sum.leaving, grad_sum.leaving = together(mixed_sum.leaving, grad_sum.leaving)
    mixed_sum.send()
    grad_sum.send()
    far_sum.add()
    far_sums = far_sum.finish()

    step = block // 2
    parts = [slice(half * step, (half + 1) * step) for half in range(2)]
    act_totals = [
        sum((there[half] for there in act_across), value[0]) for half, value in enumerate(act_sums)
    ]
    total = jnp.maximum(act_totals[1][-1:, 0:1], 1.0)
    act_halves = [old_act[here] + 0.5 * (value / total) for here, value in zip(parts, act_totals)]
    across_grad = across(jnp.stack([value[:, :, 0:width] for value in far_sums], axis=1))
    far_mixed = jnp.stack([value[:, :, width:] for value in far_sums], axis=1)
    grad_sum.add()
    grad_sums = grad_sum.finish()
    mixed_sum.held, across_grad = together(mixed_sum.held, across_grad)
    mixed_sum.add()
    mixed_sum.leaving, far_mixed = together(mixed_sum.leaving, far_mixed)
    mixed_sum.send()
    across_mixed = across(far_mixed)

    def both(near, far):
        return [sum((there[half] for there in far), value[0]) / total for half, value in enumerate(near)]

    grad_halves = [old_grad[here] + 0.5 * value for here, value in zip(parts, both(grad_sums, across_grad))]
    grad_gather = Gather(grad_halves, chips)
    grad_gather.begin()
    early = (grad_gather.whole, mixed_sum.got)
    act_halves, (grad_gather.whole, mixed_sum.got) = together(act_halves, early)
    mixed_sum.add()
    mixed_sums = mixed_sum.finish()
    act_gather = Gather(act_halves, chips)
    act_gather.begin()
    grad_gather.relay()
    act_gather.relay()
    across_mixed, _ = together(across_mixed, act_gather.whole)
    mixed_gather = Gather(both(mixed_sums, across_mixed), chips)
    mixed_gather.begin()
    mixed_gather.whole = act_gather.hold_last(mixed_gather.whole)
    mixed_gather.relay()
    mine, theirs = mixed_gather.exchange(0, -1)
    act_out, *act_square = act_factor_rows(place, act_gather.exchange(), block, feat)
    grad_blocks, act_square = together(grad_gather.exchange(), act_square)
    grad_out, inverse = grad_factor_rows(place, grad_blocks, block, feat)
    inverse = mixed_gather.hold_last(inverse)
    my_last, their_last = mixed_gather.exchange(-1)
    mixed_blocks = (mine, my_last, theirs, their_last)
    outs = update_rows(place, mixed_blocks, inverse, *act_square, momentum[0], weights[0])
    return tuple(out[None] for out in (act_out, grad_out, *outs))


def solution(mesh):
    rows = P(("dp", "expert"), None)
    matrix = P("expert", "dp", None)
    return jax.shard_map(
        on_device,
        mesh=mesh,
        in_specs=(rows,) * 4 + (matrix,) * 4,
        out_specs=(matrix,) * 4,
        check_vma=False,
    )
```

```python
import functools

import jax
import jax.numpy as jnp
from jax import lax
from jax.experimental import pallas as pl
from jax.experimental.pallas import tpu as pltpu
from jax.sharding import PartitionSpec as P

F32 = jnp.float32
BF16 = jnp.bfloat16
TILE = 128
MIB = 1024 * 1024


def split(value):
    high = value.astype(BF16)
    return high, (value - high.astype(F32)).astype(BF16)


def dot(left, right):
    return jnp.dot(left, right, preferred_element_type=F32)


def band_place(owner, block):
    per_tile = TILE // block
    if per_tile == 1:
        return pl.multiple_of(owner * TILE, TILE), 0
    return (
        pl.multiple_of(lax.div(owner, per_tile) * TILE, TILE),
        pl.multiple_of(lax.rem(owner, per_tile) * block, block),
    )


def rows_of(part, window):
    first, count = window
    return slice(0, count) if part.shape[0] == count else slice(first, first + count)


def split_rows(parts, window, high, low, feat):
    extra = high.shape[1] - feat
    count = window[1]
    for number, part in enumerate(parts):
        here = slice(number * count, (number + 1) * count)
        top, rest = split(part[rows_of(part, window), :])
        high[here, 0:feat] = top
        low[here, 0:feat] = rest
        if extra:
            high[here, feat : feat + extra] = top[:, 0:extra]
            low[here, feat : feat + extra] = rest[:, 0:extra]


def left_rows(parts, window, turned, column, row, block):
    count = window[1]
    for number, part in enumerate(parts):
        here = slice(number * count, (number + 1) * count)
        turned[:, here] = part[rows_of(part, window), pl.ds(column, TILE)].T
    return turned[pl.ds(row, block), :]


def keep_row(parts, samples, window, expert):
    first, count = window
    per_row = parts[0].shape[1] // samples
    row = samples + lax.div(expert, per_row)
    column = pl.multiple_of(lax.rem(expert, per_row) * samples, TILE)
    keeps = [part[pl.ds(row, 1), pl.ds(column, samples)] for part in parts]
    return jnp.concatenate([keep[:, first : first + count] for keep in keeps], axis=1)


def weighted(rows, keeps):
    halves = [split(rows * keep) for keep in keeps]
    tops = [half[0] for half in halves]
    return jnp.concatenate(tops + [half[1] for half in halves], axis=0), jnp.concatenate(tops, axis=0)


def three(both, tops, high, low):
    half = tops.shape[0]
    first = dot(both, high)
    return first[0:half] + first[half : 2 * half] + dot(tops, low)


def orders(chips):
    bits = list(range(chips.bit_length() - 1))
    return bits, bits[1:] + bits[:1]


def held_and_sent(chips, order):
    if not order:
        return [0], []
    held = [k for k in range(chips) if not (k >> order[0]) & 1]
    return held, [k | (1 << order[0]) for k in held]


def slots(chips):
    places = {}
    for half, order in enumerate(orders(chips)):
        for which, group in enumerate(held_and_sent(chips, order)):
            for position, k in enumerate(group):
                places[k, half] = (2 * half + which, position)
    return places


def store(outs, seeds, group, place, number, columns, value):
    output, position = 4 * group + place[0], place[1]
    if seeds:
        value = value + seeds[output][position, number, :, columns]
    outs[output][position, number, :, columns] = value


def prepare_kernel(routes_ref, counts_ref, acts, out, routes, counts, sems):
    samples, feat = acts.shape
    experts = counts.shape[1]
    copies = [
        pltpu.make_async_copy(routes_ref, routes, sems.at[0]),
        pltpu.make_async_copy(counts_ref, counts, sems.at[1]),
        pltpu.make_async_copy(acts, out.at[pl.ds(0, samples), :], sems.at[2]),
    ]
    for copy in copies:
        copy.start()
    out[samples:, :] = jnp.zeros((out.shape[0] - samples, feat), F32)
    for copy in copies[:2]:
        copy.wait()
    hits = []
    for expert in range(experts):
        same = [jnp.where(routes[k : k + 1, :] == expert, 1.0, 0.0) for k in range(routes.shape[0])]
        hits.append(sum(same[1:], same[0]))
    hit = jnp.concatenate(hits, axis=0)
    first = lax.broadcasted_iota(jnp.int32, (samples, samples), 0)
    second = lax.broadcasted_iota(jnp.int32, (samples, samples), 1)
    rank = dot(hit.astype(BF16), jnp.where(first < second, 1.0, 0.0).astype(BF16))
    per_row = feat // samples
    for expert in range(experts):
        limit = counts[0, expert].astype(F32)
        keep = jnp.where(rank[expert : expert + 1, :] < limit, hits[expert], 0.0)
        row, column = samples + expert // per_row, expert % per_row * samples
        out[row : row + 1, column : column + samples] = keep
    copies[2].wait()


def act_kernel(turns, block, chips, seeded, samples, window, place, *refs):
    parts, refs = refs[:2], refs[2:]
    refs, (high, low, turned) = refs[:-3], refs[-3:]
    seeds, outs = (refs[: len(refs) // 2], refs[len(refs) // 2 :]) if seeded else ((), refs)
    feat = parts[0].shape[1]
    width = outs[0].shape[3]
    mine, expert = place[0], place[1]
    split_rows(parts, window, high, low, feat)
    keeps = [keep_row(parts, samples, window, expert ^ (2 * turn)) for turn in turns]
    places = slots(chips)
    rows = lax.broadcasted_iota(jnp.int32, (block, width), 0)
    columns = lax.broadcasted_iota(jnp.int32, (block, width), 1)
    corner = jnp.logical_and(rows == block - 1, columns == 0)
    for k in range(chips):
        column, row = band_place(mine ^ (2 * k), block)
        both, tops = weighted(left_rows(parts, window, turned, column, row, block), keeps)
        total = three(both, tops, high[:, pl.ds(column, width)], low[:, pl.ds(column, width)])
        for number, keep in enumerate(keeps):
            count = jnp.sum(keep, axis=1, keepdims=True)
            value = jnp.where(corner, count, total[number * block : (number + 1) * block])
            for half in range(2):
                here = value[half * (block // 2) : (half + 1) * (block // 2)]
                store(outs, seeds, 0, places[k, half], number, slice(0, width), here)


def grad_kernel(turns, block, chips, seeded, samples, window, place, *refs):
    grads, acts, refs = refs[:2], refs[2:4], refs[4:]
    refs, (high, low, act_high, act_low, turned) = refs[:-5], refs[-5:]
    seeds, outs = (refs[: len(refs) // 2], refs[len(refs) // 2 :]) if seeded else ((), refs)
    feat = grads[0].shape[1]
    width = outs[0].shape[3]
    mine, expert = place[0], place[1]
    split_rows(grads, window, high, low, feat)
    split_rows(acts, window, act_high, act_low, feat)
    keeps = [keep_row(acts, samples, window, expert ^ (2 * turn)) for turn in turns]
    places = slots(chips)
    for k in range(chips):
        column, row = band_place(mine ^ (2 * k), block)
        both, tops = weighted(left_rows(grads, window, turned, column, row, block), keeps)
        total = three(both, tops, high[:, pl.ds(column, width)], low[:, pl.ds(column, width)])
        mixed = three(both, tops, act_high[...], act_low[...])
        for number in range(len(keeps)):
            for half in range(2):
                first = number * block + half * (block // 2)
                here = slice(first, first + block // 2)
                place = places[k, half]
                if number:
                    store(outs, seeds, 2, place, number - 1, slice(0, width), total[here])
                    store(outs, seeds, 2, place, number - 1, slice(width, width + feat), mixed[here])
                else:
                    store(outs, seeds, 0, place, 0, slice(0, width), total[here])
                    store(outs, seeds, 1, place, 0, slice(0, feat), mixed[here])


def whole_in_vmem(count):
    return [pl.BlockSpec(memory_space=pltpu.VMEM)] * count


def prepare(routes, counts, acts):
    samples, feat = acts.shape
    rows = samples + 8 * -(-counts.shape[1] * samples // (8 * feat))
    return pl.pallas_call(
        prepare_kernel,
        out_shape=jax.ShapeDtypeStruct((rows, feat), F32),
        in_specs=[pl.BlockSpec(memory_space=pltpu.HBM)] * 3,
        out_specs=pl.BlockSpec(memory_space=pltpu.VMEM),
        scratch_shapes=[
            pltpu.VMEM(routes.shape[::-1], jnp.int32),
            pltpu.SMEM(counts.shape, jnp.int32),
            pltpu.SemaphoreType.DMA((3,)),
        ],
        compiler_params=pltpu.CompilerParams(vmem_limit_bytes=60 * MIB),
    )(routes.T, counts, acts)


def bands(body, turns, groups, place, parts, seeds, samples, chips, block, window=None):
    feat = parts[0].shape[1]
    window = window or (0, samples)
    extended = pltpu.VMEM((2 * window[1], feat + feat // 2), BF16)
    plain = pltpu.VMEM((2 * window[1], feat), BF16)
    scratch = [extended, extended] + ([plain, plain] if len(parts) > 2 else [])
    shapes = [
        jax.ShapeDtypeStruct((len(group), count, block // 2, width), F32)
        for count, width in groups
        for order in orders(chips)
        for group in held_and_sent(chips, order)
    ]
    operands = (*parts, *seeds)
    limit = 36 if len(parts) > 2 else 20
    return pl.pallas_call(
        functools.partial(body, range(turns), block, chips, bool(seeds), samples, window),
        out_shape=shapes,
        in_specs=[pl.BlockSpec(memory_space=pltpu.SMEM)] + whole_in_vmem(len(operands)),
        out_specs=whole_in_vmem(len(shapes)),
        scratch_shapes=scratch + [pltpu.VMEM((TILE, 2 * window[1]), F32)],
        compiler_params=pltpu.CompilerParams(vmem_limit_bytes=limit * MIB),
    )(place, *operands)


def unfold(bands, full):
    tiles = full.shape[0] // TILE
    first_column = lax.broadcasted_iota(jnp.int32, (TILE, TILE), 1) == 0
    for i in range(tiles):
        for step in range(tiles // 2 + 1):
            j = (i + step) % tiles
            here = bands[i * TILE : (i + 1) * TILE, step * TILE : (step + 1) * TILE]
            if step == 0:
                here = jnp.where(first_column, here.T, here)
            full[i * TILE : (i + 1) * TILE, j * TILE : (j + 1) * TILE] = here
            if 0 < step < tiles // 2:
                full[j * TILE : (j + 1) * TILE, i * TILE : (i + 1) * TILE] = here.T


def damping(full):
    size = full.shape[0]
    value = full[...]
    lanes = lax.broadcasted_iota(jnp.int32, (size, size), 1)
    sublanes = lax.broadcasted_iota(jnp.int32, (size, size), 0)
    trace = jnp.sum(jnp.sum(jnp.where(lanes == sublanes, value, 0.0), axis=0, keepdims=True), axis=1, keepdims=True)
    largest = jnp.max(jnp.sum(jnp.abs(value), axis=0, keepdims=True), axis=1, keepdims=True)
    damp = trace * (0.1 / size)
    return damp, 1.0 / (largest + damp)


def times(left, high, low):
    rows = left.shape[0]
    top, rest = split(left)
    first = dot(jnp.concatenate([top, rest], axis=0), high[...])
    return first[0:rows] + first[rows : 2 * rows] + dot(top, low[...])


def gather_order(order):
    offsets = [0]
    for bit in order:
        offsets += [k | (1 << bit) for k in offsets]
    return offsets


def row_pieces(place, block, chips, arrays):
    step = block // 2
    blocks = [
        value[first : first + block, :] for value in arrays for first in range(0, value.shape[0], block)
    ]
    pieces = []
    for number, value in enumerate(blocks):
        core, position = number // chips, number % chips
        for half, order in enumerate(orders(chips)):
            owner = place[0] ^ (2 * gather_order(order)[position] + core)
            here = pl.ds(pl.multiple_of(owner * block + half * step, step), step)
            pieces.append((here, value[half * step : (half + 1) * step, :]))
    return pieces


def factor_rows(place, block, blocks, bands, full):
    for here, value in row_pieces(place, block, bands.shape[0] // (2 * block), blocks):
        bands[here, :] = value
    unfold(bands, full)
    return full[pl.ds(pl.multiple_of(place[0] * block, block), block), :]


def act_factor_kernel(place, *refs):
    blocks, (factor, scales, high, low), (bands, full) = refs[:-6], refs[-6:-2], refs[-2:]
    factor[...] = factor_rows(place, factor.shape[0], blocks, bands, full)
    damp, alpha = damping(full)
    scales[0:1, :] = jnp.broadcast_to(damp, (1, TILE))
    scales[1:2, :] = jnp.broadcast_to(alpha, (1, TILE))
    high[...], low[...] = split(full[...])


def grad_factor_kernel(place, *refs):
    blocks, (factor, inverse), (bands, full, high, low) = refs[:-6], refs[-6:-4], refs[-4:]
    block, feat = factor.shape
    rows = factor_rows(place, block, blocks, bands, full)
    factor[...] = rows
    damp, alpha = damping(full)
    high[...], low[...] = split(full[...])
    lanes = lax.broadcasted_iota(jnp.int32, (block, feat), 1)
    sublanes = lax.broadcasted_iota(jnp.int32, (block, feat), 0)
    unit = jnp.where(lanes == sublanes + place[0] * block, 1.0, 0.0).astype(F32)
    rest_rows = unit - alpha * (rows + damp * unit)
    once = 2.0 * rest_rows - alpha * (times(rest_rows, high, low) + damp * rest_rows)
    inverse[...] = alpha * (unit + rest_rows + once - alpha * (times(once, high, low) + damp * once))


def update_kernel(place, *refs):
    blocks = refs[:-9]
    inverse, scales, act_high, act_low, momentum, weights, moment_out, weight_out, full = refs[-9:]
    block = momentum.shape[0]
    for here, value in row_pieces(place, block, full.shape[0] // (2 * block), blocks):
        full[here, :] = value
    damp, alpha = scales[0:1, 0:1], scales[1:2, 0:1]
    half_way = times(inverse[...], *split(full[...]))
    value = half_way
    for _ in range(3):
        value = half_way + value - alpha * (times(value, act_high[...], act_low[...]) + damp * value)
    moment = 0.9 * momentum[...] + alpha * value
    moment_out[...] = moment
    weight_out[...] = weights[...] - 0.5 * moment


def on_core(body, place, operands, shapes, scratch, limit):
    return pl.pallas_call(
        body,
        out_shape=shapes,
        in_specs=[pl.BlockSpec(memory_space=pltpu.SMEM)] + whole_in_vmem(len(operands)),
        out_specs=whole_in_vmem(len(shapes)),
        scratch_shapes=scratch,
        compiler_params=pltpu.CompilerParams(vmem_limit_bytes=limit * MIB),
    )(place, *operands)


def act_factor_rows(place, blocks, block, feat):
    shapes = [((block, feat), F32), ((8, TILE), F32), ((feat, feat), BF16), ((feat, feat), BF16)]
    shapes = [jax.ShapeDtypeStruct(*shape) for shape in shapes]
    scratch = [pltpu.VMEM((feat, blocks[0].shape[1]), F32), pltpu.VMEM((feat, feat), F32)]
    return on_core(act_factor_kernel, place, blocks, shapes, scratch, 32)


def grad_factor_rows(place, blocks, block, feat):
    shapes = [jax.ShapeDtypeStruct((block, feat), F32)] * 2
    scratch = [pltpu.VMEM((feat, blocks[0].shape[1]), F32), pltpu.VMEM((feat, feat), F32)]
    scratch += [pltpu.VMEM((feat, feat), BF16)] * 2
    return on_core(grad_factor_kernel, place, blocks, shapes, scratch, 32)


def update_rows(place, blocks, inverse, scales, high, low, momentum, weights):
    block, feat = momentum.shape
    operands = (*blocks, inverse, scales, high, low, momentum, weights)
    shapes = [jax.ShapeDtypeStruct((block, feat), F32)] * 2
    return on_core(update_kernel, place, operands, shapes, [pltpu.VMEM((feat, feat), F32)], 32)


def swap(value, axis, step):
    size = lax.axis_size(axis)
    return lax.ppermute(value, axis, [(i, i ^ step) for i in range(size)])


class PlaneSum:
    def __init__(self, pieces, chips):
        self.steps = [list(order) for order in orders(chips)]
        self.offsets = [held_and_sent(chips, order)[0] for order in self.steps]
        self.held, self.leaving = list(pieces[0::2]), list(pieces[1::2])

    def send(self):
        self.got = [swap(value, "dp", 2 << order[0]) for value, order in zip(self.leaving, self.steps)]

    def add(self):
        self.leaving = []
        for half, order in enumerate(self.steps):
            offsets = self.offsets[half]
            sums = {k: self.held[half][i] + self.got[half][i] for i, k in enumerate(offsets)}
            order.pop(0)
            if order:
                offsets = [k for k in offsets if not (k >> order[0]) & 1]
                self.leaving.append(jnp.stack([sums[k | (1 << order[0])] for k in offsets]))
            self.offsets[half] = offsets
            self.held[half] = [sums[k] for k in offsets]

    def finish(self):
        while self.steps[0]:
            self.send()
            self.add()
        return [held[0] for held in self.held]


def across(far):
    return [swap(far[number], "expert", 2 * (number + 1)) for number in range(far.shape[0])]


class Gather:
    def __init__(self, halves, chips):
        self.chips, self.orders = chips, orders(chips)
        self.halves, self.whole = halves, {}

    def begin(self):
        block = jnp.concatenate(self.halves, axis=0)
        self.whole = {order[0]: swap(block, "dp", 2 << order[0]) for order in self.orders}

    def relay(self):
        step = self.halves[0].shape[0]
        self.held = []
        for half, order in enumerate(self.orders):
            held = [self.halves[half]]
            for bit in order:
                came = [swap(value, "dp", 2 << bit) for value in held[1:]]
                if bit in self.whole:
                    own = self.whole[bit][half * step : (half + 1) * step]
                else:
                    own = swap(held[0], "dp", 2 << bit)
                held += [own] + came
            self.held.append(held)

    def hold_last(self, value):
        last, value = together([held[-1] for held in self.held], value)
        self.held = [held[:-1] + [block] for held, block in zip(self.held, last)]
        return value

    def exchange(self, first=0, last=None):
        pairs = list(zip(*self.held))[first:last]
        mine = jnp.concatenate([value for pair in pairs for value in pair], axis=0)
        return mine, swap(mine, "dp", 1)


def together(*values):
    return lax.optimization_barrier(values)


def on_device(acts, grads_out, routes, counts, old_act_factor, old_grad_factor, momentum, weights):
    devices, experts = lax.axis_size("dp"), lax.axis_size("expert")
    chips = devices // 2
    samples, feat, block = acts.shape[0], acts.shape[1], weights.shape[1]
    width = feat // 2 + TILE
    mine = lax.axis_index("dp")
    place = jnp.stack([mine, lax.axis_index("expert")]).astype(jnp.int32)

    def own_band(old):
        start = mine * block // TILE * TILE
        wide = jnp.concatenate([old[0], old[0][:, 0 : width - TILE]], axis=1)
        return 0.5 * lax.dynamic_slice_in_dim(wide, start, width, 1)

    turns = experts // 2
    size = (samples, chips, block)
    act_groups = ((turns, width),)
    grad_groups = ((1, width), (1, feat), (turns - 1, width + feat))

    acts = prepare(routes, counts, acts)
    acts_far = swap(acts, "expert", 1)
    near_acts = (acts, swap(acts, "dp", 1))
    act_seeds = bands(act_kernel, turns, act_groups, place, near_acts, (), *size)
    windows = [(0, samples // 2), (samples // 2, samples - samples // 2)]
    grads_far = [swap(grads_out[first : first + count], "expert", 1) for first, count in windows]
    grad_parts = (grads_out, swap(grads_out, "dp", 1)) + near_acts
    grad_seeds = bands(grad_kernel, turns, grad_groups, place, grad_parts, (), *size)
    old_act, old_grad = own_band(old_act_factor), own_band(old_grad_factor)
    early = (act_seeds, grad_seeds, old_act, old_grad)
    acts_far, (act_seeds, grad_seeds, old_act, old_grad) = together(acts_far, early)

    far_acts = (acts_far, swap(acts_far, "dp", 1))
    act_sum = PlaneSum(bands(act_kernel, turns, act_groups, place, far_acts, act_seeds, *size), chips)
    act_sum.send()
    grads_far[0], act_sum.held = together(grads_far[0], act_sum.held)
    grad_parts = (grads_far[0], swap(grads_far[0], "dp", 1)) + far_acts
    grad_seeds = bands(grad_kernel, turns, grad_groups, place, grad_parts, grad_seeds, *size, windows[0])
    act_sum.got, grads_far[1], grad_seeds = together(act_sum.got, grads_far[1], grad_seeds)
    grad_parts = (grads_far[1], swap(grads_far[1], "dp", 1)) + far_acts
    act_sum.add()
    grad_seeds, act_sum.leaving = together(grad_seeds, act_sum.leaving)
    act_sum.send()
    pieces = bands(grad_kernel, turns, grad_groups, place, grad_parts, grad_seeds, *size, windows[1])

    grad_sum, mixed_sum, far_sum = [PlaneSum(pieces[first : first + 4], chips) for first in (0, 4, 8)]
    far_sum.send()
    act_sum.held, far_sum.held = together(act_sum.held, far_sum.held)
    act_sum.add()
    act_sums = act_sum.finish()
    act_across = across(jnp.stack([value[1:] for value in act_sums], axis=1))
    grad_sum.leaving, far_sum.got = together(grad_sum.leaving, far_sum.got)
    grad_sum.send()
    far_sum.add()
    far_sum.leaving, act_across = together(far_sum.leaving, act_across)
    far_sum.send()
    grad_sum.add()
    mixed_sum.leaving, grad_sum.leaving = together(mixed_sum.leaving, grad_sum.leaving)
    mixed_sum.send()
    grad_sum.send()
    far_sum.add()
    far_sums = far_sum.finish()

    step = block // 2
    parts = [slice(half * step, (half + 1) * step) for half in range(2)]
    act_totals = [
        sum((there[half] for there in act_across), value[0]) for half, value in enumerate(act_sums)
    ]
    total = jnp.maximum(act_totals[1][-1:, 0:1], 1.0)
    act_halves = [old_act[here] + 0.5 * (value / total) for here, value in zip(parts, act_totals)]
    across_grad = across(jnp.stack([value[:, :, 0:width] for value in far_sums], axis=1))
    far_mixed = jnp.stack([value[:, :, width:] for value in far_sums], axis=1)
    grad_sum.add()
    grad_sums = grad_sum.finish()
    mixed_sum.held, across_grad = together(mixed_sum.held, across_grad)
    mixed_sum.add()
    mixed_sum.leaving, far_mixed = together(mixed_sum.leaving, far_mixed)
    mixed_sum.send()
    across_mixed = across(far_mixed)

    def both(near, far):
        return [sum((there[half] for there in far), value[0]) / total for half, value in enumerate(near)]

    grad_halves = [old_grad[here] + 0.5 * value for here, value in zip(parts, both(grad_sums, across_grad))]
    grad_gather = Gather(grad_halves, chips)
    grad_gather.begin()
    early = (grad_gather.whole, mixed_sum.got)
    act_halves, (grad_gather.whole, mixed_sum.got) = together(act_halves, early)
    mixed_sum.add()
    mixed_sums = mixed_sum.finish()
    act_gather = Gather(act_halves, chips)
    act_gather.begin()
    grad_gather.relay()
    act_gather.relay()
    across_mixed, _ = together(across_mixed, act_gather.whole)
    mixed_gather = Gather(both(mixed_sums, across_mixed), chips)
    mixed_gather.begin()
    mixed_gather.whole = act_gather.hold_last(mixed_gather.whole)
    mixed_gather.relay()
    mine, theirs = mixed_gather.exchange(0, -1)
    act_out, *act_square = act_factor_rows(place, act_gather.exchange(), block, feat)
    grad_blocks, act_square = together(grad_gather.exchange(), act_square)
    grad_out, inverse = grad_factor_rows(place, grad_blocks, block, feat)
    inverse = mixed_gather.hold_last(inverse)
    my_last, their_last = mixed_gather.exchange(-1)
    mixed_blocks = (mine, my_last, theirs, their_last)
    outs = update_rows(place, mixed_blocks, inverse, *act_square, momentum[0], weights[0])
    return tuple(out[None] for out in (act_out, grad_out, *outs))


def solution(mesh):
    rows = P(("dp", "expert"), None)
    matrix = P("expert", "dp", None)
    return jax.shard_map(
        on_device,
        mesh=mesh,
        in_specs=(rows,) * 4 + (matrix,) * 4,
        out_specs=(matrix,) * 4,
        check_vma=False,
    )
```

```python
import functools

import jax
import jax.numpy as jnp
from jax import lax
from jax.experimental import pallas as pl
from jax.experimental.pallas import tpu as pltpu
from jax.sharding import PartitionSpec as P

F32 = jnp.float32
BF16 = jnp.bfloat16
TILE = 128
EXTRA = 8
MIB = 1024 * 1024


def split(value):
    high = value.astype(BF16)
    return high, (value - high.astype(F32)).astype(BF16)


def dot(left, right):
    return jnp.dot(left, right, preferred_element_type=F32)


def band_place(owner, block):
    per_tile = TILE // block
    if per_tile == 1:
        return pl.multiple_of(owner * TILE, TILE), 0
    return (
        pl.multiple_of(lax.div(owner, per_tile) * TILE, TILE),
        pl.multiple_of(lax.rem(owner, per_tile) * block, block),
    )


def split_rows(parts, samples, high, low, feat):
    extra = high.shape[1] - feat
    for number, part in enumerate(parts):
        here = slice(number * samples, (number + 1) * samples)
        top, rest = split(part[0:samples, :])
        high[here, 0:feat] = top
        low[here, 0:feat] = rest
        if extra:
            high[here, feat : feat + extra] = top[:, 0:extra]
            low[here, feat : feat + extra] = rest[:, 0:extra]


def left_rows(parts, samples, turned, column, row, block):
    for number, part in enumerate(parts):
        here = slice(number * samples, (number + 1) * samples)
        turned[:, here] = part[0:samples, pl.ds(column, TILE)].T
    return turned[pl.ds(row, block), :]


def keep_place(expert, samples, feat):
    per_row = feat // samples
    return lax.div(expert, per_row), pl.multiple_of(lax.rem(expert, per_row) * samples, TILE)


def keep_row(parts, samples, expert):
    row, column = keep_place(expert, samples, parts[0].shape[1])
    return jnp.concatenate([part[pl.ds(samples + row, 1), pl.ds(column, samples)] for part in parts], axis=1)


def weighted(rows, keeps):
    halves = [split(rows * keep) for keep in keeps]
    tops = [half[0] for half in halves]
    return jnp.concatenate(tops + [half[1] for half in halves], axis=0), jnp.concatenate(tops, axis=0)


def three(both, tops, high, low):
    half = tops.shape[0]
    first = dot(both, high)
    return first[0:half] + first[half : 2 * half] + dot(tops, low)


def orders(chips):
    bits = list(range(chips.bit_length() - 1))
    return bits, bits[1:] + bits[:1]


def held_and_sent(chips, order):
    if not order:
        return [0], []
    held = [k for k in range(chips) if not (k >> order[0]) & 1]
    return held, [k | (1 << order[0]) for k in held]


def slots(chips):
    places = {}
    for half, order in enumerate(orders(chips)):
        for which, group in enumerate(held_and_sent(chips, order)):
            for position, k in enumerate(group):
                places[k, half] = (2 * half + which, position)
    return places


def pack(band, row, count):
    block, width = band.shape[0], band.shape[1] - TILE
    rows = lax.broadcasted_iota(jnp.int32, (block, TILE), 0) + row
    columns = lax.broadcasted_iota(jnp.int32, (block, TILE), 1)
    last = band[:, width:]
    first = jnp.where(rows > columns, last, band[:, 0:TILE])
    diagonal = jnp.sum(jnp.where(rows == columns, last, 0.0), axis=0, keepdims=True)
    places = lax.broadcasted_iota(jnp.int32, (EXTRA, TILE), 0)
    extra = jnp.where(places == 0, diagonal, jnp.where(places == 1, count, 0.0))
    extra = jnp.concatenate([extra, jnp.zeros((EXTRA, width - TILE), F32)], axis=1)
    packed = jnp.concatenate([first, band[:, TILE:width]], axis=1)
    return packed[0 : block // 2], jnp.concatenate([packed[block // 2 :], extra], axis=0)


def piece_shape(kind, half, block, feat):
    step, width = block // 2, feat // 2
    factor = step + EXTRA * half
    if kind == "factor":
        return factor, width
    if kind == "mixed":
        return step, feat
    return factor + step * (feat // width), width


def store(outs, seeds, group, place, number, first, value):
    output, position = 4 * group + place[0], place[1]
    here = slice(first, first + value.shape[0])
    if seeds:
        value = value + seeds[output][position, number, here, :]
    outs[output][position, number, here, :] = value


def prepare_kernel(routes_ref, counts_ref, acts, out, routes, counts, sems):
    samples, feat = acts.shape
    experts = counts.shape[1]
    copies = [
        pltpu.make_async_copy(routes_ref, routes, sems.at[0]),
        pltpu.make_async_copy(counts_ref, counts, sems.at[1]),
        pltpu.make_async_copy(acts, out.at[pl.ds(0, samples), :], sems.at[2]),
    ]
    for copy in copies:
        copy.start()
    out[samples:, :] = jnp.zeros((out.shape[0] - samples, feat), F32)
    for copy in copies[:2]:
        copy.wait()
    hits = []
    for expert in range(experts):
        same = [jnp.where(routes[k : k + 1, :] == expert, 1.0, 0.0) for k in range(routes.shape[0])]
        hits.append(sum(same[1:], same[0]))
    hit = jnp.concatenate(hits, axis=0)
    first = lax.broadcasted_iota(jnp.int32, (samples, samples), 0)
    second = lax.broadcasted_iota(jnp.int32, (samples, samples), 1)
    rank = dot(hit.astype(BF16), jnp.where(first < second, 1.0, 0.0).astype(BF16))
    per_row = feat // samples
    for expert in range(experts):
        limit = counts[0, expert].astype(F32)
        keep = jnp.where(rank[expert : expert + 1, :] < limit, hits[expert], 0.0)
        row, column = samples + expert // per_row, expert % per_row * samples
        out[row : row + 1, column : column + samples] = keep
    copies[2].wait()


def act_kernel(turns, block, chips, seeded, samples, place, *refs):
    parts, refs = refs[:2], refs[2:]
    refs, (high, low, turned) = refs[:-3], refs[-3:]
    seeds, outs = (refs[: len(refs) // 2], refs[len(refs) // 2 :]) if seeded else ((), refs)
    feat = parts[0].shape[1]
    width = feat // 2 + TILE
    mine, expert = place[0], place[1]
    split_rows(parts, samples, high, low, feat)
    keeps = [keep_row(parts, samples, expert ^ (2 * turn)) for turn in turns]
    places = slots(chips)
    for k in range(chips):
        column, row = band_place(mine ^ (2 * k), block)
        both, tops = weighted(left_rows(parts, samples, turned, column, row, block), keeps)
        total = three(both, tops, high[:, pl.ds(column, width)], low[:, pl.ds(column, width)])
        for number, keep in enumerate(keeps):
            count = jnp.sum(keep, axis=1, keepdims=True)
            packed = pack(total[number * block : (number + 1) * block], row, count)
            for half in range(2):
                store(outs, seeds, 0, places[k, half], number, 0, packed[half])


def grad_kernel(turns, block, chips, seeded, samples, place, *refs):
    grads, acts, refs = refs[:2], refs[2:4], refs[4:]
    refs, (high, low, act_high, act_low, turned) = refs[:-5], refs[-5:]
    seeds, outs = (refs[: len(refs) // 2], refs[len(refs) // 2 :]) if seeded else ((), refs)
    feat = grads[0].shape[1]
    step, width = block // 2, feat // 2
    mine, expert = place[0], place[1]
    split_rows(grads, samples, high, low, feat)
    split_rows(acts, samples, act_high, act_low, feat)
    keeps = [keep_row(acts, samples, expert ^ (2 * turn)) for turn in turns]
    places = slots(chips)
    for k in range(chips):
        column, row = band_place(mine ^ (2 * k), block)
        both, tops = weighted(left_rows(grads, samples, turned, column, row, block), keeps)
        here = pl.ds(column, width + TILE)
        total = three(both, tops, high[:, here], low[:, here])
        mixed = three(both, tops, act_high[...], act_low[...])
        for number in range(len(keeps)):
            packed = pack(total[number * block : (number + 1) * block], row, 0.0)
            for half in range(2):
                spot = places[k, half]
                first = number * block + half * step
                value = mixed[first : first + step]
                if number:
                    store(outs, seeds, 2, spot, number - 1, 0, packed[half])
                    for part in range(feat // width):
                        below = packed[half].shape[0] + part * step
                        columns = slice(part * width, (part + 1) * width)
                        store(outs, seeds, 2, spot, number - 1, below, value[:, columns])
                else:
                    store(outs, seeds, 0, spot, 0, 0, packed[half])
                    store(outs, seeds, 1, spot, 0, 0, value)


def whole_in_vmem(count):
    return [pl.BlockSpec(memory_space=pltpu.VMEM)] * count


def prepare(routes, counts, acts):
    samples, feat = acts.shape
    rows = samples + 8 * -(-counts.shape[1] * samples // (8 * feat))
    return pl.pallas_call(
        prepare_kernel,
        out_shape=jax.ShapeDtypeStruct((rows, feat), F32),
        in_specs=[pl.BlockSpec(memory_space=pltpu.HBM)] * 3,
        out_specs=pl.BlockSpec(memory_space=pltpu.VMEM),
        scratch_shapes=[
            pltpu.VMEM(routes.shape[::-1], jnp.int32),
            pltpu.SMEM(counts.shape, jnp.int32),
            pltpu.SemaphoreType.DMA((3,)),
        ],
        compiler_params=pltpu.CompilerParams(vmem_limit_bytes=60 * MIB),
    )(routes.T, counts, acts)


def bands(body, turns, groups, place, parts, seeds, samples, chips, block):
    feat = parts[0].shape[1]
    extended = pltpu.VMEM((2 * samples, feat + feat // 2), BF16)
    plain = pltpu.VMEM((2 * samples, feat), BF16)
    scratch = [extended, extended] + ([plain, plain] if len(parts) > 2 else [])
    shapes = [
        jax.ShapeDtypeStruct((len(group), count, *piece_shape(kind, half, block, feat)), F32)
        for count, kind in groups
        for half, order in enumerate(orders(chips))
        for group in held_and_sent(chips, order)
    ]
    operands = (*parts, *seeds)
    limit = 36 if len(parts) > 2 else 20
    return pl.pallas_call(
        functools.partial(body, range(turns), block, chips, bool(seeds), samples),
        out_shape=shapes,
        in_specs=[pl.BlockSpec(memory_space=pltpu.SMEM)] + whole_in_vmem(len(operands)),
        out_specs=whole_in_vmem(len(shapes)),
        scratch_shapes=scratch + [pltpu.VMEM((TILE, 2 * samples), F32)],
        compiler_params=pltpu.CompilerParams(vmem_limit_bytes=limit * MIB),
    )(place, *operands)


def unfold(bands, extras, full):
    tiles = full.shape[0] // TILE
    per_tile = extras.shape[0] // EXTRA // tiles
    rows = lax.broadcasted_iota(jnp.int32, (TILE, TILE), 0)
    columns = lax.broadcasted_iota(jnp.int32, (TILE, TILE), 1)

    def put(i, j, value):
        full[i * TILE : (i + 1) * TILE, j * TILE : (j + 1) * TILE] = value

    firsts = [bands[i * TILE : (i + 1) * TILE, 0:TILE] for i in range(tiles)]
    turned = [value.T for value in firsts]
    for i in range(tiles):
        put(i, i, jnp.where(rows <= columns, firsts[i], turned[i]))
        for step in range(1, tiles // 2):
            here = bands[i * TILE : (i + 1) * TILE, step * TILE : (step + 1) * TILE]
            put(i, (i + step) % tiles, here)
            put((i + step) % tiles, i, here.T)
    for i in range(tiles // 2):
        j = i + tiles // 2
        places = [EXTRA * (i * per_tile + owner) for owner in range(per_tile)]
        diagonal = sum(extras[place : place + 1, :] for place in places)
        here = jnp.where(rows > columns, firsts[i], jnp.where(rows < columns, turned[j], diagonal))
        put(i, j, here)
        put(j, i, here.T)


def damping(full):
    size = full.shape[0]
    value = full[...]
    lanes = lax.broadcasted_iota(jnp.int32, (size, size), 1)
    sublanes = lax.broadcasted_iota(jnp.int32, (size, size), 0)
    trace = jnp.sum(jnp.sum(jnp.where(lanes == sublanes, value, 0.0), axis=0, keepdims=True), axis=1, keepdims=True)
    largest = jnp.max(jnp.sum(jnp.abs(value), axis=0, keepdims=True), axis=1, keepdims=True)
    damp = trace * (0.1 / size)
    return damp, 1.0 / (largest + damp)


def times(left, high, low):
    rows = left.shape[0]
    top, rest = split(left)
    first = dot(jnp.concatenate([top, rest], axis=0), high[...])
    return first[0:rows] + first[rows : 2 * rows] + dot(top, low[...])


def gather_order(order):
    offsets = [0]
    for bit in order:
        offsets += [k | (1 << bit) for k in offsets]
    return offsets


def row_pieces(place, block, chips, arrays, extra):
    step = block // 2
    firsts = [(value, first) for value in arrays for first in range(0, value.shape[0], block + extra)]
    pieces, extras = [], []
    for number, (value, first) in enumerate(firsts):
        core, position = number // chips, number % chips
        for half, order in enumerate(orders(chips)):
            owner = place[0] ^ (2 * gather_order(order)[position] + core)
            here = pl.ds(pl.multiple_of(owner * block + half * step, step), step)
            pieces.append((here, value.at[first + half * step : first + (half + 1) * step]))
        if extra:
            here = pl.ds(pl.multiple_of(owner * EXTRA, EXTRA), EXTRA)
            extras.append((here, value.at[first + block : first + block + extra]))
    return pieces, extras


def factor_rows(place, block, blocks, bands, extras, full):
    chips = full.shape[0] // (2 * block)
    pieces, others = row_pieces(place, block, chips, blocks, EXTRA)
    for here, value in pieces:
        bands[here, :] = value[...]
    for here, value in others:
        extras[here, :] = value[:, 0:TILE]
    unfold(bands, extras, full)
    return full[pl.ds(pl.multiple_of(place[0] * block, block), block), :]


def act_factor_kernel(place, *refs):
    blocks, (factor, scales, high, low), (bands, extras, full) = refs[:-7], refs[-7:-3], refs[-3:]
    factor[...] = factor_rows(place, factor.shape[0], blocks, bands, extras, full)
    damp, alpha = damping(full)
    scales[0:1, :] = jnp.broadcast_to(damp, (1, TILE))
    scales[1:2, :] = jnp.broadcast_to(alpha, (1, TILE))
    high[...], low[...] = split(full[...])


def grad_factor_kernel(place, *refs):
    blocks, (factor, inverse), (bands, extras, full, high, low) = refs[:-7], refs[-7:-5], refs[-5:]
    block, feat = factor.shape
    rows = factor_rows(place, block, blocks, bands, extras, full)
    factor[...] = rows
    damp, alpha = damping(full)
    high[...], low[...] = split(full[...])
    lanes = lax.broadcasted_iota(jnp.int32, (block, feat), 1)
    sublanes = lax.broadcasted_iota(jnp.int32, (block, feat), 0)
    unit = jnp.where(lanes == sublanes + place[0] * block, 1.0, 0.0).astype(F32)
    rest_rows = unit - alpha * (rows + damp * unit)
    once = 2.0 * rest_rows - alpha * (times(rest_rows, high, low) + damp * rest_rows)
    inverse[...] = alpha * (unit + rest_rows + once - alpha * (times(once, high, low) + damp * once))


def update_kernel(place, *refs):
    blocks = refs[:-9]
    inverse, scales, act_high, act_low, momentum, weights, moment_out, weight_out, full = refs[-9:]
    block = momentum.shape[0]
    for here, value in row_pieces(place, block, full.shape[0] // (2 * block), blocks, 0)[0]:
        full[here, :] = value[...]
    damp, alpha = scales[0:1, 0:1], scales[1:2, 0:1]
    half_way = times(inverse[...], *split(full[...]))
    value = half_way
    for _ in range(3):
        value = half_way + value - alpha * (times(value, act_high[...], act_low[...]) + damp * value)
    moment = 0.9 * momentum[...] + alpha * value
    moment_out[...] = moment
    weight_out[...] = weights[...] - 0.5 * moment


def on_core(body, place, operands, shapes, scratch, limit):
    return pl.pallas_call(
        body,
        out_shape=shapes,
        in_specs=[pl.BlockSpec(memory_space=pltpu.SMEM)] + whole_in_vmem(len(operands)),
        out_specs=whole_in_vmem(len(shapes)),
        scratch_shapes=scratch,
        compiler_params=pltpu.CompilerParams(vmem_limit_bytes=limit * MIB),
    )(place, *operands)


def factor_scratch(block, feat):
    shapes = [(feat, feat // 2), (EXTRA * feat // block, TILE), (feat, feat)]
    return [pltpu.VMEM(shape, F32) for shape in shapes]


def act_factor_rows(place, blocks, block, feat):
    shapes = [((block, feat), F32), ((8, TILE), F32), ((feat, feat), BF16), ((feat, feat), BF16)]
    shapes = [jax.ShapeDtypeStruct(*shape) for shape in shapes]
    scratch = factor_scratch(block, feat)
    return on_core(act_factor_kernel, place, blocks, shapes, scratch, 32)


def grad_factor_rows(place, blocks, block, feat):
    shapes = [jax.ShapeDtypeStruct((block, feat), F32)] * 2
    scratch = factor_scratch(block, feat)
    scratch += [pltpu.VMEM((feat, feat), BF16)] * 2
    return on_core(grad_factor_kernel, place, blocks, shapes, scratch, 32)


def update_rows(place, blocks, inverse, scales, high, low, momentum, weights):
    block, feat = momentum.shape
    operands = (*blocks, inverse, scales, high, low, momentum, weights)
    shapes = [jax.ShapeDtypeStruct((block, feat), F32)] * 2
    return on_core(update_kernel, place, operands, shapes, [pltpu.VMEM((feat, feat), F32)], 32)


def swap(value, axis, step):
    size = lax.axis_size(axis)
    return lax.ppermute(value, axis, [(i, i ^ step) for i in range(size)])


class PlaneSum:
    def __init__(self, pieces, chips):
        self.steps = [list(order) for order in orders(chips)]
        self.offsets = [held_and_sent(chips, order)[0] for order in self.steps]
        self.held, self.leaving = list(pieces[0::2]), list(pieces[1::2])

    def send(self):
        self.got = [swap(value, "dp", 2 << order[0]) for value, order in zip(self.leaving, self.steps)]

    def add(self):
        self.leaving = []
        for half, order in enumerate(self.steps):
            offsets = self.offsets[half]
            sums = {k: self.held[half][i] + self.got[half][i] for i, k in enumerate(offsets)}
            order.pop(0)
            if order:
                offsets = [k for k in offsets if not (k >> order[0]) & 1]
                self.leaving.append(jnp.stack([sums[k | (1 << order[0])] for k in offsets]))
            self.offsets[half] = offsets
            self.held[half] = [sums[k] for k in offsets]

    def finish(self):
        while self.steps[0]:
            self.send()
            self.add()
        return [held[0] for held in self.held]


def across(far):
    return [swap(far[number], "expert", 2 * (number + 1)) for number in range(far.shape[0])]


class Gather:
    def __init__(self, halves, chips):
        self.chips, self.orders = chips, orders(chips)
        self.halves, self.whole = halves, {}

    def begin(self):
        block = jnp.concatenate(self.halves, axis=0)
        self.whole = {order[0]: swap(block, "dp", 2 << order[0]) for order in self.orders}

    def relay(self):
        first = self.halves[0].shape[0]
        self.held = []
        for half, order in enumerate(self.orders):
            held = [self.halves[half]]
            for bit in order:
                came = [swap(value, "dp", 2 << bit) for value in held[1:]]
                if bit in self.whole:
                    own = self.whole[bit][first:] if half else self.whole[bit][:first]
                else:
                    own = swap(held[0], "dp", 2 << bit)
                held += [own] + came
            self.held.append(held)

    def hold_last(self, value):
        last, value = together([held[-1] for held in self.held], value)
        self.held = [held[:-1] + [block] for held, block in zip(self.held, last)]
        return value

    def exchange(self, first=0, last=None):
        pairs = list(zip(*self.held))[first:last]
        mine = jnp.concatenate([value for pair in pairs for value in pair], axis=0)
        return mine, swap(mine, "dp", 1)


def together(*values):
    return lax.optimization_barrier(values)


def on_device(acts, grads_out, routes, counts, old_act_factor, old_grad_factor, momentum, weights):
    devices, experts = lax.axis_size("dp"), lax.axis_size("expert")
    chips = devices // 2
    samples, feat, block = acts.shape[0], acts.shape[1], weights.shape[1]
    step, width = block // 2, feat // 2
    mine = lax.axis_index("dp")
    place = jnp.stack([mine, lax.axis_index("expert")]).astype(jnp.int32)

    def own_band(old):
        start = mine * block // TILE * TILE
        wide = jnp.concatenate([old[0], old[0][:, 0:width]], axis=1)
        band = lax.dynamic_slice_in_dim(wide, start, width + TILE, 1)
        return [0.5 * half for half in pack(band, mine * block - start, 0.0)]

    turns = experts // 2
    size = (samples, chips, block)
    act_groups = ((turns, "factor"),)
    grad_groups = ((1, "factor"), (1, "mixed"), (turns - 1, "both"))

    acts = prepare(routes, counts, acts)
    acts_far = swap(acts, "expert", 1)
    near_acts = (acts, swap(acts, "dp", 1))
    act_seeds = bands(act_kernel, turns, act_groups, place, near_acts, (), *size)
    grads_far = swap(grads_out, "expert", 1)
    grad_parts = (grads_out, swap(grads_out, "dp", 1)) + near_acts
    grad_seeds = bands(grad_kernel, turns, grad_groups, place, grad_parts, (), *size)
    old_act, old_grad = own_band(old_act_factor), own_band(old_grad_factor)
    early = (act_seeds, grad_seeds, old_act, old_grad)
    acts_far, (act_seeds, grad_seeds, old_act, old_grad) = together(acts_far, early)

    far_acts = (acts_far, swap(acts_far, "dp", 1))
    act_sum = PlaneSum(bands(act_kernel, turns, act_groups, place, far_acts, act_seeds, *size), chips)
    act_sum.send()
    act_sum.add()
    act_sum.send()
    grads_far, _ = together(grads_far, act_sum.leaving)
    grad_parts = (grads_far, swap(grads_far, "dp", 1)) + far_acts
    pieces = bands(grad_kernel, turns, grad_groups, place, grad_parts, grad_seeds, *size)

    grad_sum, mixed_sum, far_sum = [PlaneSum(pieces[first : first + 4], chips) for first in (0, 4, 8)]
    far_sum.send()
    act_sum.got, far_sum.held = together(act_sum.got, far_sum.held)
    act_sum.add()
    act_sums = act_sum.finish()
    act_across = across(jnp.concatenate([value[1:] for value in act_sums], axis=1))
    grad_sum.leaving, far_sum.got = together(grad_sum.leaving, far_sum.got)
    grad_sum.send()
    far_sum.add()
    far_sum.leaving, act_across = together(far_sum.leaving, act_across)
    far_sum.send()
    grad_sum.add()
    mixed_sum.leaving, grad_sum.leaving = together(mixed_sum.leaving, grad_sum.leaving)
    mixed_sum.send()
    grad_sum.send()
    far_sum.add()
    far_sums = far_sum.finish()

    factors = [slice(0, step), slice(step, block + EXTRA)]
    act_totals = [
        sum((there[factors[half]] for there in act_across), value[0]) for half, value in enumerate(act_sums)
    ]
    total = jnp.maximum(act_totals[1][step + 1 : step + 2, 0:1], 1.0)
    act_halves = [old + 0.5 * (value / total) for old, value in zip(old_act, act_totals)]
    sizes = [step, step + EXTRA]
    across_grad = across(jnp.concatenate([value[:, 0:size] for value, size in zip(far_sums, sizes)], axis=1))
    far_mixed = jnp.concatenate(
        [
            jnp.concatenate([value[:, size : size + step], value[:, size + step :]], axis=2)
            for value, size in zip(far_sums, sizes)
        ],
        axis=1,
    )
    grad_sum.add()
    grad_sums = grad_sum.finish()
    mixed_sum.held, across_grad = together(mixed_sum.held, across_grad)
    mixed_sum.add()
    mixed_sum.leaving, far_mixed = together(mixed_sum.leaving, far_mixed)
    mixed_sum.send()
    across_mixed = across(far_mixed)

    def both(near, far, rows):
        return [sum((there[here] for there in far), value[0]) / total for value, here in zip(near, rows)]

    grad_stats = both(grad_sums, across_grad, factors)
    grad_halves = [old + 0.5 * value for old, value in zip(old_grad, grad_stats)]
    grad_gather = Gather(grad_halves, chips)
    grad_gather.begin()
    early = (grad_gather.whole, mixed_sum.got)
    act_halves, (grad_gather.whole, mixed_sum.got) = together(act_halves, early)
    mixed_sum.add()
    mixed_sums = mixed_sum.finish()
    act_gather = Gather(act_halves, chips)
    act_gather.begin()
    grad_gather.relay()
    act_gather.relay()
    across_mixed, _ = together(across_mixed, act_gather.whole)
    mixed_gather = Gather(both(mixed_sums, across_mixed, [slice(0, step), slice(step, block)]), chips)
    mixed_gather.begin()
    mixed_gather.whole = act_gather.hold_last(mixed_gather.whole)
    mixed_gather.relay()
    mine, theirs = mixed_gather.exchange(0, -1)
    act_out, *act_square = act_factor_rows(place, act_gather.exchange(), block, feat)
    grad_blocks, act_square = together(grad_gather.exchange(), act_square)
    grad_out, inverse = grad_factor_rows(place, grad_blocks, block, feat)
    inverse = mixed_gather.hold_last(inverse)
    my_last, their_last = mixed_gather.exchange(-1)
    mixed_blocks = (mine, my_last, theirs, their_last)
    outs = update_rows(place, mixed_blocks, inverse, *act_square, momentum[0], weights[0])
    return tuple(out[None] for out in (act_out, grad_out, *outs))


def solution(mesh):
    rows = P(("dp", "expert"), None)
    matrix = P("expert", "dp", None)
    return jax.shard_map(
        on_device,
        mesh=mesh,
        in_specs=(rows,) * 4 + (matrix,) * 4,
        out_specs=(matrix,) * 4,
        check_vma=False,
    )
```

```python
import functools

import jax
import jax.numpy as jnp
from jax import lax
from jax.experimental import pallas as pl
from jax.experimental.pallas import tpu as pltpu
from jax.sharding import PartitionSpec as P

F32 = jnp.float32
BF16 = jnp.bfloat16
TILE = 128
EXTRA = 8
MIB = 1024 * 1024


def split(value):
    high = value.astype(BF16)
    return high, (value - high.astype(F32)).astype(BF16)


def dot(left, right):
    return jnp.dot(left, right, preferred_element_type=F32)


def band_place(owner, block):
    per_tile = TILE // block
    if per_tile == 1:
        return pl.multiple_of(owner * TILE, TILE), 0
    return (
        pl.multiple_of(lax.div(owner, per_tile) * TILE, TILE),
        pl.multiple_of(lax.rem(owner, per_tile) * block, block),
    )


def split_rows(parts, samples, high, low, feat):
    extra = high.shape[1] - feat
    for number, part in enumerate(parts):
        here = slice(number * samples, (number + 1) * samples)
        top, rest = split(part[0:samples, :])
        high[here, 0:feat] = top
        low[here, 0:feat] = rest
        if extra:
            high[here, feat : feat + extra] = top[:, 0:extra]
            low[here, feat : feat + extra] = rest[:, 0:extra]


def left_rows(parts, samples, turned, column, row, block):
    for number, part in enumerate(parts):
        here = slice(number * samples, (number + 1) * samples)
        turned[:, here] = part[0:samples, pl.ds(column, TILE)].T
    return turned[pl.ds(row, block), :]


def keep_place(expert, samples, feat):
    per_row = feat // samples
    return lax.div(expert, per_row), pl.multiple_of(lax.rem(expert, per_row) * samples, TILE)


def keep_row(parts, samples, expert):
    row, column = keep_place(expert, samples, parts[0].shape[1])
    return jnp.concatenate([part[pl.ds(samples + row, 1), pl.ds(column, samples)] for part in parts], axis=1)


def weighted(rows, keeps):
    halves = [split(rows * keep) for keep in keeps]
    tops = [half[0] for half in halves]
    return jnp.concatenate(tops + [half[1] for half in halves], axis=0), jnp.concatenate(tops, axis=0)


def three(both, tops, high, low):
    half = tops.shape[0]
    first = dot(both, high)
    return first[0:half] + first[half : 2 * half] + dot(tops, low)


def orders(chips):
    bits = list(range(chips.bit_length() - 1))
    return bits, bits[1:] + bits[:1]


def held_and_sent(chips, order):
    if not order:
        return [0], []
    held = [k for k in range(chips) if not (k >> order[0]) & 1]
    return held, [k | (1 << order[0]) for k in held]


def slots(chips):
    places = {}
    for half, order in enumerate(orders(chips)):
        for which, group in enumerate(held_and_sent(chips, order)):
            for position, k in enumerate(group):
                places[k, half] = (2 * half + which, position)
    return places


def pack(band, row, count):
    block, width = band.shape[0], band.shape[1] - TILE
    rows = lax.broadcasted_iota(jnp.int32, (block, TILE), 0) + row
    columns = lax.broadcasted_iota(jnp.int32, (block, TILE), 1)
    last = band[:, width:]
    first = jnp.where(rows > columns, last, band[:, 0:TILE])
    diagonal = jnp.sum(jnp.where(rows == columns, last, 0.0), axis=0, keepdims=True)
    places = lax.broadcasted_iota(jnp.int32, (EXTRA, TILE), 0)
    extra = jnp.where(places == 0, diagonal, jnp.where(places == 1, count, 0.0))
    extra = jnp.concatenate([extra, jnp.zeros((EXTRA, width - TILE), F32)], axis=1)
    packed = jnp.concatenate([first, band[:, TILE:width]], axis=1)
    return packed[0 : block // 2], jnp.concatenate([packed[block // 2 :], extra], axis=0)


def piece_shape(kind, half, block, feat):
    step, width = block // 2, feat // 2
    factor = step + EXTRA * half
    if kind == "factor":
        return factor, width
    if kind == "mixed":
        return step, feat
    return factor + step * (feat // width), width


def store(outs, seeds, group, place, number, first, value):
    output, position = 4 * group + place[0], place[1]
    here = slice(first, first + value.shape[0])
    if seeds:
        value = value + seeds[output][position, number, here, :]
    outs[output][position, number, here, :] = value


def prepare_kernel(routes_ref, counts_ref, acts, out, routes, counts, keeps, sems):
    samples, feat = acts.shape
    experts = counts.shape[1]
    copies = [
        pltpu.make_async_copy(acts, out.at[pl.ds(0, samples), :], sems.at[0]),
        pltpu.make_async_copy(routes_ref, routes, sems.at[1]),
        pltpu.make_async_copy(counts_ref, counts, sems.at[2]),
    ]
    for copy in copies:
        copy.start()
    keeps[...] = jnp.zeros(keeps.shape, F32)
    for copy in copies[1:]:
        copy.wait()
    hits = []
    for expert in range(experts):
        same = [jnp.where(routes[k : k + 1, :] == expert, 1.0, 0.0) for k in range(routes.shape[0])]
        hits.append(sum(same[1:], same[0]))
    hit = jnp.concatenate(hits, axis=0)
    first = lax.broadcasted_iota(jnp.int32, (samples, samples), 0)
    second = lax.broadcasted_iota(jnp.int32, (samples, samples), 1)
    rank = dot(hit.astype(BF16), jnp.where(first < second, 1.0, 0.0).astype(BF16))
    per_row = feat // samples
    for expert in range(experts):
        limit = counts[0, expert].astype(F32)
        keep = jnp.where(rank[expert : expert + 1, :] < limit, hits[expert], 0.0)
        row, column = expert // per_row, expert % per_row * samples
        keeps[row : row + 1, column : column + samples] = keep
    last = pltpu.make_async_copy(keeps, out.at[pl.ds(samples, keeps.shape[0]), :], sems.at[3])
    last.start()
    last.wait()
    copies[0].wait()


def act_kernel(turns, block, chips, seeded, samples, place, *refs):
    parts, refs = refs[:2], refs[2:]
    refs, (high, low, turned) = refs[:-3], refs[-3:]
    seeds, outs = (refs[: len(refs) // 2], refs[len(refs) // 2 :]) if seeded else ((), refs)
    feat = parts[0].shape[1]
    width = feat // 2 + TILE
    mine, expert = place[0], place[1]
    split_rows(parts, samples, high, low, feat)
    keeps = [keep_row(parts, samples, expert ^ (2 * turn)) for turn in turns]
    places = slots(chips)
    for k in range(chips):
        column, row = band_place(mine ^ (2 * k), block)
        both, tops = weighted(left_rows(parts, samples, turned, column, row, block), keeps)
        total = three(both, tops, high[:, pl.ds(column, width)], low[:, pl.ds(column, width)])
        for number, keep in enumerate(keeps):
            count = jnp.sum(keep, axis=1, keepdims=True)
            packed = pack(total[number * block : (number + 1) * block], row, count)
            for half in range(2):
                store(outs, seeds, 0, places[k, half], number, 0, packed[half])


def grad_kernel(turns, block, chips, seeded, samples, place, *refs):
    grads, acts, refs = refs[:2], refs[2:4], refs[4:]
    refs, (high, low, act_high, act_low, turned) = refs[:-5], refs[-5:]
    seeds, outs = (refs[: len(refs) // 2], refs[len(refs) // 2 :]) if seeded else ((), refs)
    feat = grads[0].shape[1]
    step, width = block // 2, feat // 2
    mine, expert = place[0], place[1]
    split_rows(grads, samples, high, low, feat)
    split_rows(acts, samples, act_high, act_low, feat)
    keeps = [keep_row(acts, samples, expert ^ (2 * turn)) for turn in turns]
    places = slots(chips)
    for k in range(chips):
        column, row = band_place(mine ^ (2 * k), block)
        both, tops = weighted(left_rows(grads, samples, turned, column, row, block), keeps)
        here = pl.ds(column, width + TILE)
        total = three(both, tops, high[:, here], low[:, here])
        mixed = three(both, tops, act_high[...], act_low[...])
        for number in range(len(keeps)):
            packed = pack(total[number * block : (number + 1) * block], row, 0.0)
            for half in range(2):
                spot = places[k, half]
                first = number * block + half * step
                value = mixed[first : first + step]
                if number:
                    store(outs, seeds, 2, spot, number - 1, 0, packed[half])
                    for part in range(feat // width):
                        below = packed[half].shape[0] + part * step
                        columns = slice(part * width, (part + 1) * width)
                        store(outs, seeds, 2, spot, number - 1, below, value[:, columns])
                else:
                    store(outs, seeds, 0, spot, 0, 0, packed[half])
                    store(outs, seeds, 1, spot, 0, 0, value)


def whole_in_vmem(count):
    return [pl.BlockSpec(memory_space=pltpu.VMEM)] * count


def prepare(routes, counts, acts):
    samples, feat = acts.shape
    rows = samples + 8 * -(-counts.shape[1] * samples // (8 * feat))
    return pl.pallas_call(
        prepare_kernel,
        out_shape=jax.ShapeDtypeStruct((rows, feat), F32),
        in_specs=[pl.BlockSpec(memory_space=pltpu.HBM)] * 3,
        out_specs=pl.BlockSpec(memory_space=pltpu.HBM),
        scratch_shapes=[
            pltpu.VMEM(routes.shape[::-1], jnp.int32),
            pltpu.SMEM(counts.shape, jnp.int32),
            pltpu.VMEM((rows - samples, feat), F32),
            pltpu.SemaphoreType.DMA((4,)),
        ],
        compiler_params=pltpu.CompilerParams(vmem_limit_bytes=60 * MIB),
    )(routes.T, counts, acts)


def bands(body, turns, groups, place, parts, seeds, samples, chips, block):
    feat = parts[0].shape[1]
    extended = pltpu.VMEM((2 * samples, feat + feat // 2), BF16)
    plain = pltpu.VMEM((2 * samples, feat), BF16)
    scratch = [extended, extended] + ([plain, plain] if len(parts) > 2 else [])
    shapes = [
        jax.ShapeDtypeStruct((len(group), count, *piece_shape(kind, half, block, feat)), F32)
        for count, kind in groups
        for half, order in enumerate(orders(chips))
        for group in held_and_sent(chips, order)
    ]
    operands = (*parts, *seeds)
    limit = 36 if len(parts) > 2 else 20
    return pl.pallas_call(
        functools.partial(body, range(turns), block, chips, bool(seeds), samples),
        out_shape=shapes,
        in_specs=[pl.BlockSpec(memory_space=pltpu.SMEM)] + whole_in_vmem(len(operands)),
        out_specs=whole_in_vmem(len(shapes)),
        scratch_shapes=scratch + [pltpu.VMEM((TILE, 2 * samples), F32)],
        compiler_params=pltpu.CompilerParams(vmem_limit_bytes=limit * MIB),
    )(place, *operands)


def unfold(bands, extras, full):
    tiles = full.shape[0] // TILE
    per_tile = extras.shape[0] // EXTRA // tiles
    rows = lax.broadcasted_iota(jnp.int32, (TILE, TILE), 0)
    columns = lax.broadcasted_iota(jnp.int32, (TILE, TILE), 1)

    def put(i, j, value):
        full[i * TILE : (i + 1) * TILE, j * TILE : (j + 1) * TILE] = value

    firsts = [bands[i * TILE : (i + 1) * TILE, 0:TILE] for i in range(tiles)]
    turned = [value.T for value in firsts]
    for i in range(tiles):
        put(i, i, jnp.where(rows <= columns, firsts[i], turned[i]))
        for step in range(1, tiles // 2):
            here = bands[i * TILE : (i + 1) * TILE, step * TILE : (step + 1) * TILE]
            put(i, (i + step) % tiles, here)
            put((i + step) % tiles, i, here.T)
    for i in range(tiles // 2):
        j = i + tiles // 2
        places = [EXTRA * (i * per_tile + owner) for owner in range(per_tile)]
        diagonal = sum(extras[place : place + 1, :] for place in places)
        here = jnp.where(rows > columns, firsts[i], jnp.where(rows < columns, turned[j], diagonal))
        put(i, j, here)
        put(j, i, here.T)


def damping(full):
    size = full.shape[0]
    value = full[...]
    lanes = lax.broadcasted_iota(jnp.int32, (size, size), 1)
    sublanes = lax.broadcasted_iota(jnp.int32, (size, size), 0)
    trace = jnp.sum(jnp.sum(jnp.where(lanes == sublanes, value, 0.0), axis=0, keepdims=True), axis=1, keepdims=True)
    largest = jnp.max(jnp.sum(jnp.abs(value), axis=0, keepdims=True), axis=1, keepdims=True)
    damp = trace * (0.1 / size)
    return damp, 1.0 / (largest + damp)


def times(left, high, low):
    rows = left.shape[0]
    top, rest = split(left)
    first = dot(jnp.concatenate([top, rest], axis=0), high[...])
    return first[0:rows] + first[rows : 2 * rows] + dot(top, low[...])


def gather_order(order):
    offsets = [0]
    for bit in order:
        offsets += [k | (1 << bit) for k in offsets]
    return offsets


def row_pieces(place, block, chips, arrays, extra):
    step = block // 2
    firsts = [(value, first) for value in arrays for first in range(0, value.shape[0], block + extra)]
    pieces, extras = [], []
    for number, (value, first) in enumerate(firsts):
        core, position = number // chips, number % chips
        for half, order in enumerate(orders(chips)):
            owner = place[0] ^ (2 * gather_order(order)[position] + core)
            here = pl.ds(pl.multiple_of(owner * block + half * step, step), step)
            pieces.append((here, value.at[first + half * step : first + (half + 1) * step]))
        if extra:
            here = pl.ds(pl.multiple_of(owner * EXTRA, EXTRA), EXTRA)
            extras.append((here, value.at[first + block : first + block + extra]))
    return pieces, extras


def factor_rows(place, block, blocks, bands, extras, full):
    chips = full.shape[0] // (2 * block)
    pieces, others = row_pieces(place, block, chips, blocks, EXTRA)
    for here, value in pieces:
        bands[here, :] = value[...]
    for here, value in others:
        extras[here, :] = value[:, 0:TILE]
    unfold(bands, extras, full)
    return full[pl.ds(pl.multiple_of(place[0] * block, block), block), :]


def act_factor_kernel(place, *refs):
    blocks, (factor, scales, high, low), (bands, extras, full) = refs[:-7], refs[-7:-3], refs[-3:]
    factor[...] = factor_rows(place, factor.shape[0], blocks, bands, extras, full)
    damp, alpha = damping(full)
    scales[0:1, :] = jnp.broadcast_to(damp, (1, TILE))
    scales[1:2, :] = jnp.broadcast_to(alpha, (1, TILE))
    high[...], low[...] = split(full[...])


def grad_factor_kernel(place, *refs):
    blocks, (factor, inverse), (bands, extras, full, high, low) = refs[:-7], refs[-7:-5], refs[-5:]
    block, feat = factor.shape
    rows = factor_rows(place, block, blocks, bands, extras, full)
    factor[...] = rows
    damp, alpha = damping(full)
    high[...], low[...] = split(full[...])
    lanes = lax.broadcasted_iota(jnp.int32, (block, feat), 1)
    sublanes = lax.broadcasted_iota(jnp.int32, (block, feat), 0)
    unit = jnp.where(lanes == sublanes + place[0] * block, 1.0, 0.0).astype(F32)
    rest_rows = unit - alpha * (rows + damp * unit)
    once = 2.0 * rest_rows - alpha * (times(rest_rows, high, low) + damp * rest_rows)
    inverse[...] = alpha * (unit + rest_rows + once - alpha * (times(once, high, low) + damp * once))


def update_kernel(place, *refs):
    blocks = refs[:-9]
    inverse, scales, act_high, act_low, momentum, weights, moment_out, weight_out, full = refs[-9:]
    block = momentum.shape[0]
    for here, value in row_pieces(place, block, full.shape[0] // (2 * block), blocks, 0)[0]:
        full[here, :] = value[...]
    damp, alpha = scales[0:1, 0:1], scales[1:2, 0:1]
    half_way = times(inverse[...], *split(full[...]))
    value = half_way
    for _ in range(3):
        value = half_way + value - alpha * (times(value, act_high[...], act_low[...]) + damp * value)
    moment = 0.9 * momentum[...] + alpha * value
    moment_out[...] = moment
    weight_out[...] = weights[...] - 0.5 * moment


def on_core(body, place, operands, shapes, scratch, limit):
    return pl.pallas_call(
        body,
        out_shape=shapes,
        in_specs=[pl.BlockSpec(memory_space=pltpu.SMEM)] + whole_in_vmem(len(operands)),
        out_specs=whole_in_vmem(len(shapes)),
        scratch_shapes=scratch,
        compiler_params=pltpu.CompilerParams(vmem_limit_bytes=limit * MIB),
    )(place, *operands)


def factor_scratch(block, feat):
    shapes = [(feat, feat // 2), (EXTRA * feat // block, TILE), (feat, feat)]
    return [pltpu.VMEM(shape, F32) for shape in shapes]


def act_factor_rows(place, blocks, block, feat):
    shapes = [((block, feat), F32), ((8, TILE), F32), ((feat, feat), BF16), ((feat, feat), BF16)]
    shapes = [jax.ShapeDtypeStruct(*shape) for shape in shapes]
    scratch = factor_scratch(block, feat)
    return on_core(act_factor_kernel, place, blocks, shapes, scratch, 32)


def grad_factor_rows(place, blocks, block, feat):
    shapes = [jax.ShapeDtypeStruct((block, feat), F32)] * 2
    scratch = factor_scratch(block, feat)
    scratch += [pltpu.VMEM((feat, feat), BF16)] * 2
    return on_core(grad_factor_kernel, place, blocks, shapes, scratch, 32)


def update_rows(place, blocks, inverse, scales, high, low, momentum, weights):
    block, feat = momentum.shape
    operands = (*blocks, inverse, scales, high, low, momentum, weights)
    shapes = [jax.ShapeDtypeStruct((block, feat), F32)] * 2
    return on_core(update_kernel, place, operands, shapes, [pltpu.VMEM((feat, feat), F32)], 32)


def swap(value, axis, step):
    size = lax.axis_size(axis)
    return lax.ppermute(value, axis, [(i, i ^ step) for i in range(size)])


class PlaneSum:
    def __init__(self, pieces, chips):
        self.steps = [list(order) for order in orders(chips)]
        self.offsets = [held_and_sent(chips, order)[0] for order in self.steps]
        self.held, self.leaving = list(pieces[0::2]), list(pieces[1::2])

    def send(self):
        self.got = [swap(value, "dp", 2 << order[0]) for value, order in zip(self.leaving, self.steps)]

    def add(self):
        self.leaving = []
        for half, order in enumerate(self.steps):
            offsets = self.offsets[half]
            sums = {k: self.held[half][i] + self.got[half][i] for i, k in enumerate(offsets)}
            order.pop(0)
            if order:
                offsets = [k for k in offsets if not (k >> order[0]) & 1]
                self.leaving.append(jnp.stack([sums[k | (1 << order[0])] for k in offsets]))
            self.offsets[half] = offsets
            self.held[half] = [sums[k] for k in offsets]

    def finish(self):
        while self.steps[0]:
            self.send()
            self.add()
        return [held[0] for held in self.held]


def across(far):
    return [swap(far[number], "expert", 2 * (number + 1)) for number in range(far.shape[0])]


class Gather:
    def __init__(self, halves, chips):
        self.chips, self.orders = chips, orders(chips)
        self.halves, self.whole = halves, {}

    def begin(self):
        block = jnp.concatenate(self.halves, axis=0)
        self.whole = {order[0]: swap(block, "dp", 2 << order[0]) for order in self.orders}

    def relay(self):
        first = self.halves[0].shape[0]
        self.held = []
        for half, order in enumerate(self.orders):
            held = [self.halves[half]]
            for bit in order:
                came = [swap(value, "dp", 2 << bit) for value in held[1:]]
                if bit in self.whole:
                    own = self.whole[bit][first:] if half else self.whole[bit][:first]
                else:
                    own = swap(held[0], "dp", 2 << bit)
                held += [own] + came
            self.held.append(held)

    def hold_last(self, value):
        last, value = together([held[-1] for held in self.held], value)
        self.held = [held[:-1] + [block] for held, block in zip(self.held, last)]
        return value

    def exchange(self, first=0, last=None):
        pairs = list(zip(*self.held))[first:last]
        mine = jnp.concatenate([value for pair in pairs for value in pair], axis=0)
        return mine, swap(mine, "dp", 1)


def together(*values):
    return lax.optimization_barrier(values)


def on_device(acts, grads_out, routes, counts, old_act_factor, old_grad_factor, momentum, weights):
    devices, experts = lax.axis_size("dp"), lax.axis_size("expert")
    chips = devices // 2
    samples, feat, block = acts.shape[0], acts.shape[1], weights.shape[1]
    step, width = block // 2, feat // 2
    mine = lax.axis_index("dp")
    place = jnp.stack([mine, lax.axis_index("expert")]).astype(jnp.int32)

    def own_band(old):
        start = mine * block // TILE * TILE
        wide = jnp.concatenate([old[0], old[0][:, 0:width]], axis=1)
        band = lax.dynamic_slice_in_dim(wide, start, width + TILE, 1)
        return [0.5 * half for half in pack(band, mine * block - start, 0.0)]

    turns = experts // 2
    size = (samples, chips, block)
    act_groups = ((turns, "factor"),)
    grad_groups = ((1, "factor"), (1, "mixed"), (turns - 1, "both"))

    acts = prepare(routes, counts, acts)
    acts_far = swap(acts, "expert", 1)
    near_acts = (acts, swap(acts, "dp", 1))
    act_seeds = bands(act_kernel, turns, act_groups, place, near_acts, (), *size)
    grads_far = swap(grads_out, "expert", 1)
    grad_parts = (grads_out, swap(grads_out, "dp", 1)) + near_acts
    grad_seeds = bands(grad_kernel, turns, grad_groups, place, grad_parts, (), *size)
    old_act, old_grad = own_band(old_act_factor), own_band(old_grad_factor)
    early = (act_seeds, grad_seeds, old_act, old_grad)
    acts_far, (act_seeds, grad_seeds, old_act, old_grad) = together(acts_far, early)

    far_acts = (acts_far, swap(acts_far, "dp", 1))
    act_sum = PlaneSum(bands(act_kernel, turns, act_groups, place, far_acts, act_seeds, *size), chips)
    act_sum.send()
    act_sum.add()
    act_sum.send()
    grads_far, _ = together(grads_far, act_sum.leaving)
    grad_parts = (grads_far, swap(grads_far, "dp", 1)) + far_acts
    pieces = bands(grad_kernel, turns, grad_groups, place, grad_parts, grad_seeds, *size)

    grad_sum, mixed_sum, far_sum = [PlaneSum(pieces[first : first + 4], chips) for first in (0, 4, 8)]
    far_sum.send()
    act_sum.got, far_sum.held = together(act_sum.got, far_sum.held)
    act_sum.add()
    act_sums = act_sum.finish()
    act_across = across(jnp.concatenate([value[1:] for value in act_sums], axis=1))
    grad_sum.leaving, far_sum.got = together(grad_sum.leaving, far_sum.got)
    grad_sum.send()
    far_sum.add()
    far_sum.leaving, act_across = together(far_sum.leaving, act_across)
    far_sum.send()
    grad_sum.add()
    mixed_sum.leaving, grad_sum.leaving = together(mixed_sum.leaving, grad_sum.leaving)
    mixed_sum.send()
    grad_sum.send()
    far_sum.add()
    far_sums = far_sum.finish()

    factors = [slice(0, step), slice(step, block + EXTRA)]
    act_totals = [
        sum((there[factors[half]] for there in act_across), value[0]) for half, value in enumerate(act_sums)
    ]
    total = jnp.maximum(act_totals[1][step + 1 : step + 2, 0:1], 1.0)
    act_halves = [old + 0.5 * (value / total) for old, value in zip(old_act, act_totals)]
    sizes = [step, step + EXTRA]
    across_grad = across(jnp.concatenate([value[:, 0:size] for value, size in zip(far_sums, sizes)], axis=1))
    far_mixed = jnp.concatenate(
        [
            jnp.concatenate([value[:, size : size + step], value[:, size + step :]], axis=2)
            for value, size in zip(far_sums, sizes)
        ],
        axis=1,
    )
    grad_sum.add()
    grad_sums = grad_sum.finish()
    mixed_sum.held, across_grad = together(mixed_sum.held, across_grad)
    mixed_sum.add()
    mixed_sum.leaving, far_mixed = together(mixed_sum.leaving, far_mixed)
    mixed_sum.send()
    across_mixed = across(far_mixed)

    def both(near, far, rows):
        return [sum((there[here] for there in far), value[0]) / total for value, here in zip(near, rows)]

    grad_stats = both(grad_sums, across_grad, factors)
    grad_halves = [old + 0.5 * value for old, value in zip(old_grad, grad_stats)]
    grad_gather = Gather(grad_halves, chips)
    grad_gather.begin()
    early = (grad_gather.whole, mixed_sum.got)
    act_halves, (grad_gather.whole, mixed_sum.got) = together(act_halves, early)
    mixed_sum.add()
    mixed_sums = mixed_sum.finish()
    act_gather = Gather(act_halves, chips)
    act_gather.begin()
    grad_gather.relay()
    act_gather.relay()
    across_mixed, _ = together(across_mixed, act_gather.whole)
    mixed_gather = Gather(both(mixed_sums, across_mixed, [slice(0, step), slice(step, block)]), chips)
    mixed_gather.begin()
    grad_out, inverse = grad_factor_rows(place, grad_gather.exchange(), block, feat)
    inverse = act_gather.hold_last(inverse)
    mixed_gather.whole = act_gather.hold_last(mixed_gather.whole)
    mixed_gather.relay()
    mine, theirs = mixed_gather.exchange(0, -1)
    act_out, *act_square = act_factor_rows(place, act_gather.exchange(), block, feat)
    act_square = mixed_gather.hold_last(act_square)
    my_last, their_last = mixed_gather.exchange(-1)
    mixed_blocks = (mine, my_last, theirs, their_last)
    outs = update_rows(place, mixed_blocks, inverse, *act_square, momentum[0], weights[0])
    return tuple(out[None] for out in (act_out, grad_out, *outs))


def solution(mesh):
    rows = P(("dp", "expert"), None)
    matrix = P("expert", "dp", None)
    return jax.shard_map(
        on_device,
        mesh=mesh,
        in_specs=(rows,) * 4 + (matrix,) * 4,
        out_specs=(matrix,) * 4,
        check_vma=False,
    )
```

```python
import functools

import jax
import jax.numpy as jnp
from jax import lax
from jax.experimental import pallas as pl
from jax.experimental.pallas import tpu as pltpu
from jax.sharding import PartitionSpec as P

F32 = jnp.float32
BF16 = jnp.bfloat16
TILE = 128
EXTRA = 8
MIB = 1024 * 1024


def split(value):
    high = value.astype(BF16)
    return high, (value - high.astype(F32)).astype(BF16)


def dot(left, right):
    return jnp.dot(left, right, preferred_element_type=F32)


def band_place(owner, block):
    per_tile = TILE // block
    if per_tile == 1:
        return pl.multiple_of(owner * TILE, TILE), 0
    return (
        pl.multiple_of(lax.div(owner, per_tile) * TILE, TILE),
        pl.multiple_of(lax.rem(owner, per_tile) * block, block),
    )


def split_rows(parts, samples, high, low, feat):
    extra = high.shape[1] - feat
    for number, part in enumerate(parts):
        here = slice(number * samples, (number + 1) * samples)
        top, rest = split(part[0:samples, :])
        high[here, 0:feat] = top
        low[here, 0:feat] = rest
        if extra:
            high[here, feat : feat + extra] = top[:, 0:extra]
            low[here, feat : feat + extra] = rest[:, 0:extra]


def left_rows(parts, samples, turned, column, row, block):
    for number, part in enumerate(parts):
        here = slice(number * samples, (number + 1) * samples)
        turned[:, here] = part[0:samples, pl.ds(column, TILE)].T
    return turned[pl.ds(row, block), :]


def keep_place(expert, samples, feat):
    per_row = feat // samples
    return lax.div(expert, per_row), pl.multiple_of(lax.rem(expert, per_row) * samples, TILE)


def keep_row(parts, samples, expert):
    row, column = keep_place(expert, samples, parts[0].shape[1])
    return jnp.concatenate([part[pl.ds(samples + row, 1), pl.ds(column, samples)] for part in parts], axis=1)


def weighted(rows, keeps):
    halves = [split(rows * keep) for keep in keeps]
    tops = [half[0] for half in halves]
    return jnp.concatenate(tops + [half[1] for half in halves], axis=0), jnp.concatenate(tops, axis=0)


def three(both, tops, high, low):
    half = tops.shape[0]
    first = dot(both, high)
    return first[0:half] + first[half : 2 * half] + dot(tops, low)


def orders(chips):
    bits = list(range(chips.bit_length() - 1))
    return bits, bits[1:] + bits[:1]


def held_and_sent(chips, order):
    if not order:
        return [0], []
    held = [k for k in range(chips) if not (k >> order[0]) & 1]
    return held, [k | (1 << order[0]) for k in held]


def slots(chips):
    places = {}
    for half, order in enumerate(orders(chips)):
        for which, group in enumerate(held_and_sent(chips, order)):
            for position, k in enumerate(group):
                places[k, half] = (2 * half + which, position)
    return places


def pack(band, row, count):
    block, width = band.shape[0], band.shape[1] - TILE
    rows = lax.broadcasted_iota(jnp.int32, (block, TILE), 0) + row
    columns = lax.broadcasted_iota(jnp.int32, (block, TILE), 1)
    last = band[:, width:]
    first = jnp.where(rows > columns, last, band[:, 0:TILE])
    diagonal = jnp.sum(jnp.where(rows == columns, last, 0.0), axis=0, keepdims=True)
    places = lax.broadcasted_iota(jnp.int32, (EXTRA, TILE), 0)
    extra = jnp.where(places == 0, diagonal, jnp.where(places == 1, count, 0.0))
    extra = jnp.concatenate([extra, jnp.zeros((EXTRA, width - TILE), F32)], axis=1)
    packed = jnp.concatenate([first, band[:, TILE:width]], axis=1)
    return packed[0 : block // 2], jnp.concatenate([packed[block // 2 :], extra], axis=0)


def piece_shape(kind, half, block, feat):
    step, width = block // 2, feat // 2
    factor = step + EXTRA * half
    if kind == "factor":
        return factor, width
    if kind == "mixed":
        return step, feat
    return factor + step * (feat // width), width


def store(outs, seeds, group, place, number, first, value):
    output, position = 4 * group + place[0], place[1]
    here = slice(first, first + value.shape[0])
    if seeds:
        value = value + seeds[output][position, number, here, :]
    outs[output][position, number, here, :] = value


def prepare_kernel(routes_ref, counts_ref, acts, out, routes, counts, staged, sems):
    samples, feat = acts.shape
    experts = counts.shape[1]
    pieces = [pl.ds(first, samples // 4) for first in range(0, samples, samples // 4)]
    small = [
        pltpu.make_async_copy(routes_ref, routes, sems.at[0]),
        pltpu.make_async_copy(counts_ref, counts, sems.at[1]),
    ]
    reads = [
        pltpu.make_async_copy(acts.at[here, :], staged.at[here, :], sems.at[2 + number])
        for number, here in enumerate(pieces)
    ]
    writes = [
        pltpu.make_async_copy(staged.at[here, :], out.at[here, :], sems.at[6 + number])
        for number, here in enumerate(pieces)
    ]
    for copy in small + reads:
        copy.start()
    staged[samples:, :] = jnp.zeros((out.shape[0] - samples, feat), F32)
    for read, write in zip(reads, writes):
        read.wait()
        write.start()
    for copy in small:
        copy.wait()
    hits = []
    for expert in range(experts):
        same = [jnp.where(routes[k : k + 1, :] == expert, 1.0, 0.0) for k in range(routes.shape[0])]
        hits.append(sum(same[1:], same[0]))
    hit = jnp.concatenate(hits, axis=0)
    first = lax.broadcasted_iota(jnp.int32, (samples, samples), 0)
    second = lax.broadcasted_iota(jnp.int32, (samples, samples), 1)
    rank = dot(hit.astype(BF16), jnp.where(first < second, 1.0, 0.0).astype(BF16))
    per_row = feat // samples
    for expert in range(experts):
        limit = counts[0, expert].astype(F32)
        keep = jnp.where(rank[expert : expert + 1, :] < limit, hits[expert], 0.0)
        row, column = samples + expert // per_row, expert % per_row * samples
        staged[row : row + 1, column : column + samples] = keep
    last = pl.ds(samples, out.shape[0] - samples)
    writes.append(pltpu.make_async_copy(staged.at[last, :], out.at[last, :], sems.at[10]))
    writes[-1].start()
    for write in writes:
        write.wait()


def act_kernel(turns, block, chips, seeded, samples, place, *refs):
    parts, refs = refs[:2], refs[2:]
    refs, (high, low, turned) = refs[:-3], refs[-3:]
    seeds, outs = (refs[: len(refs) // 2], refs[len(refs) // 2 :]) if seeded else ((), refs)
    feat = parts[0].shape[1]
    width = feat // 2 + TILE
    mine, expert = place[0], place[1]
    split_rows(parts, samples, high, low, feat)
    keeps = [keep_row(parts, samples, expert ^ (2 * turn)) for turn in turns]
    places = slots(chips)
    for k in range(chips):
        column, row = band_place(mine ^ (2 * k), block)
        both, tops = weighted(left_rows(parts, samples, turned, column, row, block), keeps)
        total = three(both, tops, high[:, pl.ds(column, width)], low[:, pl.ds(column, width)])
        for number, keep in enumerate(keeps):
            count = jnp.sum(keep, axis=1, keepdims=True)
            packed = pack(total[number * block : (number + 1) * block], row, count)
            for half in range(2):
                store(outs, seeds, 0, places[k, half], number, 0, packed[half])


def grad_kernel(turns, block, chips, seeded, samples, place, *refs):
    grads, acts, refs = refs[:2], refs[2:4], refs[4:]
    refs, (high, low, act_high, act_low, turned) = refs[:-5], refs[-5:]
    seeds, outs = (refs[: len(refs) // 2], refs[len(refs) // 2 :]) if seeded else ((), refs)
    feat = grads[0].shape[1]
    step, width = block // 2, feat // 2
    mine, expert = place[0], place[1]
    split_rows(grads, samples, high, low, feat)
    split_rows(acts, samples, act_high, act_low, feat)
    keeps = [keep_row(acts, samples, expert ^ (2 * turn)) for turn in turns]
    places = slots(chips)
    for k in range(chips):
        column, row = band_place(mine ^ (2 * k), block)
        both, tops = weighted(left_rows(grads, samples, turned, column, row, block), keeps)
        here = pl.ds(column, width + TILE)
        total = three(both, tops, high[:, here], low[:, here])
        mixed = three(both, tops, act_high[...], act_low[...])
        for number in range(len(keeps)):
            packed = pack(total[number * block : (number + 1) * block], row, 0.0)
            for half in range(2):
                spot = places[k, half]
                first = number * block + half * step
                value = mixed[first : first + step]
                if number:
                    store(outs, seeds, 2, spot, number - 1, 0, packed[half])
                    for part in range(feat // width):
                        below = packed[half].shape[0] + part * step
                        columns = slice(part * width, (part + 1) * width)
                        store(outs, seeds, 2, spot, number - 1, below, value[:, columns])
                else:
                    store(outs, seeds, 0, spot, 0, 0, packed[half])
                    store(outs, seeds, 1, spot, 0, 0, value)


def whole_in_vmem(count):
    return [pl.BlockSpec(memory_space=pltpu.VMEM)] * count


def prepare(routes, counts, acts):
    samples, feat = acts.shape
    rows = samples + 8 * -(-counts.shape[1] * samples // (8 * feat))
    return pl.pallas_call(
        prepare_kernel,
        out_shape=jax.ShapeDtypeStruct((rows, feat), F32),
        in_specs=[pl.BlockSpec(memory_space=pltpu.HBM)] * 3,
        out_specs=pl.BlockSpec(memory_space=pltpu.HBM),
        scratch_shapes=[
            pltpu.VMEM(routes.shape[::-1], jnp.int32),
            pltpu.SMEM(counts.shape, jnp.int32),
            pltpu.VMEM((rows, feat), F32),
            pltpu.SemaphoreType.DMA((11,)),
        ],
        compiler_params=pltpu.CompilerParams(vmem_limit_bytes=60 * MIB),
    )(routes.T, counts, acts)


def bands(body, turns, groups, place, parts, seeds, samples, chips, block):
    feat = parts[0].shape[1]
    extended = pltpu.VMEM((2 * samples, feat + feat // 2), BF16)
    plain = pltpu.VMEM((2 * samples, feat), BF16)
    scratch = [extended, extended] + ([plain, plain] if len(parts) > 2 else [])
    shapes = [
        jax.ShapeDtypeStruct((len(group), count, *piece_shape(kind, half, block, feat)), F32)
        for count, kind in groups
        for half, order in enumerate(orders(chips))
        for group in held_and_sent(chips, order)
    ]
    operands = (*parts, *seeds)
    limit = 36 if len(parts) > 2 else 20
    return pl.pallas_call(
        functools.partial(body, range(turns), block, chips, bool(seeds), samples),
        out_shape=shapes,
        in_specs=[pl.BlockSpec(memory_space=pltpu.SMEM)] + whole_in_vmem(len(operands)),
        out_specs=whole_in_vmem(len(shapes)),
        scratch_shapes=scratch + [pltpu.VMEM((TILE, 2 * samples), F32)],
        compiler_params=pltpu.CompilerParams(vmem_limit_bytes=limit * MIB),
    )(place, *operands)


def unfold(bands, extras, full):
    tiles = full.shape[0] // TILE
    per_tile = extras.shape[0] // EXTRA // tiles
    rows = lax.broadcasted_iota(jnp.int32, (TILE, TILE), 0)
    columns = lax.broadcasted_iota(jnp.int32, (TILE, TILE), 1)

    def put(i, j, value):
        full[i * TILE : (i + 1) * TILE, j * TILE : (j + 1) * TILE] = value

    firsts = [bands[i * TILE : (i + 1) * TILE, 0:TILE] for i in range(tiles)]
    turned = [value.T for value in firsts]
    for i in range(tiles):
        put(i, i, jnp.where(rows <= columns, firsts[i], turned[i]))
        for step in range(1, tiles // 2):
            here = bands[i * TILE : (i + 1) * TILE, step * TILE : (step + 1) * TILE]
            put(i, (i + step) % tiles, here)
            put((i + step) % tiles, i, here.T)
    for i in range(tiles // 2):
        j = i + tiles // 2
        places = [EXTRA * (i * per_tile + owner) for owner in range(per_tile)]
        diagonal = sum(extras[place : place + 1, :] for place in places)
        here = jnp.where(rows > columns, firsts[i], jnp.where(rows < columns, turned[j], diagonal))
        put(i, j, here)
        put(j, i, here.T)


def damping(full):
    size = full.shape[0]
    value = full[...]
    lanes = lax.broadcasted_iota(jnp.int32, (size, size), 1)
    sublanes = lax.broadcasted_iota(jnp.int32, (size, size), 0)
    trace = jnp.sum(jnp.sum(jnp.where(lanes == sublanes, value, 0.0), axis=0, keepdims=True), axis=1, keepdims=True)
    largest = jnp.max(jnp.sum(jnp.abs(value), axis=0, keepdims=True), axis=1, keepdims=True)
    damp = trace * (0.1 / size)
    return damp, 1.0 / (largest + damp)


def times(left, high, low):
    rows = left.shape[0]
    top, rest = split(left)
    first = dot(jnp.concatenate([top, rest], axis=0), high[...])
    return first[0:rows] + first[rows : 2 * rows] + dot(top, low[...])


def gather_order(order):
    offsets = [0]
    for bit in order:
        offsets += [k | (1 << bit) for k in offsets]
    return offsets


def row_pieces(place, block, chips, arrays, extra):
    step = block // 2
    firsts = [(value, first) for value in arrays for first in range(0, value.shape[0], block + extra)]
    pieces, extras = [], []
    for number, (value, first) in enumerate(firsts):
        core, position = number // chips, number % chips
        for half, order in enumerate(orders(chips)):
            owner = place[0] ^ (2 * gather_order(order)[position] + core)
            here = pl.ds(pl.multiple_of(owner * block + half * step, step), step)
            pieces.append((here, value.at[first + half * step : first + (half + 1) * step]))
        if extra:
            here = pl.ds(pl.multiple_of(owner * EXTRA, EXTRA), EXTRA)
            extras.append((here, value.at[first + block : first + block + extra]))
    return pieces, extras


def factor_rows(place, block, blocks, bands, extras, full):
    chips = full.shape[0] // (2 * block)
    pieces, others = row_pieces(place, block, chips, blocks, EXTRA)
    for here, value in pieces:
        bands[here, :] = value[...]
    for here, value in others:
        extras[here, :] = value[:, 0:TILE]
    unfold(bands, extras, full)
    return full[pl.ds(pl.multiple_of(place[0] * block, block), block), :]


def act_factor_kernel(place, *refs):
    blocks, (factor, scales, high, low), (bands, extras, full) = refs[:-7], refs[-7:-3], refs[-3:]
    factor[...] = factor_rows(place, factor.shape[0], blocks, bands, extras, full)
    damp, alpha = damping(full)
    scales[0:1, :] = jnp.broadcast_to(damp, (1, TILE))
    scales[1:2, :] = jnp.broadcast_to(alpha, (1, TILE))
    high[...], low[...] = split(full[...])


def grad_factor_kernel(place, *refs):
    blocks, (factor, inverse), (bands, extras, full, high, low) = refs[:-7], refs[-7:-5], refs[-5:]
    block, feat = factor.shape
    rows = factor_rows(place, block, blocks, bands, extras, full)
    factor[...] = rows
    damp, alpha = damping(full)
    high[...], low[...] = split(full[...])
    lanes = lax.broadcasted_iota(jnp.int32, (block, feat), 1)
    sublanes = lax.broadcasted_iota(jnp.int32, (block, feat), 0)
    unit = jnp.where(lanes == sublanes + place[0] * block, 1.0, 0.0).astype(F32)
    rest_rows = unit - alpha * (rows + damp * unit)
    once = 2.0 * rest_rows - alpha * (times(rest_rows, high, low) + damp * rest_rows)
    inverse[...] = alpha * (unit + rest_rows + once - alpha * (times(once, high, low) + damp * once))


def update_kernel(place, *refs):
    blocks = refs[:-10]
    inverse, scales, act_high, act_low, momentum, weights, moment_out, weight_out, high, low = refs[-10:]
    block = momentum.shape[0]
    for here, value in row_pieces(place, block, high.shape[0] // (2 * block), blocks, 0)[0]:
        high[here, :], low[here, :] = split(value[...])
    damp, alpha = scales[0:1, 0:1], scales[1:2, 0:1]
    half_way = times(inverse[...], high, low)
    value = half_way
    for _ in range(3):
        value = half_way + value - alpha * (times(value, act_high[...], act_low[...]) + damp * value)
    moment = 0.9 * momentum[...] + alpha * value
    moment_out[...] = moment
    weight_out[...] = weights[...] - 0.5 * moment


def on_core(body, place, operands, shapes, scratch, limit):
    return pl.pallas_call(
        body,
        out_shape=shapes,
        in_specs=[pl.BlockSpec(memory_space=pltpu.SMEM)] + whole_in_vmem(len(operands)),
        out_specs=whole_in_vmem(len(shapes)),
        scratch_shapes=scratch,
        compiler_params=pltpu.CompilerParams(vmem_limit_bytes=limit * MIB),
    )(place, *operands)


def factor_scratch(block, feat):
    shapes = [(feat, feat // 2), (EXTRA * feat // block, TILE), (feat, feat)]
    return [pltpu.VMEM(shape, F32) for shape in shapes]


def act_factor_rows(place, blocks, block, feat):
    shapes = [((block, feat), F32), ((8, TILE), F32), ((feat, feat), BF16), ((feat, feat), BF16)]
    shapes = [jax.ShapeDtypeStruct(*shape) for shape in shapes]
    scratch = factor_scratch(block, feat)
    return on_core(act_factor_kernel, place, blocks, shapes, scratch, 32)


def grad_factor_rows(place, blocks, block, feat):
    shapes = [jax.ShapeDtypeStruct((block, feat), F32)] * 2
    scratch = factor_scratch(block, feat)
    scratch += [pltpu.VMEM((feat, feat), BF16)] * 2
    return on_core(grad_factor_kernel, place, blocks, shapes, scratch, 32)


def update_rows(place, blocks, inverse, scales, high, low, momentum, weights):
    block, feat = momentum.shape
    operands = (*blocks, inverse, scales, high, low, momentum, weights)
    shapes = [jax.ShapeDtypeStruct((block, feat), F32)] * 2
    return on_core(update_kernel, place, operands, shapes, [pltpu.VMEM((feat, feat), BF16)] * 2, 32)


def swap(value, axis, step):
    size = lax.axis_size(axis)
    return lax.ppermute(value, axis, [(i, i ^ step) for i in range(size)])


class PlaneSum:
    def __init__(self, pieces, chips):
        self.steps = [list(order) for order in orders(chips)]
        self.offsets = [held_and_sent(chips, order)[0] for order in self.steps]
        self.held, self.leaving = list(pieces[0::2]), list(pieces[1::2])

    def send(self):
        self.got = [swap(value, "dp", 2 << order[0]) for value, order in zip(self.leaving, self.steps)]

    def add(self):
        self.leaving = []
        for half, order in enumerate(self.steps):
            offsets = self.offsets[half]
            sums = {k: self.held[half][i] + self.got[half][i] for i, k in enumerate(offsets)}
            order.pop(0)
            if order:
                offsets = [k for k in offsets if not (k >> order[0]) & 1]
                self.leaving.append(jnp.stack([sums[k | (1 << order[0])] for k in offsets]))
            self.offsets[half] = offsets
            self.held[half] = [sums[k] for k in offsets]

    def finish(self):
        while self.steps[0]:
            self.send()
            self.add()
        return [held[0] for held in self.held]


def across(far):
    return [swap(far[number], "expert", 2 * (number + 1)) for number in range(far.shape[0])]


class Gather:
    def __init__(self, halves, chips):
        self.chips, self.orders = chips, orders(chips)
        self.halves, self.whole = halves, {}

    def begin(self):
        block = jnp.concatenate(self.halves, axis=0)
        self.whole = {order[0]: swap(block, "dp", 2 << order[0]) for order in self.orders}

    def relay(self):
        first = self.halves[0].shape[0]
        self.held = []
        for half, order in enumerate(self.orders):
            held = [self.halves[half]]
            for bit in order:
                came = [swap(value, "dp", 2 << bit) for value in held[1:]]
                if bit in self.whole:
                    own = self.whole[bit][first:] if half else self.whole[bit][:first]
                else:
                    own = swap(held[0], "dp", 2 << bit)
                held += [own] + came
            self.held.append(held)

    def hold_last(self, value):
        last, value = together([held[-1] for held in self.held], value)
        self.held = [held[:-1] + [block] for held, block in zip(self.held, last)]
        return value

    def exchange(self, first=0, last=None):
        pairs = list(zip(*self.held))[first:last]
        mine = jnp.concatenate([value for pair in pairs for value in pair], axis=0)
        return mine, swap(mine, "dp", 1)


def together(*values):
    return lax.optimization_barrier(values)


def on_device(acts, grads_out, routes, counts, old_act_factor, old_grad_factor, momentum, weights):
    devices, experts = lax.axis_size("dp"), lax.axis_size("expert")
    chips = devices // 2
    samples, feat, block = acts.shape[0], acts.shape[1], weights.shape[1]
    step, width = block // 2, feat // 2
    mine = lax.axis_index("dp")
    place = jnp.stack([mine, lax.axis_index("expert")]).astype(jnp.int32)

    def own_band(old):
        start = mine * block // TILE * TILE
        wide = jnp.concatenate([old[0], old[0][:, 0:width]], axis=1)
        band = lax.dynamic_slice_in_dim(wide, start, width + TILE, 1)
        return [0.5 * half for half in pack(band, mine * block - start, 0.0)]

    turns = experts // 2
    size = (samples, chips, block)
    act_groups = ((turns, "factor"),)
    grad_groups = ((1, "factor"), (1, "mixed"), (turns - 1, "both"))

    acts = prepare(routes, counts, acts)
    acts_far = swap(acts, "expert", 1)
    near_acts = (acts, swap(acts, "dp", 1))
    act_seeds = bands(act_kernel, turns, act_groups, place, near_acts, (), *size)
    grads_far = swap(grads_out, "expert", 1)
    grad_parts = (grads_out, swap(grads_out, "dp", 1)) + near_acts
    grad_seeds = bands(grad_kernel, turns, grad_groups, place, grad_parts, (), *size)
    old_act, old_grad = own_band(old_act_factor), own_band(old_grad_factor)
    early = (act_seeds, grad_seeds, old_act, old_grad)
    acts_far, (act_seeds, grad_seeds, old_act, old_grad) = together(acts_far, early)

    far_acts = (acts_far, swap(acts_far, "dp", 1))
    act_sum = PlaneSum(bands(act_kernel, turns, act_groups, place, far_acts, act_seeds, *size), chips)
    act_sum.send()
    act_sum.add()
    act_sum.send()
    grads_far, _ = together(grads_far, act_sum.leaving)
    grad_parts = (grads_far, swap(grads_far, "dp", 1)) + far_acts
    pieces = bands(grad_kernel, turns, grad_groups, place, grad_parts, grad_seeds, *size)

    grad_sum, mixed_sum, far_sum = [PlaneSum(pieces[first : first + 4], chips) for first in (0, 4, 8)]
    far_sum.send()
    act_sum.got, far_sum.held = together(act_sum.got, far_sum.held)
    act_sum.add()
    act_sums = act_sum.finish()
    act_across = across(jnp.concatenate([value[1:] for value in act_sums], axis=1))
    grad_sum.leaving, far_sum.got = together(grad_sum.leaving, far_sum.got)
    grad_sum.send()
    far_sum.add()
    far_sum.leaving, act_across = together(far_sum.leaving, act_across)
    far_sum.send()
    grad_sum.add()
    mixed_sum.leaving, grad_sum.leaving = together(mixed_sum.leaving, grad_sum.leaving)
    mixed_sum.send()
    grad_sum.send()
    far_sum.add()
    far_sums = far_sum.finish()

    factors = [slice(0, step), slice(step, block + EXTRA)]
    act_totals = [
        sum((there[factors[half]] for there in act_across), value[0]) for half, value in enumerate(act_sums)
    ]
    total = jnp.maximum(act_totals[1][step + 1 : step + 2, 0:1], 1.0)
    act_halves = [old + 0.5 * (value / total) for old, value in zip(old_act, act_totals)]
    sizes = [step, step + EXTRA]
    across_grad = across(jnp.concatenate([value[:, 0:size] for value, size in zip(far_sums, sizes)], axis=1))
    far_mixed = jnp.concatenate(
        [
            jnp.concatenate([value[:, size : size + step], value[:, size + step :]], axis=2)
            for value, size in zip(far_sums, sizes)
        ],
        axis=1,
    )
    grad_sum.add()
    grad_sums = grad_sum.finish()
    mixed_sum.held, across_grad = together(mixed_sum.held, across_grad)
    mixed_sum.add()
    mixed_sum.leaving, far_mixed = together(mixed_sum.leaving, far_mixed)
    mixed_sum.send()
    across_mixed = across(far_mixed)

    def both(near, far, rows):
        return [sum((there[here] for there in far), value[0]) / total for value, here in zip(near, rows)]

    grad_stats = both(grad_sums, across_grad, factors)
    grad_halves = [old + 0.5 * value for old, value in zip(old_grad, grad_stats)]
    grad_gather = Gather(grad_halves, chips)
    grad_gather.begin()
    early = (grad_gather.whole, mixed_sum.got)
    act_halves, (grad_gather.whole, mixed_sum.got) = together(act_halves, early)
    mixed_sum.add()
    mixed_sums = mixed_sum.finish()
    act_gather = Gather(act_halves, chips)
    act_gather.begin()
    grad_gather.relay()
    act_gather.relay()
    across_mixed, _ = together(across_mixed, act_gather.whole)
    mixed_gather = Gather(both(mixed_sums, across_mixed, [slice(0, step), slice(step, block)]), chips)
    mixed_gather.begin()
    grad_out, inverse = grad_factor_rows(place, grad_gather.exchange(), block, feat)
    inverse = act_gather.hold_last(inverse)
    mixed_gather.whole = act_gather.hold_last(mixed_gather.whole)
    mixed_gather.relay()
    mine, theirs = mixed_gather.exchange(0, -1)
    act_out, *act_square = act_factor_rows(place, act_gather.exchange(), block, feat)
    act_square = mixed_gather.hold_last(act_square)
    my_last, their_last = mixed_gather.exchange(-1)
    mixed_blocks = (mine, my_last, theirs, their_last)
    outs = update_rows(place, mixed_blocks, inverse, *act_square, momentum[0], weights[0])
    return tuple(out[None] for out in (act_out, grad_out, *outs))


def solution(mesh):
    rows = P(("dp", "expert"), None)
    matrix = P("expert", "dp", None)
    return jax.shard_map(
        on_device,
        mesh=mesh,
        in_specs=(rows,) * 4 + (matrix,) * 4,
        out_specs=(matrix,) * 4,
        check_vma=False,
    )
```

```python
import functools

import jax
import jax.numpy as jnp
from jax import lax
from jax.experimental import pallas as pl
from jax.experimental.pallas import tpu as pltpu
from jax.sharding import PartitionSpec as P

F32 = jnp.float32
BF16 = jnp.bfloat16
TILE = 128
EXTRA = 8
MIB = 1024 * 1024


def split(value):
    high = value.astype(BF16)
    return high, (value - high.astype(F32)).astype(BF16)


def dot(left, right):
    return jnp.dot(left, right, preferred_element_type=F32)


def band_place(owner, block):
    per_tile = TILE // block
    if per_tile == 1:
        return pl.multiple_of(owner * TILE, TILE), 0
    return (
        pl.multiple_of(lax.div(owner, per_tile) * TILE, TILE),
        pl.multiple_of(lax.rem(owner, per_tile) * block, block),
    )


def split_rows(parts, samples, high, low, feat):
    extra = high.shape[1] - feat
    for number, part in enumerate(parts):
        here = slice(number * samples, (number + 1) * samples)
        top, rest = split(part[0:samples, :])
        high[here, 0:feat] = top
        low[here, 0:feat] = rest
        if extra:
            high[here, feat : feat + extra] = top[:, 0:extra]
            low[here, feat : feat + extra] = rest[:, 0:extra]


def left_rows(parts, samples, turned, column, row, block):
    for number, part in enumerate(parts):
        here = slice(number * samples, (number + 1) * samples)
        turned[:, here] = part[0:samples, pl.ds(column, TILE)].T
    return turned[pl.ds(row, block), :]


def keep_place(expert, samples, feat):
    per_row = feat // samples
    return lax.div(expert, per_row), pl.multiple_of(lax.rem(expert, per_row) * samples, TILE)


def keep_row(parts, samples, expert):
    row, column = keep_place(expert, samples, parts[0].shape[1])
    return jnp.concatenate([part[pl.ds(row, 1), pl.ds(column, samples)] for part in parts], axis=1)


def weighted(rows, keeps):
    halves = [split(rows * keep) for keep in keeps]
    tops = [half[0] for half in halves]
    return jnp.concatenate(tops + [half[1] for half in halves], axis=0), jnp.concatenate(tops, axis=0)


def three(both, tops, high, low):
    half = tops.shape[0]
    first = dot(both, high)
    return first[0:half] + first[half : 2 * half] + dot(tops, low)


def orders(chips):
    bits = list(range(chips.bit_length() - 1))
    return bits, bits[1:] + bits[:1]


def held_and_sent(chips, order):
    if not order:
        return [0], []
    held = [k for k in range(chips) if not (k >> order[0]) & 1]
    return held, [k | (1 << order[0]) for k in held]


def slots(chips):
    places = {}
    for half, order in enumerate(orders(chips)):
        for which, group in enumerate(held_and_sent(chips, order)):
            for position, k in enumerate(group):
                places[k, half] = (2 * half + which, position)
    return places


def pack(band, row, count):
    block, width = band.shape[0], band.shape[1] - TILE
    rows = lax.broadcasted_iota(jnp.int32, (block, TILE), 0) + row
    columns = lax.broadcasted_iota(jnp.int32, (block, TILE), 1)
    last = band[:, width:]
    first = jnp.where(rows > columns, last, band[:, 0:TILE])
    diagonal = jnp.sum(jnp.where(rows == columns, last, 0.0), axis=0, keepdims=True)
    places = lax.broadcasted_iota(jnp.int32, (EXTRA, TILE), 0)
    extra = jnp.where(places == 0, diagonal, jnp.where(places == 1, count, 0.0))
    extra = jnp.concatenate([extra, jnp.zeros((EXTRA, width - TILE), F32)], axis=1)
    packed = jnp.concatenate([first, band[:, TILE:width]], axis=1)
    return packed[0 : block // 2], jnp.concatenate([packed[block // 2 :], extra], axis=0)


def piece_shape(kind, half, block, feat):
    step, width = block // 2, feat // 2
    factor = step + EXTRA * half
    if kind == "factor":
        return factor, width
    if kind == "mixed":
        return step, feat
    return factor + step * (feat // width), width


def store(outs, seeds, group, place, number, first, value):
    output, position = 4 * group + place[0], place[1]
    here = slice(first, first + value.shape[0])
    if seeds:
        value = value + seeds[output][position, number, here, :]
    outs[output][position, number, here, :] = value


def prepare_kernel(routes, counts, out, samples, feat):
    experts = counts.shape[1]
    out[...] = jnp.zeros(out.shape, F32)
    hits = []
    for expert in range(experts):
        same = [jnp.where(routes[k : k + 1, :] == expert, 1.0, 0.0) for k in range(routes.shape[0])]
        hits.append(sum(same[1:], same[0]))
    hit = jnp.concatenate(hits, axis=0)
    first = lax.broadcasted_iota(jnp.int32, (samples, samples), 0)
    second = lax.broadcasted_iota(jnp.int32, (samples, samples), 1)
    rank = dot(hit.astype(BF16), jnp.where(first < second, 1.0, 0.0).astype(BF16))
    per_row = feat // samples
    for expert in range(experts):
        limit = counts[0, expert].astype(F32)
        keep = jnp.where(rank[expert : expert + 1, :] < limit, hits[expert], 0.0)
        row, column = expert // per_row, expert % per_row * samples
        out[row : row + 1, column : column + samples] = keep


def act_kernel(turns, block, chips, seeded, samples, place, *refs):
    parts, kept, refs = refs[:2], refs[2:4], refs[4:]
    refs, (high, low, turned) = refs[:-3], refs[-3:]
    seeds, outs = (refs[: len(refs) // 2], refs[len(refs) // 2 :]) if seeded else ((), refs)
    feat = parts[0].shape[1]
    width = feat // 2 + TILE
    mine, expert = place[0], place[1]
    split_rows(parts, samples, high, low, feat)
    keeps = [keep_row(kept, samples, expert ^ (2 * turn)) for turn in turns]
    places = slots(chips)
    for k in range(chips):
        column, row = band_place(mine ^ (2 * k), block)
        both, tops = weighted(left_rows(parts, samples, turned, column, row, block), keeps)
        total = three(both, tops, high[:, pl.ds(column, width)], low[:, pl.ds(column, width)])
        for number, keep in enumerate(keeps):
            count = jnp.sum(keep, axis=1, keepdims=True)
            packed = pack(total[number * block : (number + 1) * block], row, count)
            for half in range(2):
                store(outs, seeds, 0, places[k, half], number, 0, packed[half])


def grad_kernel(turns, block, chips, seeded, samples, place, *refs):
    grads, acts, kept, refs = refs[:2], refs[2:4], refs[4:6], refs[6:]
    refs, (high, low, act_high, act_low, turned) = refs[:-5], refs[-5:]
    seeds, outs = (refs[: len(refs) // 2], refs[len(refs) // 2 :]) if seeded else ((), refs)
    feat = grads[0].shape[1]
    step, width = block // 2, feat // 2
    mine, expert = place[0], place[1]
    split_rows(grads, samples, high, low, feat)
    split_rows(acts, samples, act_high, act_low, feat)
    keeps = [keep_row(kept, samples, expert ^ (2 * turn)) for turn in turns]
    places = slots(chips)
    for k in range(chips):
        column, row = band_place(mine ^ (2 * k), block)
        both, tops = weighted(left_rows(grads, samples, turned, column, row, block), keeps)
        here = pl.ds(column, width + TILE)
        total = three(both, tops, high[:, here], low[:, here])
        mixed = three(both, tops, act_high[...], act_low[...])
        for number in range(len(keeps)):
            packed = pack(total[number * block : (number + 1) * block], row, 0.0)
            for half in range(2):
                spot = places[k, half]
                first = number * block + half * step
                value = mixed[first : first + step]
                if number:
                    store(outs, seeds, 2, spot, number - 1, 0, packed[half])
                    for part in range(feat // width):
                        below = packed[half].shape[0] + part * step
                        columns = slice(part * width, (part + 1) * width)
                        store(outs, seeds, 2, spot, number - 1, below, value[:, columns])
                else:
                    store(outs, seeds, 0, spot, 0, 0, packed[half])
                    store(outs, seeds, 1, spot, 0, 0, value)


def whole_in_vmem(count):
    return [pl.BlockSpec(memory_space=pltpu.VMEM)] * count


def prepare(routes, counts, feat):
    samples = routes.shape[0]
    rows = EXTRA * -(-counts.shape[1] * samples // (EXTRA * feat))
    return pl.pallas_call(
        functools.partial(prepare_kernel, samples=samples, feat=feat),
        out_shape=jax.ShapeDtypeStruct((rows, feat), F32),
        in_specs=[pl.BlockSpec(memory_space=pltpu.VMEM), pl.BlockSpec(memory_space=pltpu.SMEM)],
        out_specs=pl.BlockSpec(memory_space=pltpu.VMEM),
        compiler_params=pltpu.CompilerParams(vmem_limit_bytes=60 * MIB),
    )(routes.T, counts)


def bands(body, turns, groups, place, parts, seeds, samples, chips, block):
    feat = parts[0].shape[1]
    extended = pltpu.VMEM((2 * samples, feat + feat // 2), BF16)
    plain = pltpu.VMEM((2 * samples, feat), BF16)
    scratch = [extended, extended] + ([plain, plain] if len(parts) > 4 else [])
    shapes = [
        jax.ShapeDtypeStruct((len(group), count, *piece_shape(kind, half, block, feat)), F32)
        for count, kind in groups
        for half, order in enumerate(orders(chips))
        for group in held_and_sent(chips, order)
    ]
    operands = (*parts, *seeds)
    limit = 36 if len(parts) > 4 else 20
    return pl.pallas_call(
        functools.partial(body, range(turns), block, chips, bool(seeds), samples),
        out_shape=shapes,
        in_specs=[pl.BlockSpec(memory_space=pltpu.SMEM)] + whole_in_vmem(len(operands)),
        out_specs=whole_in_vmem(len(shapes)),
        scratch_shapes=scratch + [pltpu.VMEM((TILE, 2 * samples), F32)],
        compiler_params=pltpu.CompilerParams(vmem_limit_bytes=limit * MIB),
    )(place, *operands)


def unfold(bands, extras, full):
    tiles = full.shape[0] // TILE
    per_tile = extras.shape[0] // EXTRA // tiles
    rows = lax.broadcasted_iota(jnp.int32, (TILE, TILE), 0)
    columns = lax.broadcasted_iota(jnp.int32, (TILE, TILE), 1)

    def put(i, j, value):
        full[i * TILE : (i + 1) * TILE, j * TILE : (j + 1) * TILE] = value

    firsts = [bands[i * TILE : (i + 1) * TILE, 0:TILE] for i in range(tiles)]
    turned = [value.T for value in firsts]
    for i in range(tiles):
        put(i, i, jnp.where(rows <= columns, firsts[i], turned[i]))
        for step in range(1, tiles // 2):
            here = bands[i * TILE : (i + 1) * TILE, step * TILE : (step + 1) * TILE]
            put(i, (i + step) % tiles, here)
            put((i + step) % tiles, i, here.T)
    for i in range(tiles // 2):
        j = i + tiles // 2
        places = [EXTRA * (i * per_tile + owner) for owner in range(per_tile)]
        diagonal = sum(extras[place : place + 1, :] for place in places)
        here = jnp.where(rows > columns, firsts[i], jnp.where(rows < columns, turned[j], diagonal))
        put(i, j, here)
        put(j, i, here.T)


def damping(full):
    size = full.shape[0]
    value = full[...]
    lanes = lax.broadcasted_iota(jnp.int32, (size, size), 1)
    sublanes = lax.broadcasted_iota(jnp.int32, (size, size), 0)
    trace = jnp.sum(jnp.sum(jnp.where(lanes == sublanes, value, 0.0), axis=0, keepdims=True), axis=1, keepdims=True)
    largest = jnp.max(jnp.sum(jnp.abs(value), axis=0, keepdims=True), axis=1, keepdims=True)
    damp = trace * (0.1 / size)
    return damp, 1.0 / (largest + damp)


def times(left, high, low):
    rows = left.shape[0]
    top, rest = split(left)
    first = dot(jnp.concatenate([top, rest], axis=0), high[...])
    return first[0:rows] + first[rows : 2 * rows] + dot(top, low[...])


def gather_order(order):
    offsets = [0]
    for bit in order:
        offsets += [k | (1 << bit) for k in offsets]
    return offsets


def row_pieces(place, block, chips, arrays, extra):
    step = block // 2
    firsts = [(value, first) for value in arrays for first in range(0, value.shape[0], block + extra)]
    pieces, extras = [], []
    for number, (value, first) in enumerate(firsts):
        core, position = number // chips, number % chips
        for half, order in enumerate(orders(chips)):
            owner = place[0] ^ (2 * gather_order(order)[position] + core)
            here = pl.ds(pl.multiple_of(owner * block + half * step, step), step)
            pieces.append((here, value.at[first + half * step : first + (half + 1) * step]))
        if extra:
            here = pl.ds(pl.multiple_of(owner * EXTRA, EXTRA), EXTRA)
            extras.append((here, value.at[first + block : first + block + extra]))
    return pieces, extras


def factor_rows(place, block, blocks, bands, extras, full):
    chips = full.shape[0] // (2 * block)
    pieces, others = row_pieces(place, block, chips, blocks, EXTRA)
    for here, value in pieces:
        bands[here, :] = value[...]
    for here, value in others:
        extras[here, :] = value[:, 0:TILE]
    unfold(bands, extras, full)
    return full[pl.ds(pl.multiple_of(place[0] * block, block), block), :]


def act_factor_kernel(place, *refs):
    blocks, (factor, scales, high, low), (bands, extras, full) = refs[:-7], refs[-7:-3], refs[-3:]
    factor[...] = factor_rows(place, factor.shape[0], blocks, bands, extras, full)
    damp, alpha = damping(full)
    scales[0:1, :] = jnp.broadcast_to(damp, (1, TILE))
    scales[1:2, :] = jnp.broadcast_to(alpha, (1, TILE))
    high[...], low[...] = split(full[...])


def grad_factor_kernel(place, *refs):
    blocks, (factor, inverse), (bands, extras, full, high, low) = refs[:-7], refs[-7:-5], refs[-5:]
    block, feat = factor.shape
    rows = factor_rows(place, block, blocks, bands, extras, full)
    factor[...] = rows
    damp, alpha = damping(full)
    high[...], low[...] = split(full[...])
    lanes = lax.broadcasted_iota(jnp.int32, (block, feat), 1)
    sublanes = lax.broadcasted_iota(jnp.int32, (block, feat), 0)
    unit = jnp.where(lanes == sublanes + place[0] * block, 1.0, 0.0).astype(F32)
    rest_rows = unit - alpha * (rows + damp * unit)
    once = 2.0 * rest_rows - alpha * (times(rest_rows, high, low) + damp * rest_rows)
    inverse[...] = alpha * (unit + rest_rows + once - alpha * (times(once, high, low) + damp * once))


def update_kernel(place, *refs):
    blocks = refs[:-9]
    inverse, scales, act_high, act_low, momentum, weights, moment_out, weight_out, full = refs[-9:]
    block = momentum.shape[0]
    for here, value in row_pieces(place, block, full.shape[0] // (2 * block), blocks, 0)[0]:
        full[here, :] = value[...]
    damp, alpha = scales[0:1, 0:1], scales[1:2, 0:1]
    half_way = times(inverse[...], *split(full[...]))
    value = half_way
    for _ in range(3):
        value = half_way + value - alpha * (times(value, act_high[...], act_low[...]) + damp * value)
    moment = 0.9 * momentum[...] + alpha * value
    moment_out[...] = moment
    weight_out[...] = weights[...] - 0.5 * moment


def on_core(body, place, operands, shapes, scratch, limit):
    return pl.pallas_call(
        body,
        out_shape=shapes,
        in_specs=[pl.BlockSpec(memory_space=pltpu.SMEM)] + whole_in_vmem(len(operands)),
        out_specs=whole_in_vmem(len(shapes)),
        scratch_shapes=scratch,
        compiler_params=pltpu.CompilerParams(vmem_limit_bytes=limit * MIB),
    )(place, *operands)


def factor_scratch(block, feat):
    shapes = [(feat, feat // 2), (EXTRA * feat // block, TILE), (feat, feat)]
    return [pltpu.VMEM(shape, F32) for shape in shapes]


def act_factor_rows(place, blocks, block, feat):
    shapes = [((block, feat), F32), ((8, TILE), F32), ((feat, feat), BF16), ((feat, feat), BF16)]
    shapes = [jax.ShapeDtypeStruct(*shape) for shape in shapes]
    scratch = factor_scratch(block, feat)
    return on_core(act_factor_kernel, place, blocks, shapes, scratch, 32)


def grad_factor_rows(place, blocks, block, feat):
    shapes = [jax.ShapeDtypeStruct((block, feat), F32)] * 2
    scratch = factor_scratch(block, feat)
    scratch += [pltpu.VMEM((feat, feat), BF16)] * 2
    return on_core(grad_factor_kernel, place, blocks, shapes, scratch, 32)


def update_rows(place, blocks, inverse, scales, high, low, momentum, weights):
    block, feat = momentum.shape
    operands = (*blocks, inverse, scales, high, low, momentum, weights)
    shapes = [jax.ShapeDtypeStruct((block, feat), F32)] * 2
    return on_core(update_kernel, place, operands, shapes, [pltpu.VMEM((feat, feat), F32)], 32)


def swap(value, axis, step):
    size = lax.axis_size(axis)
    return lax.ppermute(value, axis, [(i, i ^ step) for i in range(size)])


class PlaneSum:
    def __init__(self, pieces, chips):
        self.steps = [list(order) for order in orders(chips)]
        self.offsets = [held_and_sent(chips, order)[0] for order in self.steps]
        self.held, self.leaving = list(pieces[0::2]), list(pieces[1::2])

    def send(self):
        self.got = [swap(value, "dp", 2 << order[0]) for value, order in zip(self.leaving, self.steps)]

    def add(self):
        self.leaving = []
        for half, order in enumerate(self.steps):
            offsets = self.offsets[half]
            sums = {k: self.held[half][i] + self.got[half][i] for i, k in enumerate(offsets)}
            order.pop(0)
            if order:
                offsets = [k for k in offsets if not (k >> order[0]) & 1]
                self.leaving.append(jnp.stack([sums[k | (1 << order[0])] for k in offsets]))
            self.offsets[half] = offsets
            self.held[half] = [sums[k] for k in offsets]

    def finish(self):
        while self.steps[0]:
            self.send()
            self.add()
        return [held[0] for held in self.held]


def across(far):
    return [swap(far[number], "expert", 2 * (number + 1)) for number in range(far.shape[0])]


class Gather:
    def __init__(self, halves, chips):
        self.chips, self.orders = chips, orders(chips)
        self.halves, self.whole = halves, {}

    def begin(self):
        block = jnp.concatenate(self.halves, axis=0)
        self.whole = {order[0]: swap(block, "dp", 2 << order[0]) for order in self.orders}

    def relay(self):
        first = self.halves[0].shape[0]
        self.held = []
        for half, order in enumerate(self.orders):
            held = [self.halves[half]]
            for bit in order:
                came = [swap(value, "dp", 2 << bit) for value in held[1:]]
                if bit in self.whole:
                    own = self.whole[bit][first:] if half else self.whole[bit][:first]
                else:
                    own = swap(held[0], "dp", 2 << bit)
                held += [own] + came
            self.held.append(held)

    def hold_last(self, value):
        last, value = together([held[-1] for held in self.held], value)
        self.held = [held[:-1] + [block] for held, block in zip(self.held, last)]
        return value

    def exchange(self, first=0, last=None):
        pairs = list(zip(*self.held))[first:last]
        mine = jnp.concatenate([value for pair in pairs for value in pair], axis=0)
        return mine, swap(mine, "dp", 1)


def together(*values):
    return lax.optimization_barrier(values)


def on_device(acts, grads_out, routes, counts, old_act_factor, old_grad_factor, momentum, weights):
    devices, experts = lax.axis_size("dp"), lax.axis_size("expert")
    chips = devices // 2
    samples, feat, block = acts.shape[0], acts.shape[1], weights.shape[1]
    step, width = block // 2, feat // 2
    mine = lax.axis_index("dp")
    place = jnp.stack([mine, lax.axis_index("expert")]).astype(jnp.int32)

    def own_band(old):
        start = mine * block // TILE * TILE
        wide = jnp.concatenate([old[0], old[0][:, 0:width]], axis=1)
        band = lax.dynamic_slice_in_dim(wide, start, width + TILE, 1)
        return [0.5 * half for half in pack(band, mine * block - start, 0.0)]

    turns = experts // 2
    size = (samples, chips, block)
    act_groups = ((turns, "factor"),)
    grad_groups = ((1, "factor"), (1, "mixed"), (turns - 1, "both"))

    acts_far = swap(acts, "expert", 1)
    keep = prepare(routes, counts, feat)
    keep_far = swap(keep, "expert", 1)
    near_acts = (acts, swap(acts, "dp", 1), keep, swap(keep, "dp", 1))
    act_seeds = bands(act_kernel, turns, act_groups, place, near_acts, (), *size)
    grads_far = swap(grads_out, "expert", 1)
    grad_parts = (grads_out, swap(grads_out, "dp", 1)) + near_acts
    grad_seeds = bands(grad_kernel, turns, grad_groups, place, grad_parts, (), *size)
    old_act, old_grad = own_band(old_act_factor), own_band(old_grad_factor)
    early = (act_seeds, grad_seeds, old_act, old_grad)
    acts_far, (act_seeds, grad_seeds, old_act, old_grad) = together(acts_far, early)

    far_acts = (acts_far, swap(acts_far, "dp", 1), keep_far, swap(keep_far, "dp", 1))
    act_sum = PlaneSum(bands(act_kernel, turns, act_groups, place, far_acts, act_seeds, *size), chips)
    act_sum.send()
    act_sum.add()
    act_sum.send()
    grads_far, _ = together(grads_far, act_sum.leaving)
    grad_parts = (grads_far, swap(grads_far, "dp", 1)) + far_acts
    pieces = bands(grad_kernel, turns, grad_groups, place, grad_parts, grad_seeds, *size)

    grad_sum, mixed_sum, far_sum = [PlaneSum(pieces[first : first + 4], chips) for first in (0, 4, 8)]
    far_sum.send()
    act_sum.got, far_sum.held = together(act_sum.got, far_sum.held)
    act_sum.add()
    act_sums = act_sum.finish()
    act_across = across(jnp.concatenate([value[1:] for value in act_sums], axis=1))
    grad_sum.leaving, far_sum.got = together(grad_sum.leaving, far_sum.got)
    grad_sum.send()
    far_sum.add()
    far_sum.leaving, act_across = together(far_sum.leaving, act_across)
    far_sum.send()
    grad_sum.add()
    mixed_sum.leaving, grad_sum.leaving = together(mixed_sum.leaving, grad_sum.leaving)
    mixed_sum.send()
    grad_sum.send()
    far_sum.add()
    far_sums = far_sum.finish()

    factors = [slice(0, step), slice(step, block + EXTRA)]
    act_totals = [
        sum((there[factors[half]] for there in act_across), value[0]) for half, value in enumerate(act_sums)
    ]
    total = jnp.maximum(act_totals[1][step + 1 : step + 2, 0:1], 1.0)
    act_halves = [old + 0.5 * (value / total) for old, value in zip(old_act, act_totals)]
    sizes = [step, step + EXTRA]
    across_grad = across(jnp.concatenate([value[:, 0:size] for value, size in zip(far_sums, sizes)], axis=1))
    far_mixed = jnp.concatenate(
        [
            jnp.concatenate([value[:, size : size + step], value[:, size + step :]], axis=2)
            for value, size in zip(far_sums, sizes)
        ],
        axis=1,
    )
    grad_sum.add()
    grad_sums = grad_sum.finish()
    mixed_sum.held, across_grad = together(mixed_sum.held, across_grad)
    mixed_sum.add()
    mixed_sum.leaving, far_mixed = together(mixed_sum.leaving, far_mixed)
    mixed_sum.send()
    across_mixed = across(far_mixed)

    def both(near, far, rows):
        return [sum((there[here] for there in far), value[0]) / total for value, here in zip(near, rows)]

    grad_stats = both(grad_sums, across_grad, factors)
    grad_halves = [old + 0.5 * value for old, value in zip(old_grad, grad_stats)]
    grad_gather = Gather(grad_halves, chips)
    grad_gather.begin()
    early = (grad_gather.whole, mixed_sum.got)
    act_halves, (grad_gather.whole, mixed_sum.got) = together(act_halves, early)
    mixed_sum.add()
    mixed_sums = mixed_sum.finish()
    act_gather = Gather(act_halves, chips)
    act_gather.begin()
    grad_gather.relay()
    act_gather.relay()
    across_mixed, _ = together(across_mixed, act_gather.whole)
    mixed_gather = Gather(both(mixed_sums, across_mixed, [slice(0, step), slice(step, block)]), chips)
    mixed_gather.begin()
    grad_out, inverse = grad_factor_rows(place, grad_gather.exchange(), block, feat)
    inverse = act_gather.hold_last(inverse)
    mixed_gather.whole = act_gather.hold_last(mixed_gather.whole)
    mixed_gather.relay()
    mine, theirs = mixed_gather.exchange(0, -1)
    act_out, *act_square = act_factor_rows(place, act_gather.exchange(), block, feat)
    act_square = mixed_gather.hold_last(act_square)
    my_last, their_last = mixed_gather.exchange(-1)
    mixed_blocks = (mine, my_last, theirs, their_last)
    outs = update_rows(place, mixed_blocks, inverse, *act_square, momentum[0], weights[0])
    return tuple(out[None] for out in (act_out, grad_out, *outs))


def solution(mesh):
    rows = P(("dp", "expert"), None)
    matrix = P("expert", "dp", None)
    return jax.shard_map(
        on_device,
        mesh=mesh,
        in_specs=(rows,) * 4 + (matrix,) * 4,
        out_specs=(matrix,) * 4,
        check_vma=False,
    )
```

```python
import functools

import jax
import jax.numpy as jnp
from jax import lax
from jax.experimental import pallas as pl
from jax.experimental.pallas import tpu as pltpu
from jax.sharding import PartitionSpec as P

F32 = jnp.float32
BF16 = jnp.bfloat16
TILE = 128
EXTRA = 8
MIB = 1024 * 1024


def split(value):
    high = value.astype(BF16)
    return high, (value - high.astype(F32)).astype(BF16)


def dot(left, right):
    return jnp.dot(left, right, preferred_element_type=F32)


def band_place(owner, block):
    per_tile = TILE // block
    if per_tile == 1:
        return pl.multiple_of(owner * TILE, TILE), 0
    return (
        pl.multiple_of(lax.div(owner, per_tile) * TILE, TILE),
        pl.multiple_of(lax.rem(owner, per_tile) * block, block),
    )


def split_rows(parts, samples, high, low, feat):
    extra = high.shape[1] - feat
    for number, part in enumerate(parts):
        here = slice(number * samples, (number + 1) * samples)
        top, rest = split(part[0:samples, :])
        high[here, 0:feat] = top
        low[here, 0:feat] = rest
        if extra:
            high[here, feat : feat + extra] = top[:, 0:extra]
            low[here, feat : feat + extra] = rest[:, 0:extra]


def left_rows(parts, samples, turned, column, row, block):
    for number, part in enumerate(parts):
        here = slice(number * samples, (number + 1) * samples)
        turned[:, here] = part[0:samples, pl.ds(column, TILE)].T
    return turned[pl.ds(row, block), :]


def keep_place(expert, samples, feat):
    per_row = feat // samples
    return lax.div(expert, per_row), pl.multiple_of(lax.rem(expert, per_row) * samples, TILE)


def keep_row(parts, samples, expert):
    row, column = keep_place(expert, samples, parts[0].shape[1])
    return jnp.concatenate([part[pl.ds(row, 1), pl.ds(column, samples)] for part in parts], axis=1)


def weighted(rows, keeps):
    halves = [split(rows * keep) for keep in keeps]
    tops = [half[0] for half in halves]
    return jnp.concatenate(tops + [half[1] for half in halves], axis=0), jnp.concatenate(tops, axis=0)


def three(both, tops, high, low):
    half = tops.shape[0]
    first = dot(both, high)
    return first[0:half] + first[half : 2 * half] + dot(tops, low)


def orders(chips):
    bits = list(range(chips.bit_length() - 1))
    return bits, bits[1:] + bits[:1]


def held_and_sent(chips, order):
    if not order:
        return [0], []
    held = [k for k in range(chips) if not (k >> order[0]) & 1]
    return held, [k | (1 << order[0]) for k in held]


def slots(chips):
    places = {}
    for half, order in enumerate(orders(chips)):
        for which, group in enumerate(held_and_sent(chips, order)):
            for position, k in enumerate(group):
                places[k, half] = (2 * half + which, position)
    return places


def pack(band, row, count):
    block, width = band.shape[0], band.shape[1] - TILE
    rows = lax.broadcasted_iota(jnp.int32, (block, TILE), 0) + row
    columns = lax.broadcasted_iota(jnp.int32, (block, TILE), 1)
    last = band[:, width:]
    first = jnp.where(rows > columns, last, band[:, 0:TILE])
    diagonal = jnp.sum(jnp.where(rows == columns, last, 0.0), axis=0, keepdims=True)
    places = lax.broadcasted_iota(jnp.int32, (EXTRA, TILE), 0)
    extra = jnp.where(places == 0, diagonal, jnp.where(places == 1, count, 0.0))
    extra = jnp.concatenate([extra, jnp.zeros((EXTRA, width - TILE), F32)], axis=1)
    packed = jnp.concatenate([first, band[:, TILE:width]], axis=1)
    return packed[0 : block // 2], jnp.concatenate([packed[block // 2 :], extra], axis=0)


def piece_shape(kind, half, block, feat):
    step, width = block // 2, feat // 2
    factor = step + EXTRA * half
    if kind == "factor":
        return factor, width
    if kind == "mixed":
        return step, feat
    return factor + step * (feat // width), width


def store(outs, seeds, group, place, number, first, value):
    output, position = 4 * group + place[0], place[1]
    here = slice(first, first + value.shape[0])
    if seeds:
        value = value + seeds[output][position, number, here, :]
    outs[output][position, number, here, :] = value


def prepare_kernel(routes, counts, out, samples, feat):
    experts = counts.shape[1]
    out[...] = jnp.zeros(out.shape, F32)
    hits = []
    for expert in range(experts):
        same = [jnp.where(routes[k : k + 1, :] == expert, 1.0, 0.0) for k in range(routes.shape[0])]
        hits.append(sum(same[1:], same[0]))
    hit = jnp.concatenate(hits, axis=0)
    first = lax.broadcasted_iota(jnp.int32, (samples, samples), 0)
    second = lax.broadcasted_iota(jnp.int32, (samples, samples), 1)
    rank = dot(hit.astype(BF16), jnp.where(first < second, 1.0, 0.0).astype(BF16))
    per_row = feat // samples
    for expert in range(experts):
        limit = counts[0, expert].astype(F32)
        keep = jnp.where(rank[expert : expert + 1, :] < limit, hits[expert], 0.0)
        row, column = expert // per_row, expert % per_row * samples
        out[row : row + 1, column : column + samples] = keep


def act_kernel(turns, block, chips, seeded, samples, place, *refs):
    parts, kept, refs = refs[:2], refs[2:4], refs[4:]
    refs, (high, low, turned) = refs[:-3], refs[-3:]
    seeds, outs = (refs[: len(refs) // 2], refs[len(refs) // 2 :]) if seeded else ((), refs)
    feat = parts[0].shape[1]
    width = feat // 2 + TILE
    mine, expert = place[0], place[1]
    split_rows(parts, samples, high, low, feat)
    keeps = [keep_row(kept, samples, expert ^ (2 * turn)) for turn in turns]
    places = slots(chips)
    for k in range(chips):
        column, row = band_place(mine ^ (2 * k), block)
        both, tops = weighted(left_rows(parts, samples, turned, column, row, block), keeps)
        total = three(both, tops, high[:, pl.ds(column, width)], low[:, pl.ds(column, width)])
        for number, keep in enumerate(keeps):
            count = jnp.sum(keep, axis=1, keepdims=True)
            packed = pack(total[number * block : (number + 1) * block], row, count)
            for half in range(2):
                store(outs, seeds, 0, places[k, half], number, 0, packed[half])


def grad_kernel(turns, block, chips, seeded, samples, place, *refs):
    grads, acts, kept, refs = refs[:2], refs[2:4], refs[4:6], refs[6:]
    refs, (high, low, act_high, act_low, turned) = refs[:-5], refs[-5:]
    seeds, outs = (refs[: len(refs) // 2], refs[len(refs) // 2 :]) if seeded else ((), refs)
    feat = grads[0].shape[1]
    step, width = block // 2, feat // 2
    mine, expert = place[0], place[1]
    split_rows(grads, samples, high, low, feat)
    split_rows(acts, samples, act_high, act_low, feat)
    keeps = [keep_row(kept, samples, expert ^ (2 * turn)) for turn in turns]
    places = slots(chips)
    for k in range(chips):
        column, row = band_place(mine ^ (2 * k), block)
        both, tops = weighted(left_rows(grads, samples, turned, column, row, block), keeps)
        here = pl.ds(column, width + TILE)
        total = three(both, tops, high[:, here], low[:, here])
        mixed = three(both, tops, act_high[...], act_low[...])
        for number in range(len(keeps)):
            packed = pack(total[number * block : (number + 1) * block], row, 0.0)
            for half in range(2):
                spot = places[k, half]
                first = number * block + half * step
                value = mixed[first : first + step]
                if number:
                    store(outs, seeds, 2, spot, number - 1, 0, packed[half])
                    for part in range(feat // width):
                        below = packed[half].shape[0] + part * step
                        columns = slice(part * width, (part + 1) * width)
                        store(outs, seeds, 2, spot, number - 1, below, value[:, columns])
                else:
                    store(outs, seeds, 0, spot, 0, 0, packed[half])
                    store(outs, seeds, 1, spot, 0, 0, value)


def whole_in_vmem(count):
    return [pl.BlockSpec(memory_space=pltpu.VMEM)] * count


def prepare(routes, counts, feat):
    samples = routes.shape[0]
    rows = EXTRA * -(-counts.shape[1] * samples // (EXTRA * feat))
    return pl.pallas_call(
        functools.partial(prepare_kernel, samples=samples, feat=feat),
        out_shape=jax.ShapeDtypeStruct((rows, feat), F32),
        in_specs=[pl.BlockSpec(memory_space=pltpu.VMEM), pl.BlockSpec(memory_space=pltpu.SMEM)],
        out_specs=pl.BlockSpec(memory_space=pltpu.VMEM),
        compiler_params=pltpu.CompilerParams(vmem_limit_bytes=60 * MIB),
    )(routes.T, counts)


def bands(body, turns, groups, place, parts, seeds, samples, chips, block):
    feat = parts[0].shape[1]
    extended = pltpu.VMEM((2 * samples, feat + feat // 2), BF16)
    plain = pltpu.VMEM((2 * samples, feat), BF16)
    scratch = [extended, extended] + ([plain, plain] if len(parts) > 4 else [])
    shapes = [
        jax.ShapeDtypeStruct((len(group), count, *piece_shape(kind, half, block, feat)), F32)
        for count, kind in groups
        for half, order in enumerate(orders(chips))
        for group in held_and_sent(chips, order)
    ]
    operands = (*parts, *seeds)
    limit = 36 if len(parts) > 4 else 20
    return pl.pallas_call(
        functools.partial(body, range(turns), block, chips, bool(seeds), samples),
        out_shape=shapes,
        in_specs=[pl.BlockSpec(memory_space=pltpu.SMEM)] + whole_in_vmem(len(operands)),
        out_specs=whole_in_vmem(len(shapes)),
        scratch_shapes=scratch + [pltpu.VMEM((TILE, 2 * samples), F32)],
        compiler_params=pltpu.CompilerParams(vmem_limit_bytes=limit * MIB),
    )(place, *operands)


def unfold(bands, extras, full):
    tiles = full.shape[0] // TILE
    per_tile = extras.shape[0] // EXTRA // tiles
    rows = lax.broadcasted_iota(jnp.int32, (TILE, TILE), 0)
    columns = lax.broadcasted_iota(jnp.int32, (TILE, TILE), 1)

    def put(i, j, value):
        full[i * TILE : (i + 1) * TILE, j * TILE : (j + 1) * TILE] = value

    firsts = [bands[i * TILE : (i + 1) * TILE, 0:TILE] for i in range(tiles)]
    turned = [value.T for value in firsts]
    for i in range(tiles):
        put(i, i, jnp.where(rows <= columns, firsts[i], turned[i]))
        for step in range(1, tiles // 2):
            here = bands[i * TILE : (i + 1) * TILE, step * TILE : (step + 1) * TILE]
            put(i, (i + step) % tiles, here)
            put((i + step) % tiles, i, here.T)
    for i in range(tiles // 2):
        j = i + tiles // 2
        places = [EXTRA * (i * per_tile + owner) for owner in range(per_tile)]
        diagonal = sum(extras[place : place + 1, :] for place in places)
        here = jnp.where(rows > columns, firsts[i], jnp.where(rows < columns, turned[j], diagonal))
        put(i, j, here)
        put(j, i, here.T)


def damping(full):
    size = full.shape[0]
    value = full[...]
    lanes = lax.broadcasted_iota(jnp.int32, (size, size), 1)
    sublanes = lax.broadcasted_iota(jnp.int32, (size, size), 0)
    trace = jnp.sum(jnp.sum(jnp.where(lanes == sublanes, value, 0.0), axis=0, keepdims=True), axis=1, keepdims=True)
    largest = jnp.max(jnp.sum(jnp.abs(value), axis=0, keepdims=True), axis=1, keepdims=True)
    damp = trace * (0.1 / size)
    return damp, 1.0 / (largest + damp)


def times(left, high, low):
    rows = left.shape[0]
    top, rest = split(left)
    first = dot(jnp.concatenate([top, rest], axis=0), high[...])
    return first[0:rows] + first[rows : 2 * rows] + dot(top, low[...])


def gather_order(order):
    offsets = [0]
    for bit in order:
        offsets += [k | (1 << bit) for k in offsets]
    return offsets


def row_pieces(place, block, chips, arrays, extra):
    step = block // 2
    firsts = [(value, first) for value in arrays for first in range(0, value.shape[0], block + extra)]
    pieces, extras = [], []
    for number, (value, first) in enumerate(firsts):
        core, position = number // chips, number % chips
        for half, order in enumerate(orders(chips)):
            owner = place[0] ^ (2 * gather_order(order)[position] + core)
            here = pl.ds(pl.multiple_of(owner * block + half * step, step), step)
            pieces.append((here, value.at[first + half * step : first + (half + 1) * step]))
        if extra:
            here = pl.ds(pl.multiple_of(owner * EXTRA, EXTRA), EXTRA)
            extras.append((here, value.at[first + block : first + block + extra]))
    return pieces, extras


def factor_rows(place, block, blocks, bands, extras, full):
    chips = full.shape[0] // (2 * block)
    pieces, others = row_pieces(place, block, chips, blocks, EXTRA)
    for here, value in pieces:
        bands[here, :] = value[...]
    for here, value in others:
        extras[here, :] = value[:, 0:TILE]
    unfold(bands, extras, full)
    return full[pl.ds(pl.multiple_of(place[0] * block, block), block), :]


def act_factor_kernel(place, *refs):
    blocks, (factor, scales, high, low), (bands, extras, full) = refs[:-7], refs[-7:-3], refs[-3:]
    factor[...] = factor_rows(place, factor.shape[0], blocks, bands, extras, full)
    damp, alpha = damping(full)
    scales[0:1, :] = jnp.broadcast_to(damp, (1, TILE))
    scales[1:2, :] = jnp.broadcast_to(alpha, (1, TILE))
    high[...], low[...] = split(full[...])


def grad_factor_kernel(place, *refs):
    blocks, (factor, inverse), (bands, extras, full, high, low) = refs[:-7], refs[-7:-5], refs[-5:]
    block, feat = factor.shape
    rows = factor_rows(place, block, blocks, bands, extras, full)
    factor[...] = rows
    damp, alpha = damping(full)
    high[...], low[...] = split(full[...])
    lanes = lax.broadcasted_iota(jnp.int32, (block, feat), 1)
    sublanes = lax.broadcasted_iota(jnp.int32, (block, feat), 0)
    unit = jnp.where(lanes == sublanes + place[0] * block, 1.0, 0.0).astype(F32)
    rest_rows = unit - alpha * (rows + damp * unit)
    once = 2.0 * rest_rows - alpha * (times(rest_rows, high, low) + damp * rest_rows)
    inverse[...] = alpha * (unit + rest_rows + once - alpha * (times(once, high, low) + damp * once))


def update_kernel(place, *refs):
    blocks = refs[:-9]
    inverse, scales, act_high, act_low, momentum, weights, moment_out, weight_out, full = refs[-9:]
    block = momentum.shape[0]
    for here, value in row_pieces(place, block, full.shape[0] // (2 * block), blocks, 0)[0]:
        full[here, :] = value[...]
    damp, alpha = scales[0:1, 0:1], scales[1:2, 0:1]
    half_way = times(inverse[...], *split(full[...]))
    value = half_way
    for _ in range(3):
        value = half_way + value - alpha * (times(value, act_high[...], act_low[...]) + damp * value)
    moment = 0.9 * momentum[...] + alpha * value
    moment_out[...] = moment
    weight_out[...] = weights[...] - 0.5 * moment


def on_core(body, place, operands, shapes, scratch, limit):
    return pl.pallas_call(
        body,
        out_shape=shapes,
        in_specs=[pl.BlockSpec(memory_space=pltpu.SMEM)] + whole_in_vmem(len(operands)),
        out_specs=whole_in_vmem(len(shapes)),
        scratch_shapes=scratch,
        compiler_params=pltpu.CompilerParams(vmem_limit_bytes=limit * MIB),
    )(place, *operands)


def factor_scratch(block, feat):
    shapes = [(feat, feat // 2), (EXTRA * feat // block, TILE), (feat, feat)]
    return [pltpu.VMEM(shape, F32) for shape in shapes]


def act_factor_rows(place, blocks, block, feat):
    shapes = [((block, feat), F32), ((8, TILE), F32), ((feat, feat), BF16), ((feat, feat), BF16)]
    shapes = [jax.ShapeDtypeStruct(*shape) for shape in shapes]
    scratch = factor_scratch(block, feat)
    return on_core(act_factor_kernel, place, blocks, shapes, scratch, 32)


def grad_factor_rows(place, blocks, block, feat):
    shapes = [jax.ShapeDtypeStruct((block, feat), F32)] * 2
    scratch = factor_scratch(block, feat)
    scratch += [pltpu.VMEM((feat, feat), BF16)] * 2
    return on_core(grad_factor_kernel, place, blocks, shapes, scratch, 32)


def update_rows(place, blocks, inverse, scales, high, low, momentum, weights):
    block, feat = momentum.shape
    operands = (*blocks, inverse, scales, high, low, momentum, weights)
    shapes = [jax.ShapeDtypeStruct((block, feat), F32)] * 2
    return on_core(update_kernel, place, operands, shapes, [pltpu.VMEM((feat, feat), F32)], 32)


def swap(value, axis, step):
    size = lax.axis_size(axis)
    return lax.ppermute(value, axis, [(i, i ^ step) for i in range(size)])


class PlaneSum:
    def __init__(self, pieces, chips):
        self.steps = [list(order) for order in orders(chips)]
        self.offsets = [held_and_sent(chips, order)[0] for order in self.steps]
        self.held, self.leaving = list(pieces[0::2]), list(pieces[1::2])

    def send(self):
        self.got = [swap(value, "dp", 2 << order[0]) for value, order in zip(self.leaving, self.steps)]

    def add(self):
        self.leaving = []
        for half, order in enumerate(self.steps):
            offsets = self.offsets[half]
            sums = {k: self.held[half][i] + self.got[half][i] for i, k in enumerate(offsets)}
            order.pop(0)
            if order:
                offsets = [k for k in offsets if not (k >> order[0]) & 1]
                self.leaving.append(jnp.stack([sums[k | (1 << order[0])] for k in offsets]))
            self.offsets[half] = offsets
            self.held[half] = [sums[k] for k in offsets]

    def finish(self):
        while self.steps[0]:
            self.send()
            self.add()
        return [held[0] for held in self.held]


def across(far):
    return [swap(far[number], "expert", 2 * (number + 1)) for number in range(far.shape[0])]


class Gather:
    def __init__(self, halves, chips):
        self.chips, self.orders = chips, orders(chips)
        self.halves, self.whole = halves, {}

    def begin(self):
        block = jnp.concatenate(self.halves, axis=0)
        self.whole = {order[0]: swap(block, "dp", 2 << order[0]) for order in self.orders}

    def relay(self):
        first = self.halves[0].shape[0]
        self.held = []
        for half, order in enumerate(self.orders):
            held = [self.halves[half]]
            for bit in order:
                came = [swap(value, "dp", 2 << bit) for value in held[1:]]
                if bit in self.whole:
                    own = self.whole[bit][first:] if half else self.whole[bit][:first]
                else:
                    own = swap(held[0], "dp", 2 << bit)
                held += [own] + came
            self.held.append(held)

    def hold_last(self, value):
        last, value = together([held[-1] for held in self.held], value)
        self.held = [held[:-1] + [block] for held, block in zip(self.held, last)]
        return value

    def exchange(self, first=0, last=None):
        pairs = list(zip(*self.held))[first:last]
        mine = jnp.concatenate([value for pair in pairs for value in pair], axis=0)
        return mine, swap(mine, "dp", 1)


def together(*values):
    return lax.optimization_barrier(values)


def on_device(acts, grads_out, routes, counts, old_act_factor, old_grad_factor, momentum, weights):
    devices, experts = lax.axis_size("dp"), lax.axis_size("expert")
    chips = devices // 2
    samples, feat, block = acts.shape[0], acts.shape[1], weights.shape[1]
    step, width = block // 2, feat // 2
    mine = lax.axis_index("dp")
    place = jnp.stack([mine, lax.axis_index("expert")]).astype(jnp.int32)

    def own_band(old):
        start = mine * block // TILE * TILE
        wide = jnp.concatenate([old[0], old[0][:, 0:width]], axis=1)
        band = lax.dynamic_slice_in_dim(wide, start, width + TILE, 1)
        return [0.5 * half for half in pack(band, mine * block - start, 0.0)]

    turns = experts // 2
    size = (samples, chips, block)
    act_groups = ((turns, "factor"),)
    grad_groups = ((1, "factor"), (1, "mixed"), (turns - 1, "both"))

    acts_far = swap(acts, "expert", 1)
    keep = prepare(routes, counts, feat)
    keep_far = swap(keep, "expert", 1)
    later_acts, keep = together(acts, keep)
    near_acts = (acts, swap(later_acts, "dp", 1), keep, swap(keep, "dp", 1))
    act_seeds = bands(act_kernel, turns, act_groups, place, near_acts, (), *size)
    grads_far = swap(grads_out, "expert", 1)
    grad_parts = (grads_out, swap(grads_out, "dp", 1)) + near_acts
    grad_seeds = bands(grad_kernel, turns, grad_groups, place, grad_parts, (), *size)
    old_act, old_grad = own_band(old_act_factor), own_band(old_grad_factor)
    early = (act_seeds, grad_seeds, old_act, old_grad)
    acts_far, (act_seeds, grad_seeds, old_act, old_grad) = together(acts_far, early)

    far_acts = (acts_far, swap(acts_far, "dp", 1), keep_far, swap(keep_far, "dp", 1))
    act_sum = PlaneSum(bands(act_kernel, turns, act_groups, place, far_acts, act_seeds, *size), chips)
    act_sum.send()
    act_sum.add()
    act_sum.send()
    grads_far, _ = together(grads_far, act_sum.leaving)
    grad_parts = (grads_far, swap(grads_far, "dp", 1)) + far_acts
    pieces = bands(grad_kernel, turns, grad_groups, place, grad_parts, grad_seeds, *size)

    grad_sum, mixed_sum, far_sum = [PlaneSum(pieces[first : first + 4], chips) for first in (0, 4, 8)]
    far_sum.send()
    act_sum.got, far_sum.held = together(act_sum.got, far_sum.held)
    act_sum.add()
    act_sums = act_sum.finish()
    act_across = across(jnp.concatenate([value[1:] for value in act_sums], axis=1))
    grad_sum.leaving, far_sum.got = together(grad_sum.leaving, far_sum.got)
    grad_sum.send()
    far_sum.add()
    far_sum.leaving, act_across = together(far_sum.leaving, act_across)
    far_sum.send()
    grad_sum.add()
    mixed_sum.leaving, grad_sum.leaving = together(mixed_sum.leaving, grad_sum.leaving)
    mixed_sum.send()
    grad_sum.send()
    far_sum.add()
    far_sums = far_sum.finish()

    factors = [slice(0, step), slice(step, block + EXTRA)]
    act_totals = [
        sum((there[factors[half]] for there in act_across), value[0]) for half, value in enumerate(act_sums)
    ]
    total = jnp.maximum(act_totals[1][step + 1 : step + 2, 0:1], 1.0)
    act_halves = [old + 0.5 * (value / total) for old, value in zip(old_act, act_totals)]
    sizes = [step, step + EXTRA]
    across_grad = across(jnp.concatenate([value[:, 0:size] for value, size in zip(far_sums, sizes)], axis=1))
    far_mixed = jnp.concatenate(
        [
            jnp.concatenate([value[:, size : size + step], value[:, size + step :]], axis=2)
            for value, size in zip(far_sums, sizes)
        ],
        axis=1,
    )
    grad_sum.add()
    grad_sums = grad_sum.finish()
    mixed_sum.held, across_grad = together(mixed_sum.held, across_grad)
    mixed_sum.add()
    mixed_sum.leaving, far_mixed = together(mixed_sum.leaving, far_mixed)
    mixed_sum.send()
    across_mixed = across(far_mixed)

    def both(near, far, rows):
        return [sum((there[here] for there in far), value[0]) / total for value, here in zip(near, rows)]

    grad_stats = both(grad_sums, across_grad, factors)
    grad_halves = [old + 0.5 * value for old, value in zip(old_grad, grad_stats)]
    grad_gather = Gather(grad_halves, chips)
    grad_gather.begin()
    early = (grad_gather.whole, mixed_sum.got)
    act_halves, (grad_gather.whole, mixed_sum.got) = together(act_halves, early)
    mixed_sum.add()
    mixed_sums = mixed_sum.finish()
    act_gather = Gather(act_halves, chips)
    act_gather.begin()
    grad_gather.relay()
    act_gather.relay()
    across_mixed, _ = together(across_mixed, act_gather.whole)
    mixed_gather = Gather(both(mixed_sums, across_mixed, [slice(0, step), slice(step, block)]), chips)
    mixed_gather.begin()
    grad_out, inverse = grad_factor_rows(place, grad_gather.exchange(), block, feat)
    inverse = act_gather.hold_last(inverse)
    mixed_gather.whole = act_gather.hold_last(mixed_gather.whole)
    mixed_gather.relay()
    mine, theirs = mixed_gather.exchange(0, -1)
    act_out, *act_square = act_factor_rows(place, act_gather.exchange(), block, feat)
    act_square = mixed_gather.hold_last(act_square)
    my_last, their_last = mixed_gather.exchange(-1)
    mixed_blocks = (mine, my_last, theirs, their_last)
    outs = update_rows(place, mixed_blocks, inverse, *act_square, momentum[0], weights[0])
    return tuple(out[None] for out in (act_out, grad_out, *outs))


def solution(mesh):
    rows = P(("dp", "expert"), None)
    matrix = P("expert", "dp", None)
    return jax.shard_map(
        on_device,
        mesh=mesh,
        in_specs=(rows,) * 4 + (matrix,) * 4,
        out_specs=(matrix,) * 4,
        check_vma=False,
    )
```
